32 devices in a mesh: dp: 4 (over y, x), expert: 8 (over z, core).
Axes of the slice: x: 2, y: 2, z: 4, core: 2. Of those that a mesh axis runs over, the one named last changes fastest.
Arguments:
- hidden_in: bfloat16 [8, 1024, 1024], P('dp', 'expert'), may hold values from -6 to 6
- out_grad: bfloat16 [8, 1024, 1024], P('dp', 'expert'), may hold values from -6 to 6
- expert_ids: int32 [8, 1024, 8], P('dp', 'expert'), may hold values from 0 to 31, all different within a row; in each aligned block of 128 rows (0 to 127, 128 to 255, ..., all dimensions but the last counted through in order) at most 48 rows name the same one
- route_gates: float32 [8, 1024, 8], P('dp', 'expert'), may hold values from 0.06 to 0.19
- norm_gains: float32 [2, 1024], P(None, 'dp'), may hold values from 0.5 to 1.5
- qkv_weight: float32 [1024, 2048], P('dp'), may hold values from -0.25 to 0.25
- out_weight: float32 [1024, 1024], P('dp'), may hold values from -0.75 to 0.75
- gate_up_weight: float32 [32, 1024, 1024], P('expert', 'dp'), may hold values from -0.1875 to 0.1875
- down_weight: float32 [32, 512, 1024], P('expert', 'dp'), may hold values from -1 to 1
- gains_first: float32 [2, 1024], P(None, 'dp'), may hold values from -128 to 128
- gains_second: float32 [2, 1024], P(None, 'dp'), may hold values from 1720.32 to 6881.28
- qkv_first: float32 [1024, 2048], P('dp'), may hold values from -96 to 96
- qkv_second: float32 [1024, 2048], P('dp'), may hold values from 983.04 to 3850.24
- out_first: float32 [1024, 1024], P('dp'), may hold values from -24 to 24
- out_second: float32 [1024, 1024], P('dp'), may hold values from 68.8128 to 278.528
- gate_up_first: float32 [32, 1024, 1024], P('expert', 'dp'), may hold values from -12 to 12
- gate_up_second: float32 [32, 1024, 1024], P('expert', 'dp'), may hold values from 17.2032 to 69.632
- down_first: float32 [32, 512, 1024], P('expert', 'dp'), may hold values from -2 to 2
- down_second: float32 [32, 512, 1024], P('expert', 'dp'), may hold values from 0.6144 to 2.4576
Outputs:
- hidden_out: bfloat16 [8, 1024, 1024], P('dp', 'expert')
- input_grad: float32 [8, 1024, 1024], P('dp', 'expert')
- gains_first_new: float32 [2, 1024], P(None, 'dp')
- gains_second_new: float32 [2, 1024], P(None, 'dp')
- gains_new: float32 [2, 1024], P(None, 'dp')
- qkv_first_new: float32 [1024, 2048], P('dp')
- qkv_second_new: float32 [1024, 2048], P('dp')
- qkv_new: float32 [1024, 2048], P('dp')
- out_first_new: float32 [1024, 1024], P('dp')
- out_second_new: float32 [1024, 1024], P('dp')
- out_new: float32 [1024, 1024], P('dp')
- gate_up_first_new: float32 [32, 1024, 1024], P('expert', 'dp')
- gate_up_second_new: float32 [32, 1024, 1024], P('expert', 'dp')
- gate_up_new: float32 [32, 1024, 1024], P('expert', 'dp')
- down_first_new: float32 [32, 512, 1024], P('expert', 'dp')
- down_second_new: float32 [32, 512, 1024], P('expert', 'dp')
- down_new: float32 [32, 512, 1024], P('expert', 'dp')
The draws below stay inside these ranges and needn't reach their ends.
Inputs may be any that keep to these rules, and one draw needn't show every extreme that they name: `expert_ids`: each token names 8 different experts; among the 128 tokens of one block of a sequence (positions c * 128 to c * 128 + 127), at most 48 name any one expert.
All inputs are finite; a program needn't handle non-finite values.
Results may differ from the reference program's by a relative error of at most 0.02.
Values may be sent and summed in bfloat16 or wider, within the bound.
No kernel may reach another device: no remote copies, remote signals or barrier semaphores. Data moves between devices by JAX's collectives and lax.ppermute only.
A program may use at most 192 MiB of HBM per device.

```python
import math
import jax
import jax.numpy as jnp
import numpy as np
from jax import lax

D = 1024
HEADS = 16
KV_HEADS = 8
HEAD = 64
EXPERTS = 32
FF = 512
TOP = 8
SPAN = 128
STEP = 10
SEQ_LEN = 1024
BATCH = 8
CAP = 48


def block_scale(own_key, shape, cuts, least, top_value):
    level = 1.0
    for position, parts in cuts:
        draws = jax.random.uniform(jax.random.fold_in(jax.random.fold_in(own_key, 6), position), (parts,), jnp.float32, least / len(cuts), top_value / len(cuts))
        level = level * jnp.repeat(jnp.exp(draws), shape[position] // parts).reshape((-1,) + (1,) * (len(shape) - 1 - position))
    return level


def assign_block(rng, own, number, rows, count, top, limit, lean):
    ranking = jax.random.permutation(rng, count)
    crowded, common = load_shares(count, rows * top, limit, lean, True), load_shares(count, rows * top, limit, lean, False)
    places = jnp.arange(count)

    def named(lengths, turn):
        used = int((lengths > 0).sum())
        fixed = max(1, used // 4)
        moved = fixed + (places - fixed + turn * (used - fixed)) % max(1, count - fixed)
        return jnp.zeros((count,), jnp.int32).at[ranking[jnp.where(places < fixed, places, moved)]].set(jnp.asarray(lengths, jnp.int32))

    lengths = jnp.where(number % 4 == 0, named(crowded, number // 4), named(common, number - number // 4 - 1))
    mixed = jax.random.permutation(jax.random.fold_in(own, 3), count)
    source_of, sink = mixed[0:count // 2 * 2:2], mixed[1:count // 2 * 2:2]
    slack = jnp.minimum(lengths[source_of] - 1, limit - lengths[sink]) // 2
    slack = jnp.where((source_of == ranking[0]) | (sink == ranking[0]) | (lengths[sink] == 0), 0, jnp.maximum(slack, 0))
    moved = jax.random.randint(jax.random.fold_in(own, 4), (count // 2,), 0, 1 << 20) % (slack + 1)
    lengths = lengths.at[source_of].add(-moved).at[sink].add(moved)
    labels = jnp.searchsorted(jnp.cumsum(lengths), jnp.arange(rows * top), side="right").astype(jnp.int32)
    table = labels.reshape(top, rows).T
    table = table[jax.random.permutation(jax.random.fold_in(own, 1), rows)]
    turn = jax.random.randint(jax.random.fold_in(own, 2), (rows, 1), 0, top)
    return jnp.take_along_axis(table, (jnp.arange(top)[None, :] + turn) % top, axis=1)


def load_shares(number_of, total, most, slope, full):
    portions = [(1 << 20) // math.isqrt(standing ** slope) + 1 for standing in range(1, number_of + 1)]
    largest = most if full else min(most, max(-(-total // number_of), total * portions[0] // sum(portions)))
    least = 1 if total - largest >= number_of - 1 else 0
    holding, surplus = [largest] + [least] * (number_of - 1), total - largest - least * (number_of - 1)
    while surplus > 0:
        movable = [i for i in range(1, number_of) if holding[i] < largest] or [i for i in range(1, number_of) if holding[i] < most]
        mass, left = sum([portions[i] for i in movable]), surplus
        for i in movable:
            more = min(most - holding[i], max(1, left * portions[i] // mass), surplus)
            holding[i] = holding[i] + more
            surplus = surplus - more
    return np.array(holding)


def gaussian(rng, dims, deviation, bound, shards=(), kind=jnp.bfloat16):
    values = deviation * jax.random.normal(rng, dims, jnp.float32)
    if shards:
        values = values * block_scale(rng, dims, shards, -0.22, 0.18)
    return jnp.clip(values, -bound, bound).astype(kind)


def setup_inputs(seed: int = 0) -> dict:
    arg_keys = jax.random.split(jax.random.key(seed), 20)
    hidden_in = gaussian(arg_keys[0], (BATCH, SEQ_LEN, D), 1.0, 6.0, ((0, 4), (1, 8)))
    out_grad = gaussian(arg_keys[1], (BATCH, SEQ_LEN, D), 1.0, 6.0, ((0, 4), (1, 8)))
    expert_ids_keys = jax.random.split(jax.random.fold_in(arg_keys[2], 1), BATCH * SEQ_LEN // SPAN)
    expert_ids_turns = jax.random.permutation(jax.random.fold_in(arg_keys[2], 3), BATCH * SEQ_LEN // SPAN)
    expert_ids = jax.vmap(lambda own, number: assign_block(jax.random.fold_in(arg_keys[2], 2), own, number, SPAN, EXPERTS, TOP, CAP, 2))(expert_ids_keys, expert_ids_turns).reshape((BATCH, SEQ_LEN, TOP))
    route_gates = jnp.clip(0.06 + 0.13 * jax.random.uniform(arg_keys[3], (BATCH, SEQ_LEN, TOP), jnp.float32) ** block_scale(arg_keys[3], (BATCH, SEQ_LEN, TOP), ((0, 4), (1, 8)), -0.2, 0.2), 0.06, 0.19)
    norm_gains = jnp.clip(1.0 + 0.1 * jax.random.normal(arg_keys[4], (2, D), jnp.float32), 0.5, 1.5)
    qkv_weight = gaussian(arg_keys[5], (D, (HEADS + 2 * KV_HEADS) * HEAD), (D // 2) ** -0.5, 0.25, ((0, 4),), jnp.float32)
    out_weight = gaussian(arg_keys[6], (D, D), (D // 16) ** -0.5, 0.75, ((0, 4),), jnp.float32)
    gate_up_weight = gaussian(arg_keys[7], (EXPERTS, D, 2 * FF), D ** -0.5, 0.1875, ((0, 8), (1, 4)), jnp.float32)
    down_weight = gaussian(arg_keys[8], (EXPERTS, FF, D), (FF // 16) ** -0.5, 1.0, ((0, 8), (1, 4)), jnp.float32)
    gains_first = gaussian(arg_keys[9], (2, D), (0.22 * (BATCH * SEQ_LEN) ** 0.5), 128.0, ((1, 4),), jnp.float32)
    gains_second = jnp.clip(jnp.exp(math.log(6881.28) - 1.3862944 * jax.random.uniform(arg_keys[10], (2, D), jnp.float32) ** block_scale(arg_keys[10], (2, D), ((1, 4),), -0.2, 0.2)), 1720.32, 6881.28)
    qkv_first = gaussian(arg_keys[11], (D, (HEADS + 2 * KV_HEADS) * HEAD), (0.17 * (BATCH * SEQ_LEN) ** 0.5), 96.0, ((0, 4),), jnp.float32)
    qkv_second = jnp.clip(jnp.exp(math.log(3850.24) - 1.36524097 * jax.random.uniform(arg_keys[12], (D, (HEADS + 2 * KV_HEADS) * HEAD), jnp.float32) ** block_scale(arg_keys[12], (D, (HEADS + 2 * KV_HEADS) * HEAD), ((0, 4),), -0.2, 0.2)), 983.04, 3850.24)
    out_first = gaussian(arg_keys[13], (D, D), (0.044 * (BATCH * SEQ_LEN) ** 0.5), 24.0, ((0, 4),), jnp.float32)
    out_second = jnp.clip(jnp.exp(math.log(278.528) - 1.3981289 * jax.random.uniform(arg_keys[14], (D, D), jnp.float32) ** block_scale(arg_keys[14], (D, D), ((0, 4),), -0.2, 0.2)), 68.8128, 278.528)
    gate_up_first = gaussian(arg_keys[15], (EXPERTS, D, 2 * FF), (0.044 * (BATCH * SEQ_LEN * TOP // EXPERTS) ** 0.5), 12.0, ((0, 8), (1, 4)), jnp.float32)
    gate_up_second = jnp.clip(jnp.exp(math.log(69.632) - 1.3981289 * jax.random.uniform(arg_keys[16], (EXPERTS, D, 2 * FF), jnp.float32) ** block_scale(arg_keys[16], (EXPERTS, D, 2 * FF), ((0, 8), (1, 4)), -0.2, 0.2)), 17.2032, 69.632)
    down_first = gaussian(arg_keys[17], (EXPERTS, FF, D), (0.0083 * (BATCH * SEQ_LEN * TOP // EXPERTS) ** 0.5), 2.0, ((0, 8), (1, 4)), jnp.float32)
    down_second = jnp.clip(jnp.exp(math.log(2.4576) - 1.3862944 * jax.random.uniform(arg_keys[18], (EXPERTS, FF, D), jnp.float32) ** block_scale(arg_keys[18], (EXPERTS, FF, D), ((0, 8), (1, 4)), -0.2, 0.2)), 0.6144, 2.4576)
    return dict(hidden_in=hidden_in, out_grad=out_grad, expert_ids=expert_ids, route_gates=route_gates, norm_gains=norm_gains, qkv_weight=qkv_weight, out_weight=out_weight, gate_up_weight=gate_up_weight, down_weight=down_weight, gains_first=gains_first, gains_second=gains_second, qkv_first=qkv_first, qkv_second=qkv_second, out_first=out_first, out_second=out_second, gate_up_first=gate_up_first, gate_up_second=gate_up_second, down_first=down_first, down_second=down_second)


EPS_NORM = 1e-06
EPS_ADAM = 1e-08
BETA_ONE = 0.9
BETA_TWO = 0.95
DECAY = 0.1
THETA = 10000.0
NEG_FILL = -1e+30
HIGH = lax.Precision.HIGHEST

@jax.custom_vjp
def low(v):
    return lax.optimization_barrier(v.astype(jnp.bfloat16)).astype(jnp.float32)

@jax.custom_vjp
def low_back(v):
    return v

def low_keep(v):
    return (low(v), None)

def low_pass(kept, grad):
    return (grad,)

def back_keep(v):
    return (v, None)

def back_low(kept, grad):
    return (low(grad),)
low.defvjp(low_keep, low_pass)
low_back.defvjp(back_keep, back_low)

def rotation(positions):
    half_width = HEAD // 2
    frequency = jnp.power(THETA, -jnp.arange(half_width, dtype=jnp.float32) * (2.0 / HEAD))
    angles = positions[:, None] * frequency[None, :]
    return (jnp.cos(angles), jnp.sin(angles))

def rotate(values, cosine, sine):
    half_width = HEAD // 2
    first_half = values[..., :half_width]
    second_half = values[..., half_width:]
    cos_part = cosine[:, None, :]
    sin_part = sine[:, None, :]
    return jnp.concatenate([first_half * cos_part - second_half * sin_part, second_half * cos_part + first_half * sin_part], axis=-1)

def rms_norm(values, gain):
    return values * lax.rsqrt(lax.optimization_barrier(jnp.mean(values * values, axis=-1, keepdims=True)) + EPS_NORM) * gain

def routing(ids):
    blocks = SEQ_LEN // SPAN
    flat_ids = ids.reshape(blocks, SPAN * TOP).astype(jnp.int32)
    chosen = (flat_ids[:, :, None] == jnp.arange(EXPERTS, dtype=jnp.int32)[None, None, :]).astype(jnp.int32)
    earlier = jnp.cumsum(chosen, axis=1) - chosen
    place_rank = lax.optimization_barrier(jnp.sum(earlier * chosen, axis=2))
    slot_index = flat_ids * CAP + place_rank
    token_rows = jnp.broadcast_to(jnp.arange(SPAN * TOP, dtype=jnp.int32) // TOP, flat_ids.shape)
    block_ids = jnp.broadcast_to(jnp.arange(blocks, dtype=jnp.int32)[:, None], flat_ids.shape)
    source = jnp.full((blocks, EXPERTS * CAP), -1, jnp.int32).at[block_ids, slot_index].set(token_rows)
    return (source, slot_index)

def layer(params, hidden, gates, source, slot_index, cosine, sine):
    gains_w, qkv_w, out_w, gu_w, down_w = [low(piece) for piece in params]
    kv_width = KV_HEADS * HEAD
    group = HEADS // KV_HEADS
    normed = low(rms_norm(hidden, gains_w[0]))
    projected = low_back(jnp.dot(normed, qkv_w, precision=HIGH))
    queries = low(rotate(projected[:, :D].reshape(SEQ_LEN, HEADS, HEAD), cosine, sine))
    keys = low(rotate(projected[:, D:D + kv_width].reshape(SEQ_LEN, KV_HEADS, HEAD), cosine, sine))
    values = low(projected[:, D + kv_width:].reshape(SEQ_LEN, KV_HEADS, HEAD))
    block_rows = min(512, SEQ_LEN)
    query_blocks = queries.reshape(SEQ_LEN // block_rows, block_rows, KV_HEADS, group, HEAD)
    starts = jnp.arange(SEQ_LEN // block_rows, dtype=jnp.int32) * block_rows

    def attend(inputs):
        query_block, start = inputs
        scores = jnp.einsum('qkgd,tkd->kgqt', query_block, keys, precision=HIGH) * HEAD ** (-0.5)
        query_pos = start + jnp.arange(block_rows, dtype=jnp.int32)
        causal = query_pos[:, None] >= jnp.arange(SEQ_LEN, dtype=jnp.int32)[None, :]
        scores = low_back(jnp.where(causal, scores, NEG_FILL))
        row_max = lax.optimization_barrier(jnp.max(scores, axis=-1, keepdims=True))
        exponent = jnp.exp(scores - row_max)
        probability = exponent / lax.optimization_barrier(jnp.sum(exponent, axis=-1, keepdims=True))
        mixed = jnp.einsum('kgqt,tkd->qkgd', low(probability), values, precision=HIGH)
        return mixed.reshape(block_rows, D)
    attn_mix = lax.map(jax.checkpoint(attend), (query_blocks, starts)).reshape(SEQ_LEN, D)
    attn_mix = low(low_back(attn_mix))
    residual = hidden + low_back(jnp.dot(attn_mix, out_w, precision=HIGH))
    normed_two = low(rms_norm(residual, gains_w[1]))
    blocks = SEQ_LEN // SPAN
    by_block = normed_two.reshape(blocks, SPAN, D)
    valid = source >= 0
    taken = jax.vmap(lambda block_rows_in, index: block_rows_in[index])(by_block, jnp.maximum(source, 0))
    expert_in = jnp.where(valid[:, :, None], taken, jnp.zeros_like(taken))
    expert_in = expert_in.reshape(blocks, EXPERTS, CAP, D).transpose(1, 0, 2, 3).reshape(EXPERTS, blocks * CAP, D)
    expert_in = low_back(expert_in)
    gate_up = low_back(jnp.einsum('erd,edf->erf', expert_in, gu_w, precision=HIGH))
    hidden_act = low(jax.nn.silu(gate_up[..., :FF]) * gate_up[..., FF:])
    expert_out = low(low_back(jnp.einsum('erf,efd->erd', hidden_act, down_w, precision=HIGH)))
    returned = expert_out.reshape(EXPERTS, blocks, CAP, D).transpose(1, 0, 2, 3).reshape(blocks, EXPERTS * CAP, D)
    picked = jax.vmap(lambda block_rows_in, index: block_rows_in[index])(returned, slot_index)
    picked = picked.reshape(SEQ_LEN, TOP, D)
    return residual + lax.optimization_barrier(jnp.sum(gates[:, :, None] * picked, axis=1))

def adamw(weight, grad, first, second, rate, decay):
    first = BETA_ONE * first + (1.0 - BETA_ONE) * grad
    second = BETA_TWO * second + (1.0 - BETA_TWO) * grad * grad
    first_hat = first / (1.0 - BETA_ONE ** STEP)
    second_hat = second / (1.0 - BETA_TWO ** STEP)
    weight = weight - rate * (first_hat / (jnp.sqrt(second_hat) + EPS_ADAM) + decay * weight)
    return (first, second, weight)

def learning_rates():
    return (0.6, 3.0 * (2.0 / D) ** 0.5, 3.0 * (16.0 / D) ** 0.5, 3.0 * D ** (-0.5), 3.0 * (16.0 / FF) ** 0.5)

def reference(hidden_in, out_grad, expert_ids, route_gates, norm_gains, qkv_weight, out_weight, gate_up_weight, down_weight, gains_first, gains_second, qkv_first, qkv_second, out_first, out_second, gate_up_first, gate_up_second, down_first, down_second):
    params = (norm_gains, qkv_weight, out_weight, gate_up_weight, down_weight)
    cosine, sine = rotation(jnp.arange(SEQ_LEN, dtype=jnp.float32))

    def one_sequence(totals, inputs):
        hidden, cotangent, ids, gates = inputs
        source, slot_index = routing(ids)

        def forward(weights, tokens):
            return layer(weights, tokens, gates, source, slot_index, cosine, sine)
        result, pullback = jax.vjp(forward, params, hidden.astype(jnp.float32))
        weight_grads, token_grad = pullback(cotangent.astype(jnp.float32))
        totals = jax.tree.map(jnp.add, totals, weight_grads)
        return (totals, (result.astype(jnp.bfloat16), token_grad))
    grad_start = jax.tree.map(jnp.zeros_like, params)
    weight_sums, (outputs, input_grads) = lax.scan(one_sequence, grad_start, (hidden_in, out_grad, expert_ids, route_gates))
    rates = learning_rates()
    gains_up = adamw(norm_gains, weight_sums[0], gains_first, gains_second, rates[0], 0.0)
    qkv_up = adamw(qkv_weight, weight_sums[1], qkv_first, qkv_second, rates[1], DECAY)
    out_up = adamw(out_weight, weight_sums[2], out_first, out_second, rates[2], DECAY)
    gate_up_up = adamw(gate_up_weight, weight_sums[3], gate_up_first, gate_up_second, rates[3], DECAY)
    down_up = adamw(down_weight, weight_sums[4], down_first, down_second, rates[4], DECAY)
    return (outputs, input_grads, gains_up[0], gains_up[1], gains_up[2], qkv_up[0], qkv_up[1], qkv_up[2], out_up[0], out_up[1], out_up[2], gate_up_up[0], gate_up_up[1], gate_up_up[2], down_up[0], down_up[1], down_up[2])
```

```python
import jax
import jax.numpy as jnp
from jax import lax
from jax.sharding import PartitionSpec as P

D = 1024
HEADS = 16
KV_HEADS = 8
HEAD = 64
EXPERTS = 32
FF = 512
TOP = 8
STEP = 10
CAP = 48


EPS_NORM = 1e-06
EPS_ADAM = 1e-08
BETA_ONE = 0.9
BETA_TWO = 0.95
DECAY = 0.1
THETA = 10000.0
NEG_FILL = -1e30


def rotation(positions):
    half_width = HEAD // 2
    frequency = jnp.power(THETA, -jnp.arange(half_width, dtype=jnp.float32) * (2.0 / HEAD))
    angles = positions[:, None] * frequency[None, :]
    return (jnp.cos(angles), jnp.sin(angles))


def rotate(values, cosine, sine):
    half_width = HEAD // 2
    first_half = values[..., :half_width]
    second_half = values[..., half_width:]
    cos_part = cosine[:, None, :]
    sin_part = sine[:, None, :]
    return jnp.concatenate(
        [
            first_half * cos_part - second_half * sin_part,
            second_half * cos_part + first_half * sin_part,
        ],
        axis=-1,
    )


def rms_norm(values, gain):
    return values * lax.rsqrt(jnp.mean(values * values, axis=-1, keepdims=True) + EPS_NORM) * gain


def norm_backward(values, gain, upstream_grad):
    result, pullback = jax.vjp(rms_norm, values, gain)
    return pullback(upstream_grad)


def adamw(weight, grad, first, second, rate, decay):
    first = BETA_ONE * first + (1.0 - BETA_ONE) * grad
    second = BETA_TWO * second + (1.0 - BETA_TWO) * grad * grad
    first_hat = first / (1.0 - BETA_ONE**STEP)
    second_hat = second / (1.0 - BETA_TWO**STEP)
    weight = weight - rate * (first_hat / (jnp.sqrt(second_hat) + EPS_ADAM) + decay * weight)
    return (first, second, weight)


def learning_rates():
    return (
        0.6,
        3.0 * (2.0 / D) ** 0.5,
        3.0 * (16.0 / D) ** 0.5,
        3.0 * D ** (-0.5),
        3.0 * (16.0 / FF) ** 0.5,
    )


def head_scores(query_head, key_head, causal):
    scores = jnp.einsum(
        "sgqd,std->sgqt", query_head, key_head, preferred_element_type=jnp.float32
    ) * HEAD ** (-0.5)
    return jnp.where(causal, scores, NEG_FILL)


def xor_pairs(size, step):
    return [(index, index ^ step) for index in range(size)]


def square_gather(first, second):
    size = lax.axis_size("dp")
    near, far = xor_pairs(size, 1), xor_pairs(size, 2)
    first_one = lax.ppermute(first, "dp", near)
    second_two = lax.ppermute(second, "dp", far)
    first_rest = lax.ppermute(jnp.stack([first, first_one]), "dp", far)
    second_rest = lax.ppermute(jnp.stack([second, second_two]), "dp", near)
    return (
        (first, second),
        (first_one, second_rest[0]),
        (first_rest[0], second_two),
        (first_rest[1], second_rest[1]),
    )


def square_scatter(first, second):
    size = lax.axis_size("dp")
    near, far = xor_pairs(size, 1), xor_pairs(size, 2)

    def add(left, right):
        return (left.astype(jnp.float32) + right.astype(jnp.float32)).astype(jnp.bfloat16)

    first_got = lax.ppermute(jnp.stack([first[1], first[3]]), "dp", near)
    second_got = lax.ppermute(jnp.stack([second[2], second[3]]), "dp", far)
    first_got_two = lax.ppermute(add(first[2], first_got[1]), "dp", far)
    second_got_two = lax.ppermute(add(second[1], second_got[1]), "dp", near)

    def total(own, one, two):
        return own.astype(jnp.float32) + one.astype(jnp.float32) + two.astype(jnp.float32)

    return (
        total(first[0], first_got[0], first_got_two),
        total(second[0], second_got[0], second_got_two),
    )


def place_blocks(pieces, axis):
    me = lax.axis_index("dp")
    rows = pieces[0].shape[axis]
    shape = list(pieces[0].shape)
    shape[axis] = rows * len(pieces)
    whole = jnp.zeros(shape, pieces[0].dtype)
    for step, piece in enumerate(pieces):
        whole = lax.dynamic_update_slice_in_dim(whole, piece, (me ^ step) * rows, axis)
    return whole


def gather_rows(shard):
    size, cores = lax.axis_size("dp"), lax.axis_size("expert")
    if size != 4 or cores % 2:
        return lax.all_gather(shard, "dp", axis=0, tiled=True)
    rows, columns = shard.shape
    core = lax.axis_index("expert") % 2
    mine = lax.dynamic_slice_in_dim(shard, core * (rows // 2), rows // 2, 0)
    half = columns // 2
    got = square_gather(mine[:, :half], mine[:, half:])
    me = lax.axis_index("dp")
    whole = jnp.zeros((size, rows, columns), shard.dtype)
    stacked = jnp.stack([jnp.concatenate(pair, axis=1) for pair in got])
    other = lax.ppermute(stacked, "expert", xor_pairs(cores, 1))
    for step in range(size):
        for block, which in ((stacked, core), (other, 1 - core)):
            whole = lax.dynamic_update_slice(
                whole, block[step][None], (me ^ step, which * (rows // 2), 0)
            )
    return whole


def gather_experts(packed):
    size = lax.axis_size("dp")
    if size != 4:
        return lax.all_gather(packed, "dp", axis=1, tiled=False)
    half = packed.shape[0] // 2
    got = square_gather(packed[:half], packed[half:])
    return jnp.concatenate(
        [place_blocks([pair[part][:, None] for pair in got], 1) for part in range(2)], axis=0
    )


def scatter_experts(packed):
    size = lax.axis_size("dp")
    if size != 4:
        summed = lax.psum_scatter(packed, "dp", scatter_dimension=1, tiled=False)
        return summed.astype(jnp.float32)
    me = lax.axis_index("dp")
    half = packed.shape[0] // 2
    parts = [
        [lax.dynamic_index_in_dim(part, me ^ step, 1, keepdims=False) for step in range(size)]
        for part in (packed[:half], packed[half:])
    ]
    return jnp.concatenate(square_scatter(parts[0], parts[1]), axis=0)


def sum_everywhere(grad):
    size, owners = lax.axis_size("dp"), lax.axis_size("expert")
    width, columns = grad.shape
    rows = width // size
    spread = grad.astype(jnp.bfloat16).reshape(size, rows, columns)
    small = lax.psum_scatter(spread, "expert", scatter_dimension=1, tiled=True)
    if size == 4:
        me = lax.axis_index("dp")
        half = columns // 2
        parts = [lax.dynamic_index_in_dim(small, me ^ step, 0, keepdims=False) for step in range(size)]
        summed = square_scatter([p[:, :half] for p in parts], [p[:, half:] for p in parts])
        part = jnp.concatenate(summed, axis=1).astype(jnp.bfloat16)
    else:
        part = lax.psum_scatter(small, "dp", scatter_dimension=0, tiled=False)
    return lax.all_gather(part, "expert", axis=0, tiled=True).astype(jnp.float32)


def per_device(
    hidden_in,
    out_grad,
    expert_ids,
    route_gates,
    norm_gains,
    qkv_weight,
    out_weight,
    gate_up_weight,
    down_weight,
    gains_first,
    gains_second,
    qkv_first,
    qkv_second,
    out_first,
    out_second,
    gate_up_first,
    gate_up_second,
    down_first,
    down_second,
):
    sequences, span_len, model_width = hidden_in.shape
    owners = lax.axis_size("expert")
    dp_size = lax.axis_size("dp")
    position = lax.axis_index("expert")
    seq_len = span_len * owners
    group = HEADS // KV_HEADS
    kv_width = KV_HEADS * HEAD
    tok_rows = sequences * span_len
    local_experts = EXPERTS // owners
    blocks = owners * sequences
    low = jnp.bfloat16

    gain_rows = jnp.zeros((16, qkv_weight.shape[1]), low)
    gain_rows = gain_rows.at[:2, : norm_gains.shape[1]].set(norm_gains.astype(low))
    shard_rows = qkv_weight.shape[0]
    qkv_pack = jnp.concatenate(
        [qkv_weight[: shard_rows // 2].astype(low), gain_rows, qkv_weight[shard_rows // 2 :].astype(low), gain_rows],
        axis=0,
    )
    qkv_got = gather_rows(qkv_pack).reshape(dp_size, 2, shard_rows // 2 + 16, -1)
    qkv_low = qkv_got[:, :, : shard_rows // 2].reshape(model_width, -1)
    gains_used = (
        qkv_got[:, 0, shard_rows // 2 : shard_rows // 2 + 2, : norm_gains.shape[1]]
        .transpose(1, 0, 2)
        .reshape(2, model_width)
        .astype(jnp.float32)
    )
    out_low = gather_rows(out_weight.astype(low)).reshape(model_width, -1)
    up_rows = gate_up_weight.shape[1]
    down_rows = down_weight.shape[1]
    experts_low = gather_experts(
        jnp.concatenate([gate_up_weight.astype(low), down_weight.astype(low)], axis=1)
    )
    gate_up_low = experts_low[:, :, :up_rows].reshape(local_experts, model_width, -1)
    down_low = experts_low[:, :, up_rows:].reshape(local_experts, -1, model_width)

    tokens = hidden_in.astype(jnp.float32).reshape(tok_rows, model_width)
    normed = rms_norm(tokens, gains_used[0]).astype(low)
    projected = jnp.dot(normed, qkv_low, preferred_element_type=jnp.float32)
    query_pos = position * span_len + jnp.arange(span_len, dtype=jnp.int32)
    cosine, sine = rotation(query_pos.astype(jnp.float32))
    queries = rotate(
        projected[:, :D].reshape(sequences, span_len, HEADS, HEAD), cosine, sine
    ).astype(low)
    keys = rotate(
        projected[:, D : D + kv_width].reshape(sequences, span_len, KV_HEADS, HEAD), cosine, sine
    ).astype(low)
    values = projected[:, D + kv_width :].astype(low).reshape(sequences, span_len, kv_width)
    kv_local = jnp.stack([keys.reshape(sequences, span_len, kv_width), values], axis=0)
    kv_all = lax.all_gather(kv_local, "expert", axis=0, tiled=False)

    gates = route_gates.reshape(tok_rows, TOP)
    gates_high = gates.astype(low)
    gates_rest = (gates - gates_high.astype(jnp.float32)).astype(low)
    routes = jnp.concatenate([expert_ids.reshape(tok_rows, TOP).astype(low), gates_high, gates_rest], axis=1)
    route_rows = -(-tok_rows * 3 * TOP // model_width)
    pad_rows = -(-route_rows // 16) * 16
    routes = jnp.pad(routes.reshape(-1), (0, pad_rows * model_width - routes.size))
    upstream_low = out_grad.reshape(tok_rows, model_width)
    upstream_pack = jnp.concatenate([upstream_low, routes.reshape(pad_rows, model_width)], axis=0)
    upstream_pack, kv_all = lax.optimization_barrier((upstream_pack, kv_all))
    upstream_got = lax.all_gather(upstream_pack, "expert", axis=0, tiled=False)
    upstream_all = upstream_got[:, :tok_rows].reshape(blocks, span_len, model_width)
    routes_all = (
        upstream_got[:, tok_rows:]
        .reshape(owners, -1)[:, : tok_rows * 3 * TOP]
        .reshape(blocks, span_len, 3, TOP)
        .astype(jnp.float32)
    )
    local_ids = position * local_experts + jnp.arange(local_experts, dtype=jnp.int32)
    named = (routes_all[:, :, 0, None, :] == local_ids.astype(jnp.float32)[None, None, :, None]).astype(
        jnp.float32
    )
    hits = jnp.sum(named, axis=3)
    hit_gates = jnp.sum(named * (routes_all[:, :, 1] + routes_all[:, :, 2])[:, :, None, :], axis=3)
    before = jnp.tril(jnp.ones((span_len, span_len), jnp.float32), -1).astype(low)
    ranks = jnp.einsum("tu,bul->blt", before, hits.astype(low), preferred_element_type=jnp.float32)
    hits = hits.transpose(0, 2, 1)
    hit_gates = hit_gates.transpose(0, 2, 1)
    place = jnp.where(hits > 0.5, ranks, -1.0)
    chosen = place[:, :, None, :] == jnp.arange(CAP, dtype=jnp.float32)[None, None, :, None]
    slot_gates = jnp.sum(jnp.where(chosen, hit_gates[:, :, None, :], 0.0), axis=3)
    chosen = chosen.astype(low)

    causal = query_pos[:, None] >= jnp.arange(seq_len, dtype=jnp.int32)[None, :]
    query_heads = queries.reshape(sequences, span_len, KV_HEADS, group, HEAD).transpose(
        2, 0, 3, 1, 4
    )
    paired = (
        kv_all.reshape(owners, 2, sequences, span_len, KV_HEADS, HEAD)
        .transpose(1, 4, 2, 0, 3, 5)
        .reshape(2, KV_HEADS, sequences, seq_len, HEAD)
    )
    key_heads, value_heads = paired[0], paired[1]

    def head_forward(inputs):
        query_head, key_head, value_head = inputs
        scores = head_scores(query_head, key_head, causal)
        row_max = jnp.max(scores, axis=-1, keepdims=True)
        exponent = jnp.exp(scores - row_max)
        row_sum = jnp.sum(exponent, axis=-1, keepdims=True)
        weights_low = (exponent / row_sum).astype(low)
        mixed = jnp.einsum(
            "sgqt,std->sgqd", weights_low, value_head, preferred_element_type=jnp.float32
        )
        return (mixed.astype(low), row_max, row_sum)

    mixed_heads, row_maxes, row_sums = lax.map(head_forward, (query_heads, key_heads, value_heads))
    attn_mix = mixed_heads.transpose(1, 3, 0, 2, 4).reshape(tok_rows, D)
    residual = tokens + jnp.dot(attn_mix, out_low, preferred_element_type=jnp.float32)
    normed_two = rms_norm(residual, gains_used[1]).astype(low)
    normed_two_all = lax.all_gather(normed_two, "expert", axis=0, tiled=False).reshape(
        blocks, span_len, model_width
    )

    def take(rows, which):
        return jnp.einsum("brt,btd->brd", chosen[:, which], rows, preferred_element_type=jnp.float32)

    slot_rows = blocks * CAP
    slots, hidden_acts, gate_ups, outs = [], [], [], []
    for which in range(local_experts):
        slot_in = take(normed_two_all, which).astype(low).reshape(slot_rows, model_width)
        gate_up = jnp.dot(slot_in, gate_up_low[which], preferred_element_type=jnp.float32)
        hidden_act = (jax.nn.silu(gate_up[:, :FF]) * gate_up[:, FF:]).astype(low)
        result = jnp.dot(hidden_act, down_low[which], preferred_element_type=jnp.float32)
        outs.append(
            (result.reshape(blocks, CAP, model_width) * slot_gates[:, which, :, None]).astype(low)
        )
        slots.append(slot_in)
        hidden_acts.append(hidden_act)
        gate_ups.append(gate_up)
    chosen_all = chosen.reshape(blocks, local_experts * CAP, span_len)

    def combine(parts):
        joined = jnp.concatenate(parts, axis=1)
        partial = jnp.einsum("brt,brd->btd", chosen_all, joined, preferred_element_type=jnp.float32)
        return lax.psum_scatter(
            partial.astype(low).reshape(owners, tok_rows, model_width), "expert", scatter_dimension=0, tiled=False
        ).astype(jnp.float32)

    hidden_out = (
        (residual + combine(outs)).astype(low).reshape(sequences, span_len, model_width)
    )
    upstream = upstream_low.astype(jnp.float32)
    slot_backs, gate_up_backs, slot_grads = [], [], []
    for which in range(local_experts):
        slot_grad = (
            (take(upstream_all, which) * slot_gates[:, which, :, None])
            .astype(low)
            .reshape(slot_rows, model_width)
        )
        act_back = jnp.einsum("rd,fd->rf", slot_grad, down_low[which], preferred_element_type=jnp.float32)
        gate_part = gate_ups[which][:, :FF]
        up_part = gate_ups[which][:, FF:]
        sigmoid_g = jax.nn.sigmoid(gate_part)
        gate_up_back = jnp.concatenate(
            [
                act_back * up_part * sigmoid_g * (1.0 + gate_part * (1.0 - sigmoid_g)),
                act_back * gate_part * sigmoid_g,
            ],
            axis=-1,
        ).astype(low)
        slot_back = jnp.einsum(
            "rf,df->rd", gate_up_back, gate_up_low[which], preferred_element_type=jnp.float32
        ).astype(low)
        slot_backs.append(slot_back.reshape(blocks, CAP, model_width))
        gate_up_backs.append(gate_up_back)
        slot_grads.append(slot_grad)
    normed_two_back = combine(slot_backs)
    expert_grads = []
    for which in range(local_experts):
        down_grad = jnp.einsum(
            "rf,rd->fd", hidden_acts[which], slot_grads[which], preferred_element_type=jnp.float32
        ).astype(low)
        gate_up_grad = jnp.einsum(
            "rd,rf->df", slots[which], gate_up_backs[which], preferred_element_type=jnp.float32
        ).astype(low)
        expert_grads.append(
            jnp.concatenate(
                [
                    gate_up_grad.reshape(dp_size, up_rows, -1),
                    down_grad.reshape(dp_size, down_rows, -1),
                ],
                axis=1,
            )
        )
    expert_sum = scatter_experts(jnp.stack(expert_grads))
    gate_up_sum = expert_sum[:, :up_rows]
    down_sum = expert_sum[:, up_rows:]

    residual_part, gain_two_grad = norm_backward(residual, gains_used[1], normed_two_back)
    residual_back = upstream + residual_part
    mix_back = residual_back.astype(low)
    out_weight_grad = jnp.einsum(
        "rd,re->de", attn_mix, mix_back, preferred_element_type=jnp.float32
    )
    out_sum = sum_everywhere(out_weight_grad)
    attn_back = jnp.einsum(
        "re,de->rd", mix_back, out_low, preferred_element_type=jnp.float32
    ).astype(low)
    back_heads = attn_back.reshape(sequences, span_len, KV_HEADS, group, HEAD).transpose(
        2, 0, 3, 1, 4
    )

    def head_backward(inputs):
        query_head, key_head, value_head, back_head, row_max, row_sum = inputs
        scores = head_scores(query_head, key_head, causal)
        probability = jnp.exp(scores - row_max) / row_sum
        weights_low = probability.astype(low)
        weight_back = jnp.einsum(
            "sgqd,std->sgqt", back_head, value_head, preferred_element_type=jnp.float32
        )
        row_dot = jnp.sum(probability * weight_back, axis=-1, keepdims=True)
        score_back = (probability * (weight_back - row_dot)).astype(low)
        query_back = jnp.einsum(
            "sgqt,std->sgqd", score_back, key_head, preferred_element_type=jnp.float32
        ) * HEAD ** (-0.5)
        key_back = jnp.einsum(
            "sgqt,sgqd->std", score_back, query_head, preferred_element_type=jnp.float32
        ) * HEAD ** (-0.5)
        value_back = jnp.einsum(
            "sgqt,sgqd->std", weights_low, back_head, preferred_element_type=jnp.float32
        )
        return (query_back, jnp.stack([key_back, value_back]).astype(low))

    query_back, kv_term = lax.map(
        head_backward, (query_heads, key_heads, value_heads, back_heads, row_maxes, row_sums)
    )
    kv_term = kv_term.reshape(KV_HEADS, 2, sequences, owners, span_len, HEAD).transpose(3, 1, 2, 4, 0, 5)
    kv_back = lax.psum_scatter(
        kv_term.reshape(owners, 2, tok_rows, kv_width), "expert", scatter_dimension=0, tiled=False
    ).astype(jnp.float32)
    query_back = query_back.transpose(1, 3, 0, 2, 4).reshape(sequences, span_len, HEADS, HEAD)
    key_back = kv_back[0].reshape(sequences, span_len, KV_HEADS, HEAD)
    projected_back = jnp.concatenate(
        [
            rotate(query_back, cosine, -sine).reshape(tok_rows, D),
            rotate(key_back, cosine, -sine).reshape(tok_rows, kv_width),
            kv_back[1],
        ],
        axis=1,
    ).astype(low)
    qkv_grad = jnp.einsum("rd,rf->df", normed, projected_back, preferred_element_type=jnp.float32)
    normed_back = jnp.einsum(
        "rf,df->rd", projected_back, qkv_low, preferred_element_type=jnp.float32
    )
    input_part, gain_one_grad = norm_backward(tokens, gains_used[0], normed_back)
    input_grad = (residual_back + input_part).reshape(sequences, span_len, model_width)
    gains_grad = jnp.stack([gain_one_grad, gain_two_grad])
    gain_columns = jnp.zeros((model_width, 128), jnp.float32).at[:, :2].set(gains_grad.T)
    qkv_sum = sum_everywhere(jnp.concatenate([qkv_grad, gain_columns], axis=1))
    gains_sum = qkv_sum[:, qkv_grad.shape[1] : qkv_grad.shape[1] + 2].T
    qkv_sum = qkv_sum[:, : qkv_grad.shape[1]]
    rates = learning_rates()
    gains_up = adamw(norm_gains, gains_sum, gains_first, gains_second, rates[0], 0.0)
    qkv_up = adamw(qkv_weight, qkv_sum, qkv_first, qkv_second, rates[1], DECAY)
    out_up = adamw(out_weight, out_sum, out_first, out_second, rates[2], DECAY)
    gate_up_up = adamw(gate_up_weight, gate_up_sum, gate_up_first, gate_up_second, rates[3], DECAY)
    down_up = adamw(down_weight, down_sum, down_first, down_second, rates[4], DECAY)
    return (
        hidden_out,
        input_grad,
        *gains_up,
        *qkv_up,
        *out_up,
        *gate_up_up,
        *down_up,
    )


def solution(mesh):
    return jax.shard_map(
        per_device,
        mesh=mesh,
        in_specs=(
            P("dp", "expert", None),
            P("dp", "expert", None),
            P("dp", "expert", None),
            P("dp", "expert", None),
            P(None, "dp"),
            P("dp", None),
            P("dp", None),
            P("expert", "dp", None),
            P("expert", "dp", None),
            P(None, "dp"),
            P(None, "dp"),
            P("dp", None),
            P("dp", None),
            P("dp", None),
            P("dp", None),
            P("expert", "dp", None),
            P("expert", "dp", None),
            P("expert", "dp", None),
            P("expert", "dp", None),
        ),
        out_specs=(
            P("dp", "expert", None),
            P("dp", "expert", None),
            P(None, "dp"),
            P(None, "dp"),
            P(None, "dp"),
            P("dp", None),
            P("dp", None),
            P("dp", None),
            P("dp", None),
            P("dp", None),
            P("dp", None),
            P("expert", "dp", None),
            P("expert", "dp", None),
            P("expert", "dp", None),
            P("expert", "dp", None),
            P("expert", "dp", None),
            P("expert", "dp", None),
        ),
        check_vma=False,
    )
```

```python
import jax
import jax.numpy as jnp
from jax import lax
from jax.experimental import pallas as pl
from jax.experimental.layout import Layout, with_layout_constraint
from jax.experimental.pallas import tpu as pltpu
from jax.sharding import PartitionSpec as P

D = 1024
HEADS = 16
KV_HEADS = 8
HEAD = 64
EXPERTS = 32
FF = 512
TOP = 8
STEP = 10
CAP = 48


EPS_NORM = 1e-06
EPS_ADAM = 1e-08
BETA_ONE = 0.9
BETA_TWO = 0.95
DECAY = 0.1
THETA = 10000.0
NEG_FILL = -1e30


def rotation(positions):
    half_width = HEAD // 2
    frequency = jnp.power(THETA, -jnp.arange(half_width, dtype=jnp.float32) * (2.0 / HEAD))
    angles = positions[:, None] * frequency[None, :]
    return (jnp.cos(angles), jnp.sin(angles))


def rotate(values, cosine, sine):
    half_width = HEAD // 2
    first_half = values[..., :half_width]
    second_half = values[..., half_width:]
    cos_part = cosine[:, None, :]
    sin_part = sine[:, None, :]
    return jnp.concatenate(
        [
            first_half * cos_part - second_half * sin_part,
            second_half * cos_part + first_half * sin_part,
        ],
        axis=-1,
    )


def rms_norm(values, gain):
    return values * lax.rsqrt(jnp.mean(values * values, axis=-1, keepdims=True) + EPS_NORM) * gain


def norm_backward(values, gain, upstream_grad):
    result, pullback = jax.vjp(rms_norm, values, gain)
    return pullback(upstream_grad)


def adamw(weight, grad, first, second, rate, decay):
    first = BETA_ONE * first + (1.0 - BETA_ONE) * grad
    second = BETA_TWO * second + (1.0 - BETA_TWO) * grad * grad
    first_hat = first / (1.0 - BETA_ONE**STEP)
    second_hat = second / (1.0 - BETA_TWO**STEP)
    weight = weight - rate * (first_hat / (jnp.sqrt(second_hat) + EPS_ADAM) + decay * weight)
    return (first, second, weight)


def learning_rates():
    return (
        0.6,
        3.0 * (2.0 / D) ** 0.5,
        3.0 * (16.0 / D) ** 0.5,
        3.0 * D ** (-0.5),
        3.0 * (16.0 / FF) ** 0.5,
    )


def head_scores(query_head, key_head, causal):
    scores = jnp.einsum(
        "sgqd,std->sgqt", query_head, key_head, preferred_element_type=jnp.float32
    ) * HEAD ** (-0.5)
    return jnp.where(causal, scores, NEG_FILL)


VMEM_BYTES = 56 * 1024 * 1024
CHUNK = 2


def dot(left, right, left_dim, right_dim):
    return lax.dot_general(
        left, right, (((left_dim,), (right_dim,)), ((), ())), preferred_element_type=jnp.float32
    )


def turn(values, cosine, sine):
    lane = lax.broadcasted_iota(jnp.int32, values.shape, 1)
    half = HEAD // 2
    swapped = jnp.where(
        lane % HEAD < half, pltpu.roll(values, 2 * HEAD - half, 1), pltpu.roll(values, half, 1)
    )
    return values * cosine + swapped * sine


def project_kernel(normed_ref, weight_ref, cosine_ref, sine_ref, query_ref, kv_ref):
    step = pl.program_id(0)
    product = dot(normed_ref[...], weight_ref[...], 1, 0)
    halves = [product[:, : 2 * HEAD], product[:, 2 * HEAD :]]
    turned = [turn(half, cosine_ref[...], sine_ref[...]) for half in halves]

    @pl.when(step < 4)
    def _():
        query_ref[...] = (jnp.concatenate(turned, axis=1) * HEAD ** (-0.5)).astype(jnp.bfloat16)

    @pl.when((step >= 4) & (step < 6))
    def _():
        kv_ref[...] = jnp.concatenate(turned, axis=1).astype(jnp.bfloat16)

    @pl.when(step >= 6)
    def _():
        kv_ref[...] = product.astype(jnp.bfloat16)


def project(normed, weight, cosine, sine):
    rows, depth = normed.shape
    kv_width = KV_HEADS * HEAD
    return pl.pallas_call(
        project_kernel,
        grid=(8,),
        in_specs=[
            pl.BlockSpec((rows, depth), lambda i: (0, 0)),
            pl.BlockSpec((depth, 256), lambda i: (0, i)),
            pl.BlockSpec((rows, 2 * HEAD), lambda i: (0, 0)),
            pl.BlockSpec((rows, 2 * HEAD), lambda i: (0, 0)),
        ],
        out_specs=[
            pl.BlockSpec((rows, 256), lambda i: (0, jnp.minimum(i, 3))),
            pl.BlockSpec((rows, 256), lambda i: (0, jnp.maximum(i - 4, 0))),
        ],
        out_shape=[
            jax.ShapeDtypeStruct((rows, D), jnp.bfloat16),
            jax.ShapeDtypeStruct((rows, 2 * kv_width), jnp.bfloat16),
        ],
        compiler_params=pltpu.CompilerParams(vmem_limit_bytes=VMEM_BYTES),
    )(normed, weight, cosine, sine)


def spread_heads(tile):
    flipped = jnp.transpose(tile.astype(jnp.float32), (1, 0))
    blank = jnp.zeros((HEAD, flipped.shape[1]), jnp.float32)
    parts = [flipped[h * HEAD : (h + 1) * HEAD] for h in range(4)]
    return jnp.concatenate(
        [
            jnp.concatenate([parts[0], blank], axis=0),
            jnp.concatenate([parts[1], blank], axis=0),
            jnp.concatenate([blank, parts[2]], axis=0),
            jnp.concatenate([blank, parts[3]], axis=0),
        ],
        axis=1,
    )


def gather_heads(wide):
    span = wide.shape[1] // 4
    first = jnp.concatenate([wide[:HEAD, :span], wide[:HEAD, span : 2 * span]], axis=0)
    second = jnp.concatenate([wide[HEAD:, 2 * span : 3 * span], wide[HEAD:, 3 * span :]], axis=0)
    return jnp.transpose(first, (1, 0)), jnp.transpose(second, (1, 0))


def key_lead(rows, span):
    key_row = lax.broadcasted_iota(jnp.int32, (rows, 4 * span), 0)
    query_column = lax.broadcasted_iota(jnp.int32, (rows, 4 * span), 1) % span
    return key_row - query_column


def attend_kernel(place_ref, query_ref, key_ref, value_ref, mix_ref, wide_ref, stat_ref, score_ref):
    place = place_ref[0]
    owners, span, width = key_ref.shape
    query = spread_heads(query_ref[...]).astype(jnp.bfloat16)
    rows = CHUNK * span
    lead = key_lead(rows, span)
    top = jnp.full((1, 4 * span), NEG_FILL, jnp.float32)
    for chunk in range(owners // CHUNK):
        key = key_ref[chunk * CHUNK : (chunk + 1) * CHUNK].reshape(rows, width)
        scores = jnp.where(lead <= place * span - chunk * rows, dot(key, query, 1, 0), NEG_FILL)
        score_ref[chunk] = scores
        top = jnp.maximum(top, jnp.max(scores, axis=0, keepdims=True))
    total = jnp.zeros((1, 4 * span), jnp.float32)
    mixed = jnp.zeros((width, 4 * span), jnp.float32)
    for chunk in range(owners // CHUNK):
        value = value_ref[chunk * CHUNK : (chunk + 1) * CHUNK].reshape(rows, width)
        exponent = jnp.exp(score_ref[chunk] - top)
        total = total + jnp.sum(exponent, axis=0, keepdims=True)
        mixed = mixed + dot(value, exponent.astype(jnp.bfloat16), 0, 0)
    mixed = mixed / total
    wide_ref[0] = mixed
    stat_ref[0] = top + jnp.log(total)
    first, second = gather_heads(mixed)
    mix_ref[...] = jnp.concatenate([first, second], axis=1).astype(jnp.bfloat16)


def attend(place, queries, kv_all):
    owners, rows, kv_columns = kv_all.shape
    span = 128
    pairs = KV_HEADS // 2
    sequences = rows // span
    steps = sequences * pairs
    return pl.pallas_call(
        attend_kernel,
        grid=(sequences, pairs),
        in_specs=[
            pl.BlockSpec(memory_space=pltpu.SMEM),
            pl.BlockSpec((span, 4 * HEAD), lambda s, j: (s, j)),
            pl.BlockSpec((owners, span, 2 * HEAD), lambda s, j: (0, s, j)),
            pl.BlockSpec((owners, span, 2 * HEAD), lambda s, j: (0, s, j + pairs)),
        ],
        out_specs=[
            pl.BlockSpec((span, 4 * HEAD), lambda s, j: (s, j)),
            pl.BlockSpec((1, 2 * HEAD, 4 * span), lambda s, j: (s * pairs + j, 0, 0)),
            pl.BlockSpec((1, 1, 4 * span), lambda s, j: (s * pairs + j, 0, 0)),
        ],
        out_shape=[
            jax.ShapeDtypeStruct((rows, D), jnp.bfloat16),
            jax.ShapeDtypeStruct((steps, 2 * HEAD, 4 * span), jnp.float32),
            jax.ShapeDtypeStruct((steps, 1, 4 * span), jnp.float32),
        ],
        scratch_shapes=[pltpu.VMEM((owners // CHUNK, CHUNK * span, 4 * span), jnp.float32)],
        compiler_params=pltpu.CompilerParams(vmem_limit_bytes=VMEM_BYTES),
    )(place, queries, kv_all, kv_all)


def turn_back(values, cosine, sine):
    rows, columns = values.shape
    heads = values.reshape(rows, columns // HEAD, 2, HEAD // 2)
    swapped = heads[:, :, ::-1].reshape(rows, columns)
    times = columns // (2 * HEAD)
    return values * jnp.tile(cosine, (1, times)) - swapped * jnp.tile(sine, (1, times))


def attend_back_kernel(
    place_ref, query_ref, back_ref, key_ref, value_ref, wide_ref, stat_ref, cosine_ref, sine_ref,
    query_back_ref, kv_back_ref,
):
    place = place_ref[0]
    span = query_ref.shape[0]
    owners = key_ref.shape[0]
    query = spread_heads(query_ref[...]).astype(jnp.bfloat16)
    back_wide = spread_heads(back_ref[...])
    back = back_wide.astype(jnp.bfloat16)
    stat = stat_ref[0]
    row_dot = jnp.sum(back_wide * wide_ref[0], axis=0, keepdims=True)

    width = key_ref.shape[2]
    rows = CHUNK * span
    lead = key_lead(rows, span)
    total = jnp.zeros((width, 4 * span), jnp.float32)
    for chunk in range(owners // CHUNK):
        part = slice(chunk * CHUNK, (chunk + 1) * CHUNK)
        key = key_ref[part].reshape(rows, width)
        value = value_ref[part].reshape(rows, width)
        probability = jnp.exp(dot(key, query, 1, 0) - stat)
        probability = jnp.where(lead <= place * span - chunk * rows, probability, 0.0)
        weight_back = dot(value, back, 1, 0)
        score_back = (probability * (weight_back - row_dot)).astype(jnp.bfloat16)
        key_back = dot(score_back, query, 1, 1)
        value_back = dot(probability.astype(jnp.bfloat16), back, 1, 1)
        for first, result in ((0, key_back), (KV_HEADS * HEAD, value_back)):
            column = pl.multiple_of(first + pl.program_id(1) * width, width)
            kv_back_ref[part, :, pl.ds(column, width)] = result.astype(jnp.bfloat16).reshape(
                CHUNK, span, width
            )
        total = total + dot(key, score_back, 0, 0)

    halves = gather_heads(total * HEAD ** (-0.5))
    query_back_ref[...] = jnp.concatenate(
        [turn(half, cosine_ref[...], -sine_ref[...]) for half in halves], axis=1
    ).astype(jnp.bfloat16)


def attend_back(place, queries, attn_back, kv_all, wide, stat, cosine, sine):
    owners, rows, kv_columns = kv_all.shape
    span = 128
    pairs = KV_HEADS // 2
    sequences = rows // span
    kv_width = KV_HEADS * HEAD
    flat = pl.BlockSpec((span, 4 * HEAD), lambda s, j: (s, j))
    kv_block = (owners, span, 2 * HEAD)
    table = pl.BlockSpec((span, 2 * HEAD), lambda s, j: (s, 0))
    return pl.pallas_call(
        attend_back_kernel,
        grid=(sequences, pairs),
        in_specs=[
            pl.BlockSpec(memory_space=pltpu.SMEM),
            flat,
            flat,
            pl.BlockSpec(kv_block, lambda s, j: (0, s, j)),
            pl.BlockSpec(kv_block, lambda s, j: (0, s, j + pairs)),
            pl.BlockSpec((1, 2 * HEAD, 4 * span), lambda s, j: (s * pairs + j, 0, 0)),
            pl.BlockSpec((1, 1, 4 * span), lambda s, j: (s * pairs + j, 0, 0)),
            table,
            table,
        ],
        out_specs=[
            flat,
            pl.BlockSpec((owners, span, 2 * kv_width), lambda s, j: (0, s, 0)),
        ],
        out_shape=[
            jax.ShapeDtypeStruct((rows, D), jnp.bfloat16),
            jax.ShapeDtypeStruct((owners, rows, 2 * kv_width), jnp.bfloat16),
        ],
        compiler_params=pltpu.CompilerParams(vmem_limit_bytes=VMEM_BYTES),
    )(place, queries, attn_back, kv_all, kv_all, wide, stat, cosine, sine)


def pass_through(pairs, hold_ref, in_sems, out_sems):
    reads = [
        pltpu.make_async_copy(source, hold_ref.at[slot], in_sems.at[slot])
        for slot, (source, targets) in enumerate(pairs)
    ]
    for read in reads:
        read.start()
    writes = []
    for slot, (source, targets) in enumerate(pairs):
        reads[slot].wait()
        for number, (row, rows, column, columns, target) in enumerate(targets):
            write = pltpu.make_async_copy(
                hold_ref.at[slot, pl.ds(row, rows), pl.ds(column, columns)],
                target,
                out_sems.at[slot, number],
            )
            write.start()
            writes.append(write)
    for write in writes:
        write.wait()


def place_rows_kernel(
    where_ref, mine_ref, other_ref, first_ref, second_ref, extra_ref, hold_ref, in_sems, out_sems
):
    me, core = where_ref[0], where_ref[1]
    half, rest = first_ref.shape[2], extra_ref.shape[2]
    columns = first_ref.shape[3]
    pairs = []
    for source, which in ((mine_ref, core), (other_ref, 1 - core)):
        for step in range(source.shape[0]):
            targets = (
                (0, half, 0, columns, first_ref.at[me ^ step, which]),
                (0, half, columns, second_ref.shape[3], second_ref.at[me ^ step, which]),
                (half, rest, 0, columns, extra_ref.at[me ^ step, which]),
            )
            pairs.append((source.at[step], targets))
    pass_through(pairs, hold_ref, in_sems, out_sems)


def place_experts_kernel(where_ref, *refs):
    pieces, (up_ref, down_ref, hold_ref, in_sems, out_sems) = refs[:5], refs[5:]
    own, one, two, first, second = pieces
    me = where_ref[0]
    up_rows, down_rows, columns = up_ref.shape[2], down_ref.shape[2], up_ref.shape[3]
    half = first.shape[0]
    pairs = []
    for target in range(own.shape[0]):
        last = first.at[target] if target < half else second.at[target - half]
        for step, source in enumerate((own.at[target], one.at[target], two.at[target], last)):
            targets = (
                (0, up_rows, 0, columns, up_ref.at[target, step]),
                (up_rows, down_rows, 0, columns, down_ref.at[target, me ^ step]),
            )
            pairs.append((source, targets))
    pass_through(pairs, hold_ref, in_sems, out_sems)


def place(kernel, where, pieces, slots, shapes):
    anywhere = pl.BlockSpec(memory_space=pl.ANY)
    rows, columns = pieces[0].shape[-2:]
    kind = pieces[0].dtype
    return pl.pallas_call(
        kernel,
        in_specs=[pl.BlockSpec(memory_space=pltpu.SMEM)] + [anywhere] * len(pieces),
        out_specs=[anywhere] * len(shapes),
        out_shape=[jax.ShapeDtypeStruct(shape, kind) for shape in shapes],
        scratch_shapes=[
            pltpu.VMEM((slots, rows, columns), kind),
            pltpu.SemaphoreType.DMA((slots,)),
            pltpu.SemaphoreType.DMA((slots, len(shapes))),
        ],
        compiler_params=pltpu.CompilerParams(vmem_limit_bytes=VMEM_BYTES),
    )(where, *pieces)


def row_major(values):
    return with_layout_constraint(values, Layout(major_to_minor=tuple(range(values.ndim))))


def xor_pairs(size, step):
    return [(index, index ^ step) for index in range(size)]


def square_gather(first, second):
    size = lax.axis_size("dp")
    near, far = xor_pairs(size, 1), xor_pairs(size, 2)
    first_one = lax.ppermute(first, "dp", near)
    second_two = lax.ppermute(second, "dp", far)
    first_rest = lax.ppermute(jnp.stack([first, first_one]), "dp", far)
    second_rest = lax.ppermute(jnp.stack([second, second_two]), "dp", near)
    return (first, first_one, first_rest, second, second_two, second_rest)


def add_low(left, right):
    return (left.astype(jnp.float32) + right.astype(jnp.float32)).astype(jnp.bfloat16)


def square_scatter(first, second):
    size = lax.axis_size("dp")
    near, far = xor_pairs(size, 1), xor_pairs(size, 2)
    first_got = lax.ppermute(jnp.stack([first[1], first[3]]), "dp", near)
    second_got = lax.ppermute(jnp.stack([second[2], second[3]]), "dp", far)
    first_got_two = lax.ppermute(add_low(first[2], first_got[1]), "dp", far)
    second_got_two = lax.ppermute(add_low(second[1], second_got[1]), "dp", near)

    def total(own, one, two):
        return own.astype(jnp.float32) + one.astype(jnp.float32) + two.astype(jnp.float32)

    return (
        total(first[0], first_got[0], first_got_two),
        total(second[0], second_got[0], second_got_two),
    )


def gather_rows(shard, half, columns, later):
    size, cores = lax.axis_size("dp"), lax.axis_size("expert")
    rows, width = shard.shape
    if size != 4 or cores % 2:
        got = lax.all_gather(shard, "dp", axis=0, tiled=False).reshape(size, 2, rows // 2, width)
        first, second = got[:, :, :half, :columns], got[:, :, :half, columns:]
        extra = got[:, :, half:, :columns]
        return first.reshape(-1, columns), second.reshape(-1, width - columns), extra, later
    core = lax.axis_index("expert") % 2
    mine = lax.dynamic_slice_in_dim(shard, core * (rows // 2), rows // 2, 0)
    first, first_one, first_rest, second, second_two, second_rest = square_gather(
        mine[:, : width // 2], mine[:, width // 2 :]
    )
    stacked = jnp.concatenate(
        [
            jnp.stack([first, first_one, first_rest[0], first_rest[1]]),
            jnp.stack([second, second_rest[0], second_two, second_rest[1]]),
        ],
        axis=2,
    )
    stacked, later = lax.optimization_barrier((stacked, later))
    other = lax.ppermute(stacked, "expert", xor_pairs(cores, 1))
    where = jnp.stack([lax.axis_index("dp"), core]).astype(jnp.int32)
    shapes = [
        (size, 2, half, columns),
        (size, 2, half, width - columns),
        (size, 2, rows // 2 - half, columns),
    ]
    whole, second, extra = place(place_rows_kernel, where, (stacked, other), 2 * size, shapes)
    return whole.reshape(-1, columns), second.reshape(-1, width - columns), extra, later


def expert_pieces(packed):
    if lax.axis_size("dp") != 4:
        return (lax.all_gather(packed, "dp", axis=1, tiled=False),)
    return (
        packed,
        lax.ppermute(packed, "dp", xor_pairs(4, 1)),
        lax.ppermute(packed, "dp", xor_pairs(4, 2)),
    )


def expert_weights(pieces, up_rows):
    if len(pieces) == 1:
        return pieces[0][:, :, :up_rows], pieces[0][:, :, up_rows:]
    own, one, two = pieces
    experts, rows, columns = own.shape
    first = lax.ppermute(one[: experts // 2], "dp", xor_pairs(4, 2))
    second = lax.ppermute(two[experts // 2 :], "dp", xor_pairs(4, 1))
    where = lax.axis_index("dp").astype(jnp.int32).reshape(1)
    shapes = [(experts, 4, up_rows, columns), (experts, 4, rows - up_rows, columns)]
    return place(place_experts_kernel, where, (own, one, two, first, second), 4 * experts, shapes)


def by_distance(values):
    size = lax.axis_size("dp")
    if size != 4:
        return values
    rows, columns = values.shape
    blocks = values.reshape(rows, size, columns // size)
    me = lax.axis_index("dp")
    parts = [
        lax.dynamic_index_in_dim(blocks, me ^ step, 1, keepdims=False) for step in range(size)
    ]
    return jnp.concatenate(parts, axis=1)


def expert_grad_kernel(
    where_ref, slot_ref, up_back_ref, act_ref, slot_grad_ref, send_ref, keep_ref, up_ref, down_ref, *, order
):
    step = pl.program_id(0)
    up = dot(slot_ref[...], up_back_ref[...], 0, 0)
    down = dot(act_ref[...], slot_grad_ref[...], 0, 0)

    @pl.when(step == 0)
    def _():
        up_ref[...] = up
        down_ref[...] = down

    @pl.when(step > 0)
    def _():
        up_ref[...] += up
        down_ref[...] += down

    @pl.when(step == pl.num_programs(0) - 1)
    def _():
        up_rows, down_rows = up_ref.shape[0] // 4, down_ref.shape[0] // 4
        for number, part in enumerate(order):
            target = send_ref if number < 2 else keep_ref
            target[number % 2, :up_rows] = up_ref[part * up_rows : (part + 1) * up_rows].astype(jnp.bfloat16)
            row = pl.multiple_of((where_ref[0] ^ part) * down_rows, down_rows)
            target[number % 2, up_rows:] = down_ref[pl.ds(row, down_rows), :].astype(jnp.bfloat16)


def expert_grads(where, slot, up_back, act, slot_grad, order):
    rows, depth = slot.shape
    hidden, width = act.shape[1], slot_grad.shape[1]
    part_rows = (depth + hidden) // 4
    steps = 2
    blocks = [
        pl.BlockSpec((rows // steps, array.shape[1]), lambda i: (i, 0))
        for array in (slot, up_back, act, slot_grad)
    ]
    result = jax.ShapeDtypeStruct((2, part_rows, width), jnp.bfloat16)
    return pl.pallas_call(
        lambda *refs: expert_grad_kernel(*refs, order=order),
        grid=(steps,),
        in_specs=[pl.BlockSpec(memory_space=pltpu.SMEM)] + blocks,
        out_specs=[pl.BlockSpec((2, part_rows, width), lambda i: (0, 0, 0))] * 2,
        out_shape=[result, result],
        scratch_shapes=[
            pltpu.VMEM((depth, up_back.shape[1]), jnp.float32),
            pltpu.VMEM((hidden, width), jnp.float32),
        ],
        compiler_params=pltpu.CompilerParams(vmem_limit_bytes=VMEM_BYTES),
    )(where, slot, up_back, act, slot_grad)


def by_core(values):
    rows, columns = values.shape
    me, core = lax.axis_index("dp"), lax.axis_index("expert") % 2
    blocks = values.reshape(rows, 8, columns // 8)
    parts = [
        lax.dynamic_index_in_dim(blocks, 2 * (me ^ step) + side, 1, keepdims=False)
        for side in (core, 1 - core)
        for step in range(4)
    ]
    return jnp.concatenate(parts, axis=1)


def core_sums(grad):
    owners = lax.axis_size("expert")
    rows, columns = grad.shape
    grad = row_major(grad.astype(jnp.bfloat16)).reshape(2, 4, rows // 8, columns)
    return row_major(add_low(grad[0], lax.ppermute(grad[1], "expert", xor_pairs(owners, 1))))


def square_sums(pair):
    half = pair.shape[2] // 2
    summed = square_scatter(
        [pair[step, :, :half] for step in range(4)], [pair[step, :, half:] for step in range(4)]
    )
    return row_major(jnp.concatenate(summed, axis=1).astype(jnp.bfloat16))


def line_sums(total):
    owners = lax.axis_size("expert")
    place_index = lax.axis_index("expert")
    step = 2
    while step < owners:
        side = (place_index // step) % 2
        half = total.shape[0] // 2
        mine = lax.dynamic_slice_in_dim(total, side * half, half, 0)
        other = lax.dynamic_slice_in_dim(total, (1 - side) * half, half, 0)
        total = row_major(add_low(mine, lax.ppermute(other, "expert", xor_pairs(owners, step))))
        step *= 2
    while step > 1:
        step //= 2
        side = (place_index // step) % 2
        other = lax.ppermute(total, "expert", xor_pairs(owners, step))
        total = jnp.where(
            side == 0,
            jnp.concatenate([total, other], axis=0),
            jnp.concatenate([other, total], axis=0),
        )
    return row_major(total.astype(jnp.float32))


def plain_sums(grad):
    part = lax.psum_scatter(grad.astype(jnp.bfloat16), "dp", scatter_dimension=0, tiled=True)
    return lax.psum(part.astype(jnp.float32), "expert")


def per_device(
    hidden_in,
    out_grad,
    expert_ids,
    route_gates,
    norm_gains,
    qkv_weight,
    out_weight,
    gate_up_weight,
    down_weight,
    gains_first,
    gains_second,
    qkv_first,
    qkv_second,
    out_first,
    out_second,
    gate_up_first,
    gate_up_second,
    down_first,
    down_second,
):
    sequences, span_len, model_width = hidden_in.shape
    owners = lax.axis_size("expert")
    dp_size = lax.axis_size("dp")
    position = lax.axis_index("expert")
    seq_len = span_len * owners
    group = HEADS // KV_HEADS
    kv_width = KV_HEADS * HEAD
    tok_rows = sequences * span_len
    local_experts = EXPERTS // owners
    blocks = owners * sequences
    low = jnp.bfloat16

    square = dp_size == 4 and owners % 2 == 0 and owners & (owners - 1) == 0
    shard_rows = qkv_weight.shape[0]
    half_rows = shard_rows // 2
    attention_low = jnp.concatenate([qkv_weight.astype(low), out_weight.astype(low)], axis=1)
    gain_rows = jnp.zeros((16, attention_low.shape[1]), low)
    gain_rows = gain_rows.at[:2, : norm_gains.shape[1]].set(norm_gains.astype(low))
    attention_pack = jnp.concatenate(
        [attention_low[:half_rows], gain_rows, attention_low[half_rows:], gain_rows], axis=0
    )
    up_rows = gate_up_weight.shape[1]
    down_rows = down_weight.shape[1]
    packed = jnp.concatenate([gate_up_weight.astype(low), down_weight.astype(low)], axis=1)
    qkv_low, out_low, extra, packed = gather_rows(
        attention_pack, half_rows, qkv_weight.shape[1], packed
    )
    gains_used = (
        extra[:, 0, :2, : norm_gains.shape[1]]
        .transpose(1, 0, 2)
        .reshape(2, model_width)
        .astype(jnp.float32)
    )
    pieces = expert_pieces(packed)

    tokens = hidden_in.astype(jnp.float32).reshape(tok_rows, model_width)
    normed = rms_norm(tokens, gains_used[0]).astype(low)
    query_pos = position * span_len + jnp.arange(span_len, dtype=jnp.int32)
    cosine, sine = rotation(query_pos.astype(jnp.float32))
    cosine = jnp.tile(cosine, (sequences, 4))
    sine = jnp.tile(jnp.concatenate([-sine, sine], axis=1), (sequences, 2))
    queries, kv_local = project(normed, qkv_low, cosine, sine)
    gates = route_gates.reshape(tok_rows, TOP)
    gates_high = gates.astype(low)
    gates_rest = (gates - gates_high.astype(jnp.float32)).astype(low)
    routes = jnp.concatenate([expert_ids.reshape(tok_rows, TOP).astype(low), gates_high, gates_rest], axis=1)
    route_rows = -(-tok_rows * 3 * TOP // model_width)
    pad_rows = -(-route_rows // 16) * 16
    routes = jnp.pad(routes.reshape(-1), (0, pad_rows * model_width - routes.size))
    upstream_low = out_grad.reshape(tok_rows, model_width)
    upstream_pack = jnp.concatenate([upstream_low, routes.reshape(pad_rows, model_width)], axis=0)
    upstream_got = lax.all_gather(upstream_pack, "expert", axis=0, tiled=False)
    kv_local, upstream_got = lax.optimization_barrier((kv_local, upstream_got))
    kv_all = lax.all_gather(kv_local, "expert", axis=0, tiled=False)
    place_index = position.astype(jnp.int32).reshape(1)

    upstream_all = upstream_got[:, :tok_rows].reshape(blocks, span_len, model_width)
    routes_all = (
        upstream_got[:, tok_rows:]
        .reshape(owners, -1)[:, : tok_rows * 3 * TOP]
        .reshape(blocks, span_len, 3, TOP)
        .astype(jnp.float32)
    )
    local_ids = position * local_experts + jnp.arange(local_experts, dtype=jnp.int32)
    named = (routes_all[:, :, 0, None, :] == local_ids.astype(jnp.float32)[None, None, :, None]).astype(
        jnp.float32
    )
    hits = jnp.sum(named, axis=3)
    hit_gates = jnp.sum(named * (routes_all[:, :, 1] + routes_all[:, :, 2])[:, :, None, :], axis=3)
    before = jnp.tril(jnp.ones((span_len, span_len), jnp.float32), -1).astype(low)
    ranks = jnp.einsum("tu,bul->blt", before, hits.astype(low), preferred_element_type=jnp.float32)
    hits = hits.transpose(0, 2, 1)
    hit_gates = hit_gates.transpose(0, 2, 1)
    place = jnp.where(hits > 0.5, ranks, -1.0)
    chosen = place[:, :, None, :] == jnp.arange(CAP, dtype=jnp.float32)[None, None, :, None]
    slot_gates = jnp.sum(jnp.where(chosen, hit_gates[:, :, None, :], 0.0), axis=3)
    chosen = chosen.astype(low)

    attn_mix, mix_wide, mix_stat = attend(place_index, queries, kv_all)
    residual = tokens + jnp.dot(attn_mix, out_low, preferred_element_type=jnp.float32)
    normed_two = rms_norm(residual, gains_used[1]).astype(low)
    normed_two, pieces = lax.optimization_barrier((normed_two, pieces))
    gate_up_low, down_low = expert_weights(pieces, up_rows)
    gate_up_low = gate_up_low.reshape(local_experts, model_width, -1)
    down_low = down_low.reshape(local_experts, -1, model_width)
    normed_two_all = lax.all_gather(by_distance(normed_two), "expert", axis=0, tiled=False).reshape(
        blocks, span_len, model_width
    )

    def take(rows, which):
        return jnp.einsum("brt,btd->brd", chosen[:, which], rows, preferred_element_type=jnp.float32)

    slot_rows = blocks * CAP
    slot_grads, act_backs = [], []
    for which in range(local_experts):
        slot_grad = (
            (take(upstream_all, which) * slot_gates[:, which, :, None])
            .astype(low)
            .reshape(slot_rows, model_width)
        )
        slot_grads.append(slot_grad)
        act_backs.append(dot(slot_grad, down_low[which], 1, 1))
    slots, hidden_acts, gate_up_backs, slot_backs = [], [], [], []
    for which in range(local_experts):
        slot_in = take(normed_two_all, which).astype(low).reshape(slot_rows, model_width)
        gate_up = dot(slot_in, gate_up_low[which], 1, 0)
        gate_part = gate_up[:, :FF]
        up_part = gate_up[:, FF:]
        act_back = act_backs[which]
        sigmoid_g = jax.nn.sigmoid(gate_part)
        hidden_act = (gate_part * sigmoid_g * up_part).astype(low)
        gate_up_back = jnp.concatenate(
            [
                act_back * up_part * sigmoid_g * (1.0 + gate_part * (1.0 - sigmoid_g)),
                act_back * gate_part * sigmoid_g,
            ],
            axis=-1,
        ).astype(low)
        slot_back = dot(gate_up_back, gate_up_low[which], 1, 1).astype(low)
        slots.append(slot_in)
        hidden_acts.append(hidden_act)
        gate_up_backs.append(gate_up_back)
        slot_backs.append(slot_back.reshape(blocks, CAP, model_width))
    chosen_all = chosen.reshape(blocks, local_experts * CAP, span_len)

    def partial_sums(parts):
        joined = jnp.concatenate(parts, axis=1)
        partial = jnp.einsum("brt,brd->btd", chosen_all, joined, preferred_element_type=jnp.float32)
        return row_major(partial.astype(low).reshape(owners, tok_rows, model_width))

    def send_back(partial):
        return lax.psum_scatter(partial, "expert", scatter_dimension=0, tiled=False).astype(
            jnp.float32
        )

    back_part = partial_sums(slot_backs)
    back_part, hidden_acts = lax.optimization_barrier((back_part, hidden_acts))
    normed_two_back = send_back(back_part)
    outs = []
    for which in range(local_experts):
        result = dot(hidden_acts[which], down_low[which], 1, 0)
        outs.append(
            (result.reshape(blocks, CAP, model_width) * slot_gates[:, which, :, None]).astype(low)
        )
    out_part = partial_sums(outs)
    if square:
        where = lax.axis_index("dp").astype(jnp.int32).reshape(1)
        half = local_experts // 2
        near, far = xor_pairs(dp_size, 1), xor_pairs(dp_size, 2)
        keeps, gots = [None] * local_experts, [None] * local_experts
        for which in [e + side for e in range(half) for side in (0, half)]:
            first = which < half
            send, keeps[which] = expert_grads(
                where,
                slots[which],
                gate_up_backs[which],
                hidden_acts[which],
                slot_grads[which],
                (1, 3, 0, 2) if first else (2, 3, 0, 1),
            )
            gots[which] = lax.ppermute(send, "dp", near if first else far)
        normed_two_back, out_part, keeps = lax.optimization_barrier((normed_two_back, out_part, keeps))
    else:
        grads = [
            jnp.concatenate(
                [
                    dot(slots[which], gate_up_backs[which], 0, 0).reshape(dp_size, up_rows, -1),
                    dot(hidden_acts[which], slot_grads[which], 0, 0).reshape(dp_size, down_rows, -1),
                ],
                axis=1,
            )
            for which in range(local_experts)
        ]
        expert_sum = lax.psum_scatter(
            jnp.stack(grads).astype(low), "dp", scatter_dimension=1, tiled=False
        ).astype(jnp.float32)
    normed_two_back = by_distance(normed_two_back)
    upstream = upstream_low.astype(jnp.float32)

    residual_part, gain_two_grad = norm_backward(residual, gains_used[1], normed_two_back)
    residual_back = upstream + residual_part
    mix_back = residual_back.astype(low)
    attn_back = jnp.einsum(
        "re,de->rd", mix_back, out_low, preferred_element_type=jnp.float32
    ).astype(low)
    query_back, kv_term = attend_back(
        place_index, queries, attn_back, kv_all, mix_wide, mix_stat, cosine, sine
    )
    if square:
        early = [0, half]
        early_gots = [gots[which] for which in early]
        kv_term, early_gots = lax.optimization_barrier((kv_term, early_gots))
        for which, got in zip(early, early_gots):
            gots[which] = got
    kv_back = lax.psum_scatter(kv_term, "expert", scatter_dimension=0, tiled=False).astype(jnp.float32)
    if square:
        kv_back, out_part, gots = lax.optimization_barrier((kv_back, out_part, gots))
        first_next = lax.ppermute(
            jnp.stack([add_low(keeps[e][1], gots[e][1]) for e in range(half)]), "dp", far
        )
        second_next = lax.ppermute(
            jnp.stack([add_low(keeps[e][1], gots[e][1]) for e in range(half, local_experts)]), "dp", near
        )
    key_turned = turn_back(kv_back[:, :kv_width], cosine, sine)
    kv_low = jnp.concatenate([key_turned, kv_back[:, kv_width:]], axis=1).astype(low)
    projected_back = jnp.concatenate([query_back, kv_low], axis=1)
    normed_back = jnp.einsum(
        "rf,df->rd", projected_back, qkv_low, preferred_element_type=jnp.float32
    )
    input_part, gain_one_grad = norm_backward(tokens, gains_used[0], normed_back)
    input_grad = (residual_back + input_part).reshape(sequences, span_len, model_width)
    gains_grad = jnp.stack([gain_one_grad, gain_two_grad])
    gain_columns = jnp.zeros((model_width, 256), jnp.float32).at[:, :2].set(gains_grad.T)
    if square:
        normed_cut, mix_cut = by_core(normed), by_core(attn_mix)
        gain_columns = by_core(gain_columns.T).T
    else:
        normed_cut, mix_cut = normed, attn_mix
    attention_grad = jnp.concatenate(
        [
            dot(normed_cut, projected_back, 0, 0).astype(low),
            dot(mix_cut, mix_back, 0, 0).astype(low),
            gain_columns.astype(low),
        ],
        axis=1,
    )
    if square:
        pair = core_sums(attention_grad)
        first_next, second_next, pair = lax.optimization_barrier((first_next, second_next, pair))
        part = square_sums(pair)
        out_sum_low = send_back(out_part)
        part, out_sum_low = lax.optimization_barrier((part, out_sum_low))
        expert_sum = jnp.stack(
            [
                keeps[e][0].astype(jnp.float32)
                + gots[e][0].astype(jnp.float32)
                + (first_next[e] if e < half else second_next[e - half]).astype(jnp.float32)
                for e in range(local_experts)
            ]
        )
        attention_sum = line_sums(part)
    else:
        attention_sum = plain_sums(attention_grad)
        out_sum_low = send_back(out_part)
    hidden_out = (
        (residual + out_sum_low).astype(low).reshape(sequences, span_len, model_width)
    )
    qkv_width = qkv_weight.shape[1]
    qkv_sum = attention_sum[:, :qkv_width]
    out_sum = attention_sum[:, qkv_width : qkv_width + model_width]
    gains_sum = attention_sum[:, qkv_width + model_width : qkv_width + model_width + 2].T
    gate_up_sum = expert_sum[:, :up_rows]
    down_sum = expert_sum[:, up_rows:]
    rates = learning_rates()
    gains_up = adamw(norm_gains, gains_sum, gains_first, gains_second, rates[0], 0.0)
    qkv_up = adamw(qkv_weight, qkv_sum, qkv_first, qkv_second, rates[1], DECAY)
    out_up = adamw(out_weight, out_sum, out_first, out_second, rates[2], DECAY)
    gate_up_up = adamw(gate_up_weight, gate_up_sum, gate_up_first, gate_up_second, rates[3], DECAY)
    down_up = adamw(down_weight, down_sum, down_first, down_second, rates[4], DECAY)
    return (
        hidden_out,
        input_grad,
        *gains_up,
        *qkv_up,
        *out_up,
        *gate_up_up,
        *down_up,
    )


def solution(mesh):
    return jax.shard_map(
        per_device,
        mesh=mesh,
        in_specs=(
            P("dp", "expert", None),
            P("dp", "expert", None),
            P("dp", "expert", None),
            P("dp", "expert", None),
            P(None, "dp"),
            P("dp", None),
            P("dp", None),
            P("expert", "dp", None),
            P("expert", "dp", None),
            P(None, "dp"),
            P(None, "dp"),
            P("dp", None),
            P("dp", None),
            P("dp", None),
            P("dp", None),
            P("expert", "dp", None),
            P("expert", "dp", None),
            P("expert", "dp", None),
            P("expert", "dp", None),
        ),
        out_specs=(
            P("dp", "expert", None),
            P("dp", "expert", None),
            P(None, "dp"),
            P(None, "dp"),
            P(None, "dp"),
            P("dp", None),
            P("dp", None),
            P("dp", None),
            P("dp", None),
            P("dp", None),
            P("dp", None),
            P("expert", "dp", None),
            P("expert", "dp", None),
            P("expert", "dp", None),
            P("expert", "dp", None),
            P("expert", "dp", None),
            P("expert", "dp", None),
        ),
        check_vma=False,
    )
```

```python
import jax
import jax.numpy as jnp
from jax import lax
from jax.experimental import pallas as pl
from jax.experimental.layout import Layout, with_layout_constraint
from jax.experimental.pallas import tpu as pltpu
from jax.sharding import PartitionSpec as P

D = 1024
HEADS = 16
KV_HEADS = 8
HEAD = 64
EXPERTS = 32
FF = 512
TOP = 8
STEP = 10
CAP = 48


EPS_NORM = 1e-06
EPS_ADAM = 1e-08
BETA_ONE = 0.9
BETA_TWO = 0.95
DECAY = 0.1
THETA = 10000.0
NEG_FILL = -1e30


def rotation(positions):
    half_width = HEAD // 2
    frequency = jnp.power(THETA, -jnp.arange(half_width, dtype=jnp.float32) * (2.0 / HEAD))
    angles = positions[:, None] * frequency[None, :]
    return (jnp.cos(angles), jnp.sin(angles))


def rotate(values, cosine, sine):
    half_width = HEAD // 2
    first_half = values[..., :half_width]
    second_half = values[..., half_width:]
    cos_part = cosine[:, None, :]
    sin_part = sine[:, None, :]
    return jnp.concatenate(
        [
            first_half * cos_part - second_half * sin_part,
            second_half * cos_part + first_half * sin_part,
        ],
        axis=-1,
    )


def rms_norm(values, gain):
    return values * lax.rsqrt(jnp.mean(values * values, axis=-1, keepdims=True) + EPS_NORM) * gain


def norm_backward(values, gain, upstream_grad):
    result, pullback = jax.vjp(rms_norm, values, gain)
    return pullback(upstream_grad)


def adamw(weight, grad, first, second, rate, decay):
    first = BETA_ONE * first + (1.0 - BETA_ONE) * grad
    second = BETA_TWO * second + (1.0 - BETA_TWO) * grad * grad
    first_hat = first / (1.0 - BETA_ONE**STEP)
    second_hat = second / (1.0 - BETA_TWO**STEP)
    weight = weight - rate * (first_hat / (jnp.sqrt(second_hat) + EPS_ADAM) + decay * weight)
    return (first, second, weight)


def learning_rates():
    return (
        0.6,
        3.0 * (2.0 / D) ** 0.5,
        3.0 * (16.0 / D) ** 0.5,
        3.0 * D ** (-0.5),
        3.0 * (16.0 / FF) ** 0.5,
    )


def head_scores(query_head, key_head, causal):
    scores = jnp.einsum(
        "sgqd,std->sgqt", query_head, key_head, preferred_element_type=jnp.float32
    ) * HEAD ** (-0.5)
    return jnp.where(causal, scores, NEG_FILL)


VMEM_BYTES = 56 * 1024 * 1024
CHUNK = 4


def dot(left, right, left_dim, right_dim):
    return lax.dot_general(
        left, right, (((left_dim,), (right_dim,)), ((), ())), preferred_element_type=jnp.float32
    )


def turn(values, cosine, sine):
    lane = lax.broadcasted_iota(jnp.int32, values.shape, 1)
    half = HEAD // 2
    swapped = jnp.where(
        lane % HEAD < half, pltpu.roll(values, 2 * HEAD - half, 1), pltpu.roll(values, half, 1)
    )
    return values * cosine + swapped * sine


def project_kernel(normed_ref, weight_ref, cosine_ref, sine_ref, query_ref, kv_ref):
    step = pl.program_id(0)
    product = dot(normed_ref[...], weight_ref[...], 1, 0)
    def turned():
        parts = [product[:, first : first + 2 * HEAD] for first in range(0, product.shape[1], 2 * HEAD)]
        return jnp.concatenate([turn(part, cosine_ref[...], sine_ref[...]) for part in parts], axis=1)

    @pl.when(step < 2)
    def _():
        query_ref[...] = (turned() * HEAD ** (-0.5)).astype(jnp.bfloat16)

    @pl.when(step == 2)
    def _():
        kv_ref[...] = turned().astype(jnp.bfloat16)

    @pl.when(step == 3)
    def _():
        kv_ref[...] = product.astype(jnp.bfloat16)


def project(normed, weight, cosine, sine):
    rows, depth = normed.shape
    kv_width = KV_HEADS * HEAD
    return pl.pallas_call(
        project_kernel,
        grid=(4,),
        in_specs=[
            pl.BlockSpec((rows, depth), lambda i: (0, 0)),
            pl.BlockSpec((depth, 512), lambda i: (0, i)),
            pl.BlockSpec((rows, 2 * HEAD), lambda i: (0, 0)),
            pl.BlockSpec((rows, 2 * HEAD), lambda i: (0, 0)),
        ],
        out_specs=[
            pl.BlockSpec((rows, 512), lambda i: (0, jnp.minimum(i, 1))),
            pl.BlockSpec((rows, 512), lambda i: (0, jnp.maximum(i - 2, 0))),
        ],
        out_shape=[
            jax.ShapeDtypeStruct((rows, D), jnp.bfloat16),
            jax.ShapeDtypeStruct((rows, 2 * kv_width), jnp.bfloat16),
        ],
        compiler_params=pltpu.CompilerParams(vmem_limit_bytes=VMEM_BYTES),
    )(normed, weight, cosine, sine)


def spread_heads(tile):
    flipped = jnp.transpose(tile.astype(jnp.float32), (1, 0))
    blank = jnp.zeros((HEAD, flipped.shape[1]), jnp.float32)
    parts = [flipped[h * HEAD : (h + 1) * HEAD] for h in range(4)]
    return jnp.concatenate(
        [
            jnp.concatenate([parts[0], blank], axis=0),
            jnp.concatenate([parts[1], blank], axis=0),
            jnp.concatenate([blank, parts[2]], axis=0),
            jnp.concatenate([blank, parts[3]], axis=0),
        ],
        axis=1,
    )


def gather_heads(wide):
    span = wide.shape[1] // 4
    first = jnp.concatenate([wide[:HEAD, :span], wide[:HEAD, span : 2 * span]], axis=0)
    second = jnp.concatenate([wide[HEAD:, 2 * span : 3 * span], wide[HEAD:, 3 * span :]], axis=0)
    return jnp.transpose(first, (1, 0)), jnp.transpose(second, (1, 0))


def key_lead(rows, span):
    key_row = lax.broadcasted_iota(jnp.int32, (rows, 4 * span), 0)
    query_column = lax.broadcasted_iota(jnp.int32, (rows, 4 * span), 1) % span
    return key_row - query_column


def attend_kernel(place_ref, query_ref, key_ref, value_ref, mix_ref, wide_ref, stat_ref, score_ref):
    place = place_ref[0]
    owners, span, width = key_ref.shape
    query = spread_heads(query_ref[...]).astype(jnp.bfloat16)
    rows = CHUNK * span
    lead = key_lead(rows, span)
    top = jnp.full((1, 4 * span), NEG_FILL, jnp.float32)
    for chunk in range(owners // CHUNK):
        key = key_ref[chunk * CHUNK : (chunk + 1) * CHUNK].reshape(rows, width)
        scores = jnp.where(lead <= place * span - chunk * rows, dot(key, query, 1, 0), NEG_FILL)
        score_ref[chunk] = scores
        top = jnp.maximum(top, jnp.max(scores, axis=0, keepdims=True))
    total = jnp.zeros((1, 4 * span), jnp.float32)
    mixed = jnp.zeros((width, 4 * span), jnp.float32)
    for chunk in range(owners // CHUNK):
        value = value_ref[chunk * CHUNK : (chunk + 1) * CHUNK].reshape(rows, width)
        exponent = jnp.exp(score_ref[chunk] - top)
        total = total + jnp.sum(exponent, axis=0, keepdims=True)
        mixed = mixed + dot(value, exponent.astype(jnp.bfloat16), 0, 0)
    mixed = mixed / total
    wide_ref[0] = mixed
    stat_ref[0] = top + jnp.log(total)
    first, second = gather_heads(mixed)
    mix_ref[...] = jnp.concatenate([first, second], axis=1).astype(jnp.bfloat16)


def attend(place, queries, kv_all):
    owners, rows, kv_columns = kv_all.shape
    span = 128
    pairs = KV_HEADS // 2
    sequences = rows // span
    steps = sequences * pairs
    return pl.pallas_call(
        attend_kernel,
        grid=(sequences, pairs),
        in_specs=[
            pl.BlockSpec(memory_space=pltpu.SMEM),
            pl.BlockSpec((span, 4 * HEAD), lambda s, j: (s, j)),
            pl.BlockSpec((owners, span, 2 * HEAD), lambda s, j: (0, s, j)),
            pl.BlockSpec((owners, span, 2 * HEAD), lambda s, j: (0, s, j + pairs)),
        ],
        out_specs=[
            pl.BlockSpec((span, 4 * HEAD), lambda s, j: (s, j)),
            pl.BlockSpec((1, 2 * HEAD, 4 * span), lambda s, j: (s * pairs + j, 0, 0)),
            pl.BlockSpec((1, 1, 4 * span), lambda s, j: (s * pairs + j, 0, 0)),
        ],
        out_shape=[
            jax.ShapeDtypeStruct((rows, D), jnp.bfloat16),
            jax.ShapeDtypeStruct((steps, 2 * HEAD, 4 * span), jnp.float32),
            jax.ShapeDtypeStruct((steps, 1, 4 * span), jnp.float32),
        ],
        scratch_shapes=[pltpu.VMEM((owners // CHUNK, CHUNK * span, 4 * span), jnp.float32)],
        compiler_params=pltpu.CompilerParams(vmem_limit_bytes=VMEM_BYTES),
    )(place, queries, kv_all, kv_all)


def turn_back(values, cosine, sine):
    rows, columns = values.shape
    heads = values.reshape(rows, columns // HEAD, 2, HEAD // 2)
    swapped = heads[:, :, ::-1].reshape(rows, columns)
    times = columns // (2 * HEAD)
    return values * jnp.tile(cosine, (1, times)) - swapped * jnp.tile(sine, (1, times))


def attend_back_kernel(
    place_ref, query_ref, back_ref, key_ref, value_ref, wide_ref, stat_ref, cosine_ref, sine_ref,
    query_back_ref, kv_back_ref,
):
    place = place_ref[0]
    span = query_ref.shape[0]
    owners = key_ref.shape[0]
    query = spread_heads(query_ref[...]).astype(jnp.bfloat16)
    back_wide = spread_heads(back_ref[...])
    back = back_wide.astype(jnp.bfloat16)
    stat = stat_ref[0]
    row_dot = jnp.sum(back_wide * wide_ref[0], axis=0, keepdims=True)

    width = key_ref.shape[2]
    rows = CHUNK * span
    lead = key_lead(rows, span)
    total = jnp.zeros((width, 4 * span), jnp.float32)
    for chunk in range(owners // CHUNK):
        part = slice(chunk * CHUNK, (chunk + 1) * CHUNK)
        key = key_ref[part].reshape(rows, width)
        value = value_ref[part].reshape(rows, width)
        probability = jnp.exp(dot(key, query, 1, 0) - stat)
        probability = jnp.where(lead <= place * span - chunk * rows, probability, 0.0)
        weight_back = dot(value, back, 1, 0)
        score_back = (probability * (weight_back - row_dot)).astype(jnp.bfloat16)
        key_back = dot(score_back, query, 1, 1)
        value_back = dot(probability.astype(jnp.bfloat16), back, 1, 1)
        for first, result in ((0, key_back), (KV_HEADS * HEAD, value_back)):
            column = pl.multiple_of(first + pl.program_id(1) * width, width)
            kv_back_ref[part, :, pl.ds(column, width)] = result.astype(jnp.bfloat16).reshape(
                CHUNK, span, width
            )
        total = total + dot(key, score_back, 0, 0)

    halves = gather_heads(total * HEAD ** (-0.5))
    query_back_ref[...] = jnp.concatenate(
        [turn(half, cosine_ref[...], -sine_ref[...]) for half in halves], axis=1
    ).astype(jnp.bfloat16)


def attend_back(place, queries, attn_back, kv_all, wide, stat, cosine, sine):
    owners, rows, kv_columns = kv_all.shape
    span = 128
    pairs = KV_HEADS // 2
    sequences = rows // span
    kv_width = KV_HEADS * HEAD
    flat = pl.BlockSpec((span, 4 * HEAD), lambda s, j: (s, j))
    kv_block = (owners, span, 2 * HEAD)
    table = pl.BlockSpec((span, 2 * HEAD), lambda s, j: (s, 0))
    return pl.pallas_call(
        attend_back_kernel,
        grid=(sequences, pairs),
        in_specs=[
            pl.BlockSpec(memory_space=pltpu.SMEM),
            flat,
            flat,
            pl.BlockSpec(kv_block, lambda s, j: (0, s, j)),
            pl.BlockSpec(kv_block, lambda s, j: (0, s, j + pairs)),
            pl.BlockSpec((1, 2 * HEAD, 4 * span), lambda s, j: (s * pairs + j, 0, 0)),
            pl.BlockSpec((1, 1, 4 * span), lambda s, j: (s * pairs + j, 0, 0)),
            table,
            table,
        ],
        out_specs=[
            flat,
            pl.BlockSpec((owners, span, 2 * kv_width), lambda s, j: (0, s, 0)),
        ],
        out_shape=[
            jax.ShapeDtypeStruct((rows, D), jnp.bfloat16),
            jax.ShapeDtypeStruct((owners, rows, 2 * kv_width), jnp.bfloat16),
        ],
        compiler_params=pltpu.CompilerParams(vmem_limit_bytes=VMEM_BYTES),
    )(place, queries, attn_back, kv_all, kv_all, wide, stat, cosine, sine)


def pass_through(pairs, hold_ref, in_sems, out_sems):
    reads = [
        pltpu.make_async_copy(source, hold_ref.at[slot], in_sems.at[slot])
        for slot, (source, targets) in enumerate(pairs)
    ]
    for read in reads:
        read.start()
    writes = []
    for slot, (source, targets) in enumerate(pairs):
        reads[slot].wait()
        for number, (row, rows, column, columns, target) in enumerate(targets):
            write = pltpu.make_async_copy(
                hold_ref.at[slot, pl.ds(row, rows), pl.ds(column, columns)],
                target,
                out_sems.at[slot, number],
            )
            write.start()
            writes.append(write)
    for write in writes:
        write.wait()


def place_rows_kernel(
    where_ref, mine_ref, other_ref, first_ref, second_ref, extra_ref, hold_ref, in_sems, out_sems
):
    me, core = where_ref[0], where_ref[1]
    half, rest = first_ref.shape[2], extra_ref.shape[2]
    columns = first_ref.shape[3]
    pairs = []
    for source, which in ((mine_ref, core), (other_ref, 1 - core)):
        for step in range(source.shape[0]):
            targets = (
                (0, half, 0, columns, first_ref.at[me ^ step, which]),
                (0, half, columns, second_ref.shape[3], second_ref.at[me ^ step, which]),
                (half, rest, 0, columns, extra_ref.at[me ^ step, which]),
            )
            pairs.append((source.at[step], targets))
    pass_through(pairs, hold_ref, in_sems, out_sems)


def place_experts_kernel(where_ref, *refs):
    hold_ref, in_sems, out_sems = refs[-3:]
    experts = hold_ref.shape[0] // 4
    sources = refs[: len(refs) - 3 - 2 * experts]
    ups, downs = refs[len(sources) : len(sources) + experts], refs[len(sources) + experts : -3]
    me = where_ref[0]
    up_rows, down_rows, columns = ups[0].shape[1], downs[0].shape[1], ups[0].shape[2]
    pairs = []
    target = 0
    for first in range(0, len(sources), 4):
        for index in range(sources[first].shape[0]):
            for step, source in enumerate(sources[first : first + 4]):
                targets = (
                    (0, up_rows, 0, columns, ups[target].at[step]),
                    (up_rows, down_rows, 0, columns, downs[target].at[me ^ step]),
                )
                pairs.append((source.at[index], targets))
            target += 1
    pass_through(pairs, hold_ref, in_sems, out_sems)


def place(kernel, where, pieces, slots, shapes):
    anywhere = pl.BlockSpec(memory_space=pl.ANY)
    rows, columns = pieces[0].shape[-2:]
    kind = pieces[0].dtype
    return pl.pallas_call(
        kernel,
        in_specs=[pl.BlockSpec(memory_space=pltpu.SMEM)] + [anywhere] * len(pieces),
        out_specs=[anywhere] * len(shapes),
        out_shape=[jax.ShapeDtypeStruct(shape, kind) for shape in shapes],
        scratch_shapes=[
            pltpu.VMEM((slots, rows, columns), kind),
            pltpu.SemaphoreType.DMA((slots,)),
            pltpu.SemaphoreType.DMA((slots, 3)),
        ],
        compiler_params=pltpu.CompilerParams(vmem_limit_bytes=VMEM_BYTES),
    )(where, *pieces)


def row_major(values):
    return with_layout_constraint(values, Layout(major_to_minor=tuple(range(values.ndim))))


def xor_pairs(size, step):
    return [(index, index ^ step) for index in range(size)]


def square_gather(first, second):
    size = lax.axis_size("dp")
    near, far = xor_pairs(size, 1), xor_pairs(size, 2)
    first_one = lax.ppermute(first, "dp", near)
    second_two = lax.ppermute(second, "dp", far)
    first_rest = lax.ppermute(jnp.stack([first, first_one]), "dp", far)
    second_rest = lax.ppermute(jnp.stack([second, second_two]), "dp", near)
    return (first, first_one, first_rest, second, second_two, second_rest)


def add_low(left, right):
    return (left.astype(jnp.float32) + right.astype(jnp.float32)).astype(jnp.bfloat16)


def square_scatter(first, second):
    size = lax.axis_size("dp")
    near, far = xor_pairs(size, 1), xor_pairs(size, 2)
    first_got = lax.ppermute(jnp.stack([first[1], first[3]]), "dp", near)
    second_got = lax.ppermute(jnp.stack([second[2], second[3]]), "dp", far)
    first_got_two = lax.ppermute(add_low(first[2], first_got[1]), "dp", far)
    second_got_two = lax.ppermute(add_low(second[1], second_got[1]), "dp", near)

    def total(own, one, two):
        return own.astype(jnp.float32) + one.astype(jnp.float32) + two.astype(jnp.float32)

    return (
        total(first[0], first_got[0], first_got_two),
        total(second[0], second_got[0], second_got_two),
    )


def gather_rows(shard, half, columns, later):
    size, cores = lax.axis_size("dp"), lax.axis_size("expert")
    rows, width = shard.shape
    if size != 4 or cores % 2:
        got = lax.all_gather(shard, "dp", axis=0, tiled=False).reshape(size, 2, rows // 2, width)
        first, second = got[:, :, :half, :columns], got[:, :, :half, columns:]
        extra = got[:, :, half:, :columns]
        return first.reshape(-1, columns), second.reshape(-1, width - columns), extra, later
    core = lax.axis_index("expert") % 2
    mine = lax.dynamic_slice_in_dim(shard, core * (rows // 2), rows // 2, 0)
    first, first_one, first_rest, second, second_two, second_rest = square_gather(
        mine[:, : width // 2], mine[:, width // 2 :]
    )
    stacked = jnp.concatenate(
        [
            jnp.stack([first, first_one, first_rest[0], first_rest[1]]),
            jnp.stack([second, second_rest[0], second_two, second_rest[1]]),
        ],
        axis=2,
    )
    stacked, later = lax.optimization_barrier((stacked, later))
    other = lax.ppermute(stacked, "expert", xor_pairs(cores, 1))
    where = jnp.stack([lax.axis_index("dp"), core]).astype(jnp.int32)
    shapes = [
        (size, 2, half, columns),
        (size, 2, half, width - columns),
        (size, 2, rows // 2 - half, columns),
    ]
    whole, second, extra = place(place_rows_kernel, where, (stacked, other), 2 * size, shapes)
    return whole.reshape(-1, columns), second.reshape(-1, width - columns), extra, later


def expert_pieces(packed):
    if lax.axis_size("dp") != 4:
        return (lax.all_gather(packed, "dp", axis=1, tiled=False),)
    return (
        packed,
        lax.ppermute(packed, "dp", xor_pairs(4, 1)),
        lax.ppermute(packed, "dp", xor_pairs(4, 2)),
    )


def expert_groups(experts):
    half = max(experts // 2, 1)
    bounds = sorted({0, min(1, half), half, experts})
    return [slice(first, last) for first, last in zip(bounds[:-1], bounds[1:])]


def expert_weights(pieces, up_rows):
    if len(pieces[0]) == 1:
        got = jnp.concatenate([piece[0] for piece in pieces], axis=0)
        experts, columns = got.shape[0], got.shape[3]
        ups = [got[e, :, :up_rows].reshape(-1, columns) for e in range(experts)]
        downs = [got[e, :, up_rows:].reshape(-1, columns) for e in range(experts)]
        return ups, downs
    passed = [lax.ppermute(piece[1], "dp", xor_pairs(4, 2)) for piece in pieces[:-1]]
    passed.append(lax.ppermute(pieces[-1][2], "dp", xor_pairs(4, 1)))
    where = lax.axis_index("dp").astype(jnp.int32).reshape(1)
    experts = sum(piece[0].shape[0] for piece in pieces)
    rows, columns = pieces[0][0].shape[1:]
    shapes = [(4, up_rows, columns)] * experts + [(4, rows - up_rows, columns)] * experts
    sources = [part for piece, last in zip(pieces, passed) for part in (*piece, last)]
    placed = place(place_experts_kernel, where, sources, 4 * experts, shapes)
    placed = [part.reshape(-1, columns) for part in placed]
    return placed[:experts], placed[experts:]


def by_distance(values):
    size = lax.axis_size("dp")
    if size != 4:
        return values
    width = values.shape[1] // size
    me = lax.axis_index("dp")
    parts = [
        lax.dynamic_slice_in_dim(values, (me ^ step) * width, width, 1) for step in range(size)
    ]
    return jnp.concatenate(parts, axis=1)


def expert_grad_kernel(
    where_ref, slot_ref, up_back_ref, act_ref, slot_grad_ref, send_ref, keep_ref, up_ref, down_ref, *, order
):
    step = pl.program_id(0)
    up = dot(slot_ref[...], up_back_ref[...], 0, 0)
    down = dot(act_ref[...], slot_grad_ref[...], 0, 0)

    @pl.when(step == 0)
    def _():
        up_ref[...] = up
        down_ref[...] = down

    @pl.when(step > 0)
    def _():
        up_ref[...] += up
        down_ref[...] += down

    @pl.when(step == pl.num_programs(0) - 1)
    def _():
        up_rows, down_rows = up_ref.shape[0] // 4, down_ref.shape[0] // 4
        for number, part in enumerate(order):
            target = send_ref if number < 2 else keep_ref
            target[number % 2, :up_rows] = up_ref[part * up_rows : (part + 1) * up_rows].astype(jnp.bfloat16)
            row = pl.multiple_of((where_ref[0] ^ part) * down_rows, down_rows)
            target[number % 2, up_rows:] = down_ref[pl.ds(row, down_rows), :].astype(jnp.bfloat16)


def expert_grads(where, slot, up_back, act, slot_grad, order):
    rows, depth = slot.shape
    hidden, width = act.shape[1], slot_grad.shape[1]
    part_rows = (depth + hidden) // 4
    steps = 2
    blocks = [
        pl.BlockSpec((rows // steps, array.shape[1]), lambda i: (i, 0))
        for array in (slot, up_back, act, slot_grad)
    ]
    result = jax.ShapeDtypeStruct((2, part_rows, width), jnp.bfloat16)
    return pl.pallas_call(
        lambda *refs: expert_grad_kernel(*refs, order=order),
        grid=(steps,),
        in_specs=[pl.BlockSpec(memory_space=pltpu.SMEM)] + blocks,
        out_specs=[pl.BlockSpec((2, part_rows, width), lambda i: (0, 0, 0))] * 2,
        out_shape=[result, result],
        scratch_shapes=[
            pltpu.VMEM((depth, up_back.shape[1]), jnp.float32),
            pltpu.VMEM((hidden, width), jnp.float32),
        ],
        compiler_params=pltpu.CompilerParams(vmem_limit_bytes=VMEM_BYTES),
    )(where, slot, up_back, act, slot_grad)


def by_core(values):
    width = values.shape[1] // 8
    me, core = lax.axis_index("dp"), lax.axis_index("expert") % 2
    parts = [
        lax.dynamic_slice_in_dim(values, (2 * (me ^ step) + side) * width, width, 1)
        for side in (core, 1 - core)
        for step in range(4)
    ]
    return jnp.concatenate(parts, axis=1)


def core_sums(grad):
    owners = lax.axis_size("expert")
    rows, columns = grad.shape
    grad = row_major(grad.astype(jnp.bfloat16)).reshape(2, 4, rows // 8, columns)
    return row_major(add_low(grad[0], lax.ppermute(grad[1], "expert", xor_pairs(owners, 1))))


def square_sums(pair):
    half = pair.shape[2] // 2
    summed = square_scatter(
        [pair[step, :, :half] for step in range(4)], [pair[step, :, half:] for step in range(4)]
    )
    return row_major(jnp.concatenate(summed, axis=1).astype(jnp.bfloat16))


def line_reduce(total):
    owners = lax.axis_size("expert")
    place_index = lax.axis_index("expert")
    step = 2
    while step < owners:
        side = (place_index // step) % 2
        half = total.shape[0] // 2
        mine = lax.dynamic_slice_in_dim(total, side * half, half, 0)
        other = lax.dynamic_slice_in_dim(total, (1 - side) * half, half, 0)
        total = row_major(add_low(mine, lax.ppermute(other, "expert", xor_pairs(owners, step))))
        step *= 2
    return total


def line_gather(total):
    step = lax.axis_size("expert")
    place_index = lax.axis_index("expert")
    while step > 1:
        step //= 2
        side = (place_index // step) % 2
        other = lax.ppermute(total, "expert", xor_pairs(lax.axis_size("expert"), step))
        total = jnp.where(
            side == 0,
            jnp.concatenate([total, other], axis=0),
            jnp.concatenate([other, total], axis=0),
        )
    return row_major(total.astype(jnp.float32))


def plain_sums(grad):
    part = lax.psum_scatter(grad.astype(jnp.bfloat16), "dp", scatter_dimension=0, tiled=True)
    return lax.psum(part.astype(jnp.float32), "expert")


def per_device(
    hidden_in,
    out_grad,
    expert_ids,
    route_gates,
    norm_gains,
    qkv_weight,
    out_weight,
    gate_up_weight,
    down_weight,
    gains_first,
    gains_second,
    qkv_first,
    qkv_second,
    out_first,
    out_second,
    gate_up_first,
    gate_up_second,
    down_first,
    down_second,
):
    sequences, span_len, model_width = hidden_in.shape
    owners = lax.axis_size("expert")
    dp_size = lax.axis_size("dp")
    position = lax.axis_index("expert")
    seq_len = span_len * owners
    group = HEADS // KV_HEADS
    kv_width = KV_HEADS * HEAD
    tok_rows = sequences * span_len
    local_experts = EXPERTS // owners
    blocks = owners * sequences
    low = jnp.bfloat16

    square = dp_size == 4 and owners % 2 == 0 and owners & (owners - 1) == 0
    shard_rows = qkv_weight.shape[0]
    half_rows = shard_rows // 2
    attention_low = jnp.concatenate([qkv_weight.astype(low), out_weight.astype(low)], axis=1)
    gain_rows = jnp.zeros((16, attention_low.shape[1]), low)
    gain_rows = gain_rows.at[:2, : norm_gains.shape[1]].set(norm_gains.astype(low))
    attention_pack = jnp.concatenate(
        [attention_low[:half_rows], gain_rows, attention_low[half_rows:], gain_rows], axis=0
    )
    query_pos = position * span_len + jnp.arange(span_len, dtype=jnp.int32)
    cosine, sine = rotation(query_pos.astype(jnp.float32))
    cosine = row_major(jnp.tile(cosine, (sequences, 4)))
    sine = row_major(jnp.tile(jnp.concatenate([-sine, sine], axis=1), (sequences, 2)))
    up_rows = gate_up_weight.shape[1]
    down_rows = down_weight.shape[1]
    packed = jnp.concatenate([gate_up_weight.astype(low), down_weight.astype(low)], axis=1)
    packed = [packed[span] for span in expert_groups(local_experts)]
    qkv_low, out_low, extra, (packed, cosine, sine) = gather_rows(
        attention_pack, half_rows, qkv_weight.shape[1], (packed, cosine, sine)
    )
    gains_used = (
        extra[:, 0, :2, : norm_gains.shape[1]]
        .transpose(1, 0, 2)
        .reshape(2, model_width)
        .astype(jnp.float32)
    )
    pieces = [expert_pieces(part) for part in packed]

    tokens = hidden_in.astype(jnp.float32).reshape(tok_rows, model_width)
    normed = rms_norm(tokens, gains_used[0]).astype(low)
    queries, kv_local = project(normed, qkv_low, cosine, sine)
    gates = route_gates.reshape(tok_rows, TOP)
    gates_high = gates.astype(low)
    gates_rest = (gates - gates_high.astype(jnp.float32)).astype(low)
    routes = jnp.concatenate([expert_ids.reshape(tok_rows, TOP).astype(low), gates_high, gates_rest], axis=1)
    route_rows = -(-tok_rows * 3 * TOP // model_width)
    pad_rows = -(-route_rows // 16) * 16
    routes = jnp.pad(routes.reshape(-1), (0, pad_rows * model_width - routes.size))
    upstream_low = out_grad.reshape(tok_rows, model_width)
    upstream_pack = jnp.concatenate([upstream_low, routes.reshape(pad_rows, model_width)], axis=0)
    upstream_got = lax.all_gather(upstream_pack, "expert", axis=0, tiled=False)
    kv_local, upstream_got, pieces[0] = lax.optimization_barrier((kv_local, upstream_got, pieces[0]))
    kv_all = lax.all_gather(kv_local, "expert", axis=0, tiled=False)
    place_index = position.astype(jnp.int32).reshape(1)

    upstream_all = upstream_got[:, :tok_rows].reshape(blocks, span_len, model_width)
    routes_all = (
        upstream_got[:, tok_rows:]
        .reshape(owners, -1)[:, : tok_rows * 3 * TOP]
        .reshape(blocks, span_len, 3, TOP)
        .astype(jnp.float32)
    )
    local_ids = position * local_experts + jnp.arange(local_experts, dtype=jnp.int32)
    named = (routes_all[:, :, 0, None, :] == local_ids.astype(jnp.float32)[None, None, :, None]).astype(
        jnp.float32
    )
    hits = jnp.sum(named, axis=3)
    hit_gates = jnp.sum(named * (routes_all[:, :, 1] + routes_all[:, :, 2])[:, :, None, :], axis=3)
    before = jnp.tril(jnp.ones((span_len, span_len), jnp.float32), -1).astype(low)
    ranks = jnp.einsum("tu,bul->blt", before, hits.astype(low), preferred_element_type=jnp.float32)
    hits = hits.transpose(0, 2, 1)
    hit_gates = hit_gates.transpose(0, 2, 1)
    place = jnp.where(hits > 0.5, ranks, -1.0)
    chosen = place[:, :, None, :] == jnp.arange(CAP, dtype=jnp.float32)[None, None, :, None]
    slot_gates = jnp.sum(jnp.where(chosen, hit_gates[:, :, None, :], 0.0), axis=3)
    chosen = chosen.astype(low)

    attn_mix, mix_wide, mix_stat = attend(place_index, queries, kv_all)
    residual = tokens + jnp.dot(attn_mix, out_low, preferred_element_type=jnp.float32)
    normed_two = rms_norm(residual, gains_used[1]).astype(low)
    normed_two, pieces, chosen, slot_gates = lax.optimization_barrier(
        (normed_two, pieces, chosen, slot_gates)
    )
    gate_up_low, down_low = expert_weights(pieces, up_rows)
    normed_two_all = lax.all_gather(by_distance(normed_two), "expert", axis=0, tiled=False).reshape(
        blocks, span_len, model_width
    )

    def take(rows, which):
        return jnp.einsum("brt,btd->brd", chosen[:, which], rows, preferred_element_type=jnp.float32)

    slot_rows = blocks * CAP
    slot_grads, act_backs = [], []
    for which in range(local_experts):
        slot_grad = (
            (take(upstream_all, which) * slot_gates[:, which, :, None])
            .astype(low)
            .reshape(slot_rows, model_width)
        )
        slot_grads.append(slot_grad)
        act_backs.append(dot(slot_grad, down_low[which], 1, 1))
    slots, hidden_acts, gate_up_backs, slot_backs = [], [], [], []
    for which in range(local_experts):
        slot_in = take(normed_two_all, which).astype(low).reshape(slot_rows, model_width)
        gate_up = dot(slot_in, gate_up_low[which], 1, 0)
        gate_part = gate_up[:, :FF]
        up_part = gate_up[:, FF:]
        act_back = act_backs[which]
        sigmoid_g = jax.nn.sigmoid(gate_part)
        hidden_act = (gate_part * sigmoid_g * up_part).astype(low)
        gate_up_back = jnp.concatenate(
            [
                act_back * up_part * sigmoid_g * (1.0 + gate_part * (1.0 - sigmoid_g)),
                act_back * gate_part * sigmoid_g,
            ],
            axis=-1,
        ).astype(low)
        slot_back = dot(gate_up_back, gate_up_low[which], 1, 1).astype(low)
        slots.append(slot_in)
        hidden_acts.append(hidden_act)
        gate_up_backs.append(gate_up_back)
        slot_backs.append(slot_back.reshape(blocks, CAP, model_width))
    chosen_all = chosen.reshape(blocks, local_experts * CAP, span_len)

    def partial_sums(parts):
        joined = jnp.concatenate(parts, axis=1)
        partial = jnp.einsum("brt,brd->btd", chosen_all, joined, preferred_element_type=jnp.float32)
        return row_major(partial.astype(low).reshape(owners, tok_rows, model_width))

    def send_back(partial):
        return lax.psum_scatter(partial, "expert", scatter_dimension=0, tiled=False)

    back_part = partial_sums(slot_backs)
    back_part, hidden_acts = lax.optimization_barrier((back_part, hidden_acts))
    normed_two_back = send_back(back_part)
    outs = []
    for which in range(local_experts):
        result = dot(hidden_acts[which], down_low[which], 1, 0)
        outs.append(
            (result.reshape(blocks, CAP, model_width) * slot_gates[:, which, :, None]).astype(low)
        )
    out_part = partial_sums(outs)
    if square:
        where = lax.axis_index("dp").astype(jnp.int32).reshape(1)
        half = local_experts // 2
        near, far = xor_pairs(dp_size, 1), xor_pairs(dp_size, 2)
        keeps, gots = [None] * local_experts, [None] * local_experts
        for which in [e + side for e in range(half) for side in (0, half)]:
            first = which < half
            send, keeps[which] = expert_grads(
                where,
                slots[which],
                gate_up_backs[which],
                hidden_acts[which],
                slot_grads[which],
                (1, 3, 0, 2) if first else (2, 3, 0, 1),
            )
            gots[which] = lax.ppermute(send, "dp", near if first else far)
        normed_two_back, out_part, keeps = lax.optimization_barrier((normed_two_back, out_part, keeps))
    else:
        grads = [
            jnp.concatenate(
                [
                    dot(slots[which], gate_up_backs[which], 0, 0).reshape(dp_size, up_rows, -1),
                    dot(hidden_acts[which], slot_grads[which], 0, 0).reshape(dp_size, down_rows, -1),
                ],
                axis=1,
            )
            for which in range(local_experts)
        ]
        expert_sum = lax.psum_scatter(
            jnp.stack(grads).astype(low), "dp", scatter_dimension=1, tiled=False
        ).astype(jnp.float32)
    normed_two_back = by_distance(normed_two_back).astype(jnp.float32)
    upstream = upstream_low.astype(jnp.float32)

    residual_part, gain_two_grad = norm_backward(residual, gains_used[1], normed_two_back)
    residual_back = upstream + residual_part
    mix_back = residual_back.astype(low)
    attn_back = jnp.einsum(
        "re,de->rd", mix_back, out_low, preferred_element_type=jnp.float32
    ).astype(low)
    query_back, kv_term = attend_back(
        place_index, queries, attn_back, kv_all, mix_wide, mix_stat, cosine, sine
    )
    if square:
        early = [0, half]
        early_gots = [gots[which] for which in early]
        kv_term, early_gots = lax.optimization_barrier((kv_term, early_gots))
        for which, got in zip(early, early_gots):
            gots[which] = got

    kv_back = lax.psum_scatter(kv_term, "expert", scatter_dimension=0, tiled=False).astype(jnp.float32)
    if square:
        normed_cut, mix_cut = by_core(normed), by_core(attn_mix)
        early_pair = core_sums(
            jnp.concatenate(
                [dot(normed_cut, query_back, 0, 0).astype(low), dot(mix_cut, mix_back, 0, 0).astype(low)],
                axis=1,
            )
        )
        kv_back, out_part, gots, early_pair = lax.optimization_barrier(
            (kv_back, out_part, gots, early_pair)
        )
    key_turned = turn_back(kv_back[:, :kv_width], cosine, sine)
    kv_low = jnp.concatenate([key_turned, kv_back[:, kv_width:]], axis=1).astype(low)
    projected_back = jnp.concatenate([query_back, kv_low], axis=1)
    normed_back = jnp.einsum(
        "rf,df->rd", projected_back, qkv_low, preferred_element_type=jnp.float32
    )
    input_part, gain_one_grad = norm_backward(tokens, gains_used[0], normed_back)
    input_grad = (residual_back + input_part).reshape(sequences, span_len, model_width)
    gains_grad = jnp.stack([gain_one_grad, gain_two_grad])
    qkv_width = qkv_weight.shape[1]
    if square:
        late_pair = core_sums(dot(normed_cut, kv_low, 0, 0))
        gain_rows = by_distance(gains_grad).reshape(2, 4, -1).transpose(1, 0, 2)
        gain_rows = jnp.pad(gain_rows.reshape(4, half_rows, -1).astype(low), ((0, 0), (0, 0), (0, 256 - 4)))
        gain_rows = row_major(gain_rows)
        gain_pair = row_major(
            add_low(gain_rows, lax.ppermute(gain_rows, "expert", xor_pairs(owners, 1)))
        )
        summed = [add_low(keeps[which][1], gots[which][1]) for which in range(local_experts)]
        summed = (jnp.stack(summed[:half]), jnp.stack(summed[half:]))
        part = square_sums(jnp.concatenate([early_pair, late_pair, gain_pair], axis=2))
        out_sum_low = send_back(out_part)
        part, out_sum_low, summed = lax.optimization_barrier((part, out_sum_low, summed))
        first_last = lax.ppermute(summed[0], "dp", far)
        second_last = lax.ppermute(summed[1], "dp", near)
        part, first_last, second_last = lax.optimization_barrier(
            (line_reduce(part), first_last, second_last)
        )
        expert_sum = jnp.stack(
            [
                keeps[e][0].astype(jnp.float32)
                + gots[e][0].astype(jnp.float32)
                + (first_last[e] if e < half else second_last[e - half]).astype(jnp.float32)
                for e in range(local_experts)
            ]
        )
        attention_sum = line_gather(part)
    else:
        query_grad, kv_grad = dot(normed, query_back, 0, 0), dot(normed, kv_low, 0, 0)
        out_grad_sum = dot(attn_mix, mix_back, 0, 0)
        attention_sum = plain_sums(
            jnp.concatenate([query_grad, out_grad_sum, kv_grad, gains_grad.T], axis=1)
        )
        out_sum_low = send_back(out_part)
    hidden_out = (
        (residual + out_sum_low).astype(low).reshape(sequences, span_len, model_width)
    )
    kv_first = 2 * model_width
    qkv_sum = jnp.concatenate(
        [attention_sum[:, :D], attention_sum[:, kv_first : kv_first + qkv_width - D]], axis=1
    )
    out_sum = attention_sum[:, model_width:kv_first]
    gain_first = model_width + qkv_width
    if square:
        gains_sum = attention_sum[:half_rows, gain_first : gain_first + 4].reshape(2, -1)
    else:
        gains_sum = attention_sum[:, gain_first : gain_first + 2].T
    gains_sum = row_major(gains_sum)
    gate_up_sum = expert_sum[:, :up_rows]
    down_sum = expert_sum[:, up_rows:]
    rates = learning_rates()
    gains_up = adamw(norm_gains, gains_sum, gains_first, gains_second, rates[0], 0.0)
    qkv_up = adamw(qkv_weight, qkv_sum, qkv_first, qkv_second, rates[1], DECAY)
    out_up = adamw(out_weight, out_sum, out_first, out_second, rates[2], DECAY)
    gate_up_up = adamw(gate_up_weight, gate_up_sum, gate_up_first, gate_up_second, rates[3], DECAY)
    down_up = adamw(down_weight, down_sum, down_first, down_second, rates[4], DECAY)
    return (
        hidden_out,
        input_grad,
        *gains_up,
        *qkv_up,
        *out_up,
        *gate_up_up,
        *down_up,
    )


def solution(mesh):
    return jax.shard_map(
        per_device,
        mesh=mesh,
        in_specs=(
            P("dp", "expert", None),
            P("dp", "expert", None),
            P("dp", "expert", None),
            P("dp", "expert", None),
            P(None, "dp"),
            P("dp", None),
            P("dp", None),
            P("expert", "dp", None),
            P("expert", "dp", None),
            P(None, "dp"),
            P(None, "dp"),
            P("dp", None),
            P("dp", None),
            P("dp", None),
            P("dp", None),
            P("expert", "dp", None),
            P("expert", "dp", None),
            P("expert", "dp", None),
            P("expert", "dp", None),
        ),
        out_specs=(
            P("dp", "expert", None),
            P("dp", "expert", None),
            P(None, "dp"),
            P(None, "dp"),
            P(None, "dp"),
            P("dp", None),
            P("dp", None),
            P("dp", None),
            P("dp", None),
            P("dp", None),
            P("dp", None),
            P("expert", "dp", None),
            P("expert", "dp", None),
            P("expert", "dp", None),
            P("expert", "dp", None),
            P("expert", "dp", None),
            P("expert", "dp", None),
        ),
        check_vma=False,
    )
```

```python
import jax
import jax.numpy as jnp
from jax import lax
from jax.experimental import pallas as pl
from jax.experimental.layout import Layout, with_layout_constraint
from jax.experimental.pallas import tpu as pltpu
from jax.sharding import PartitionSpec as P

D = 1024
HEADS = 16
KV_HEADS = 8
HEAD = 64
EXPERTS = 32
FF = 512
TOP = 8
STEP = 10
CAP = 48


EPS_NORM = 1e-06
EPS_ADAM = 1e-08
BETA_ONE = 0.9
BETA_TWO = 0.95
DECAY = 0.1
THETA = 10000.0
NEG_FILL = -1e30


def rotation(positions):
    half_width = HEAD // 2
    frequency = jnp.power(THETA, -jnp.arange(half_width, dtype=jnp.float32) * (2.0 / HEAD))
    angles = positions[:, None] * frequency[None, :]
    return (jnp.cos(angles), jnp.sin(angles))


def rotate(values, cosine, sine):
    half_width = HEAD // 2
    first_half = values[..., :half_width]
    second_half = values[..., half_width:]
    cos_part = cosine[:, None, :]
    sin_part = sine[:, None, :]
    return jnp.concatenate(
        [
            first_half * cos_part - second_half * sin_part,
            second_half * cos_part + first_half * sin_part,
        ],
        axis=-1,
    )


def rms_norm(values, gain):
    return values * lax.rsqrt(jnp.mean(values * values, axis=-1, keepdims=True) + EPS_NORM) * gain


def norm_backward(values, gain, upstream_grad):
    result, pullback = jax.vjp(rms_norm, values, gain)
    return pullback(upstream_grad)


def adamw(weight, grad, first, second, rate, decay):
    first = BETA_ONE * first + (1.0 - BETA_ONE) * grad
    second = BETA_TWO * second + (1.0 - BETA_TWO) * grad * grad
    first_hat = first / (1.0 - BETA_ONE**STEP)
    second_hat = second / (1.0 - BETA_TWO**STEP)
    weight = weight - rate * (first_hat / (jnp.sqrt(second_hat) + EPS_ADAM) + decay * weight)
    return (first, second, weight)


def learning_rates():
    return (
        0.6,
        3.0 * (2.0 / D) ** 0.5,
        3.0 * (16.0 / D) ** 0.5,
        3.0 * D ** (-0.5),
        3.0 * (16.0 / FF) ** 0.5,
    )


def head_scores(query_head, key_head, causal):
    scores = jnp.einsum(
        "sgqd,std->sgqt", query_head, key_head, preferred_element_type=jnp.float32
    ) * HEAD ** (-0.5)
    return jnp.where(causal, scores, NEG_FILL)


VMEM_BYTES = 56 * 1024 * 1024
CHUNK = 4


def dot(left, right, left_dim, right_dim):
    return lax.dot_general(
        left, right, (((left_dim,), (right_dim,)), ((), ())), preferred_element_type=jnp.float32
    )


def turn(values, cosine, sine):
    lane = lax.broadcasted_iota(jnp.int32, values.shape, 1)
    half = HEAD // 2
    swapped = jnp.where(
        lane % HEAD < half, pltpu.roll(values, 2 * HEAD - half, 1), pltpu.roll(values, half, 1)
    )
    return values * cosine + swapped * sine


def project_kernel(normed_ref, weight_ref, cosine_ref, sine_ref, query_ref, kv_ref):
    step = pl.program_id(0)
    product = dot(normed_ref[...], weight_ref[...], 1, 0)
    def turned():
        parts = [product[:, first : first + 2 * HEAD] for first in range(0, product.shape[1], 2 * HEAD)]
        return jnp.concatenate([turn(part, cosine_ref[...], sine_ref[...]) for part in parts], axis=1)

    @pl.when(step < 2)
    def _():
        query_ref[...] = (turned() * HEAD ** (-0.5)).astype(jnp.bfloat16)

    @pl.when(step == 2)
    def _():
        kv_ref[...] = turned().astype(jnp.bfloat16)

    @pl.when(step == 3)
    def _():
        kv_ref[...] = product.astype(jnp.bfloat16)


def project(normed, weight, cosine, sine):
    rows, depth = normed.shape
    kv_width = KV_HEADS * HEAD
    return pl.pallas_call(
        project_kernel,
        grid=(4,),
        in_specs=[
            pl.BlockSpec((rows, depth), lambda i: (0, 0)),
            pl.BlockSpec((depth, 512), lambda i: (0, i)),
            pl.BlockSpec((rows, 2 * HEAD), lambda i: (0, 0)),
            pl.BlockSpec((rows, 2 * HEAD), lambda i: (0, 0)),
        ],
        out_specs=[
            pl.BlockSpec((rows, 512), lambda i: (0, jnp.minimum(i, 1))),
            pl.BlockSpec((rows, 512), lambda i: (0, jnp.maximum(i - 2, 0))),
        ],
        out_shape=[
            jax.ShapeDtypeStruct((rows, D), jnp.bfloat16),
            jax.ShapeDtypeStruct((rows, 2 * kv_width), jnp.bfloat16),
        ],
        compiler_params=pltpu.CompilerParams(vmem_limit_bytes=VMEM_BYTES),
    )(normed, weight, cosine, sine)


def spread_heads(tile):
    flipped = jnp.transpose(tile.astype(jnp.float32), (1, 0))
    blank = jnp.zeros((HEAD, flipped.shape[1]), jnp.float32)
    parts = [flipped[h * HEAD : (h + 1) * HEAD] for h in range(4)]
    return jnp.concatenate(
        [
            jnp.concatenate([parts[0], blank], axis=0),
            jnp.concatenate([parts[1], blank], axis=0),
            jnp.concatenate([blank, parts[2]], axis=0),
            jnp.concatenate([blank, parts[3]], axis=0),
        ],
        axis=1,
    )


def gather_heads(wide):
    span = wide.shape[1] // 4
    first = jnp.concatenate([wide[:HEAD, :span], wide[:HEAD, span : 2 * span]], axis=0)
    second = jnp.concatenate([wide[HEAD:, 2 * span : 3 * span], wide[HEAD:, 3 * span :]], axis=0)
    return jnp.transpose(first, (1, 0)), jnp.transpose(second, (1, 0))


def key_lead(rows, span):
    key_row = lax.broadcasted_iota(jnp.int32, (rows, 4 * span), 0)
    query_column = lax.broadcasted_iota(jnp.int32, (rows, 4 * span), 1) % span
    return key_row - query_column


def attend_kernel(place_ref, query_ref, key_ref, value_ref, mix_ref, wide_ref, stat_ref, score_ref):
    place = place_ref[0]
    owners, span, width = key_ref.shape
    query = spread_heads(query_ref[...]).astype(jnp.bfloat16)
    rows = CHUNK * span
    lead = key_lead(rows, span)
    top = jnp.full((1, 4 * span), NEG_FILL, jnp.float32)
    for chunk in range(owners // CHUNK):
        key = key_ref[chunk * CHUNK : (chunk + 1) * CHUNK].reshape(rows, width)
        scores = jnp.where(lead <= place * span - chunk * rows, dot(key, query, 1, 0), NEG_FILL)
        score_ref[chunk] = scores
        top = jnp.maximum(top, jnp.max(scores, axis=0, keepdims=True))
    total = jnp.zeros((1, 4 * span), jnp.float32)
    mixed = jnp.zeros((width, 4 * span), jnp.float32)
    for chunk in range(owners // CHUNK):
        value = value_ref[chunk * CHUNK : (chunk + 1) * CHUNK].reshape(rows, width)
        exponent = jnp.exp(score_ref[chunk] - top)
        total = total + jnp.sum(exponent, axis=0, keepdims=True)
        mixed = mixed + dot(value, exponent.astype(jnp.bfloat16), 0, 0)
    mixed = mixed / total
    wide_ref[0] = mixed
    stat_ref[0] = top + jnp.log(total)
    first, second = gather_heads(mixed)
    mix_ref[...] = jnp.concatenate([first, second], axis=1).astype(jnp.bfloat16)


def attend(place, queries, kv_all):
    owners, rows, kv_columns = kv_all.shape
    span = 128
    pairs = KV_HEADS // 2
    sequences = rows // span
    steps = sequences * pairs
    return pl.pallas_call(
        attend_kernel,
        grid=(sequences, pairs),
        in_specs=[
            pl.BlockSpec(memory_space=pltpu.SMEM),
            pl.BlockSpec((span, 4 * HEAD), lambda s, j: (s, j)),
            pl.BlockSpec((owners, span, 2 * HEAD), lambda s, j: (0, s, j)),
            pl.BlockSpec((owners, span, 2 * HEAD), lambda s, j: (0, s, j + pairs)),
        ],
        out_specs=[
            pl.BlockSpec((span, 4 * HEAD), lambda s, j: (s, j)),
            pl.BlockSpec((1, 2 * HEAD, 4 * span), lambda s, j: (s * pairs + j, 0, 0)),
            pl.BlockSpec((1, 1, 4 * span), lambda s, j: (s * pairs + j, 0, 0)),
        ],
        out_shape=[
            jax.ShapeDtypeStruct((rows, D), jnp.bfloat16),
            jax.ShapeDtypeStruct((steps, 2 * HEAD, 4 * span), jnp.float32),
            jax.ShapeDtypeStruct((steps, 1, 4 * span), jnp.float32),
        ],
        scratch_shapes=[pltpu.VMEM((owners // CHUNK, CHUNK * span, 4 * span), jnp.float32)],
        compiler_params=pltpu.CompilerParams(vmem_limit_bytes=VMEM_BYTES),
    )(place, queries, kv_all, kv_all)


def turn_back_kernel(values_ref, cosine_ref, sine_ref, turned_ref):
    width = 2 * HEAD
    for first in range(0, values_ref.shape[1], width):
        part = values_ref[:, first : first + width]
        if first < KV_HEADS * HEAD:
            part = turn(part.astype(jnp.float32), cosine_ref[...], -sine_ref[...]).astype(jnp.bfloat16)
        turned_ref[:, first : first + width] = part


def turn_back(values, cosine, sine):
    return pl.pallas_call(
        turn_back_kernel,
        out_shape=jax.ShapeDtypeStruct(values.shape, jnp.bfloat16),
        compiler_params=pltpu.CompilerParams(vmem_limit_bytes=VMEM_BYTES),
    )(values, cosine, sine)


def attend_back_kernel(
    place_ref, query_ref, back_ref, key_ref, value_ref, wide_ref, stat_ref, cosine_ref, sine_ref,
    query_back_ref, kv_back_ref,
):
    place = place_ref[0]
    span = query_ref.shape[0]
    owners = key_ref.shape[0]
    query = spread_heads(query_ref[...]).astype(jnp.bfloat16)
    back_wide = spread_heads(back_ref[...])
    back = back_wide.astype(jnp.bfloat16)
    stat = stat_ref[0]
    row_dot = jnp.sum(back_wide * wide_ref[0], axis=0, keepdims=True)

    width = key_ref.shape[2]
    rows = CHUNK * span
    lead = key_lead(rows, span)
    total = jnp.zeros((width, 4 * span), jnp.float32)
    for chunk in range(owners // CHUNK):
        part = slice(chunk * CHUNK, (chunk + 1) * CHUNK)
        key = key_ref[part].reshape(rows, width)
        value = value_ref[part].reshape(rows, width)
        probability = jnp.exp(dot(key, query, 1, 0) - stat)
        probability = jnp.where(lead <= place * span - chunk * rows, probability, 0.0)
        weight_back = dot(value, back, 1, 0)
        score_back = (probability * (weight_back - row_dot)).astype(jnp.bfloat16)
        key_back = dot(score_back, query, 1, 1)
        value_back = dot(probability.astype(jnp.bfloat16), back, 1, 1)
        for first, result in ((0, key_back), (KV_HEADS * HEAD, value_back)):
            column = pl.multiple_of(first + pl.program_id(1) * width, width)
            kv_back_ref[part, :, pl.ds(column, width)] = result.astype(jnp.bfloat16).reshape(
                CHUNK, span, width
            )
        total = total + dot(key, score_back, 0, 0)

    halves = gather_heads(total * HEAD ** (-0.5))
    query_back_ref[...] = jnp.concatenate(
        [turn(half, cosine_ref[...], -sine_ref[...]) for half in halves], axis=1
    ).astype(jnp.bfloat16)


def attend_back(place, queries, attn_back, kv_all, wide, stat, cosine, sine):
    owners, rows, kv_columns = kv_all.shape
    span = 128
    pairs = KV_HEADS // 2
    sequences = rows // span
    kv_width = KV_HEADS * HEAD
    flat = pl.BlockSpec((span, 4 * HEAD), lambda s, j: (s, j))
    kv_block = (owners, span, 2 * HEAD)
    table = pl.BlockSpec((span, 2 * HEAD), lambda s, j: (s, 0))
    return pl.pallas_call(
        attend_back_kernel,
        grid=(sequences, pairs),
        in_specs=[
            pl.BlockSpec(memory_space=pltpu.SMEM),
            flat,
            flat,
            pl.BlockSpec(kv_block, lambda s, j: (0, s, j)),
            pl.BlockSpec(kv_block, lambda s, j: (0, s, j + pairs)),
            pl.BlockSpec((1, 2 * HEAD, 4 * span), lambda s, j: (s * pairs + j, 0, 0)),
            pl.BlockSpec((1, 1, 4 * span), lambda s, j: (s * pairs + j, 0, 0)),
            table,
            table,
        ],
        out_specs=[
            flat,
            pl.BlockSpec((owners, span, 2 * kv_width), lambda s, j: (0, s, 0)),
        ],
        out_shape=[
            jax.ShapeDtypeStruct((rows, D), jnp.bfloat16),
            jax.ShapeDtypeStruct((owners, rows, 2 * kv_width), jnp.bfloat16),
        ],
        compiler_params=pltpu.CompilerParams(vmem_limit_bytes=VMEM_BYTES),
    )(place, queries, attn_back, kv_all, kv_all, wide, stat, cosine, sine)


def pass_through(pairs, hold_ref, in_sems, out_sems):
    reads = [
        pltpu.make_async_copy(source, hold_ref.at[slot], in_sems.at[slot])
        for slot, (source, targets) in enumerate(pairs)
    ]
    for read in reads:
        read.start()
    writes = []
    for slot, (source, targets) in enumerate(pairs):
        reads[slot].wait()
        for number, (row, rows, column, columns, target) in enumerate(targets):
            write = pltpu.make_async_copy(
                hold_ref.at[slot, pl.ds(row, rows), pl.ds(column, columns)],
                target,
                out_sems.at[slot, number],
            )
            write.start()
            writes.append(write)
    for write in writes:
        write.wait()


def place_rows_kernel(
    where_ref, mine_ref, other_ref, first_ref, second_ref, extra_ref, hold_ref, in_sems, out_sems
):
    me, core = where_ref[0], where_ref[1]
    half, rest = first_ref.shape[2], extra_ref.shape[2]
    columns = first_ref.shape[3]
    pairs = []
    for source, which in ((mine_ref, core), (other_ref, 1 - core)):
        for step in range(source.shape[0]):
            targets = (
                (0, half, 0, columns, first_ref.at[me ^ step, which]),
                (0, half, columns, second_ref.shape[3], second_ref.at[me ^ step, which]),
                (half, rest, 0, columns, extra_ref.at[me ^ step, which]),
            )
            pairs.append((source.at[step], targets))
    pass_through(pairs, hold_ref, in_sems, out_sems)


def place_experts_kernel(where_ref, *refs):
    hold_ref, in_sems, out_sems = refs[-3:]
    experts = hold_ref.shape[0] // 4
    sources = refs[: len(refs) - 3 - 2 * experts]
    ups, downs = refs[len(sources) : len(sources) + experts], refs[len(sources) + experts : -3]
    me = where_ref[0]
    up_rows, down_rows, columns = ups[0].shape[1], downs[0].shape[1], ups[0].shape[2]
    pairs = []
    target = 0
    for first in range(0, len(sources), 4):
        for index in range(sources[first].shape[0]):
            for step, source in enumerate(sources[first : first + 4]):
                targets = (
                    (0, up_rows, 0, columns, ups[target].at[step]),
                    (up_rows, down_rows, 0, columns, downs[target].at[me ^ step]),
                )
                pairs.append((source.at[index], targets))
            target += 1
    pass_through(pairs, hold_ref, in_sems, out_sems)


def place(kernel, where, pieces, slots, shapes):
    anywhere = pl.BlockSpec(memory_space=pl.ANY)
    rows, columns = pieces[0].shape[-2:]
    kind = pieces[0].dtype
    return pl.pallas_call(
        kernel,
        in_specs=[pl.BlockSpec(memory_space=pltpu.SMEM)] + [anywhere] * len(pieces),
        out_specs=[anywhere] * len(shapes),
        out_shape=[jax.ShapeDtypeStruct(shape, kind) for shape in shapes],
        scratch_shapes=[
            pltpu.VMEM((slots, rows, columns), kind),
            pltpu.SemaphoreType.DMA((slots,)),
            pltpu.SemaphoreType.DMA((slots, 3)),
        ],
        compiler_params=pltpu.CompilerParams(vmem_limit_bytes=VMEM_BYTES),
    )(where, *pieces)


def row_major(values):
    return with_layout_constraint(values, Layout(major_to_minor=tuple(range(values.ndim))))


def xor_pairs(size, step):
    return [(index, index ^ step) for index in range(size)]


def square_gather(first, second):
    size = lax.axis_size("dp")
    near, far = xor_pairs(size, 1), xor_pairs(size, 2)
    first_one = lax.ppermute(first, "dp", near)
    second_two = lax.ppermute(second, "dp", far)
    first_rest = lax.ppermute(jnp.stack([first, first_one]), "dp", far)
    second_rest = lax.ppermute(jnp.stack([second, second_two]), "dp", near)
    return (first, first_one, first_rest, second, second_two, second_rest)


def add_low(left, right):
    return (left.astype(jnp.float32) + right.astype(jnp.float32)).astype(jnp.bfloat16)


def gather_rows(shard, half, columns, later):
    size, cores = lax.axis_size("dp"), lax.axis_size("expert")
    rows, width = shard.shape
    if size != 4 or cores % 2:
        got = lax.all_gather(shard, "dp", axis=0, tiled=False).reshape(size, 2, rows // 2, width)
        first, second = got[:, :, :half, :columns], got[:, :, :half, columns:]
        extra = got[:, :, half:, :columns]
        return first.reshape(-1, columns), second.reshape(-1, width - columns), extra, later
    core = lax.axis_index("expert") % 2
    mine = lax.dynamic_slice_in_dim(shard, core * (rows // 2), rows // 2, 0)
    first, first_one, first_rest, second, second_two, second_rest = square_gather(
        mine[:, : width // 2], mine[:, width // 2 :]
    )
    stacked = jnp.concatenate(
        [
            jnp.stack([first, first_one, first_rest[0], first_rest[1]]),
            jnp.stack([second, second_rest[0], second_two, second_rest[1]]),
        ],
        axis=2,
    )
    stacked, later = lax.optimization_barrier((stacked, later))
    other = lax.ppermute(stacked, "expert", xor_pairs(cores, 1))
    where = jnp.stack([lax.axis_index("dp"), core]).astype(jnp.int32)
    shapes = [
        (size, 2, half, columns),
        (size, 2, half, width - columns),
        (size, 2, rows // 2 - half, columns),
    ]
    whole, second, extra = place(place_rows_kernel, where, (stacked, other), 2 * size, shapes)
    return whole.reshape(-1, columns), second.reshape(-1, width - columns), extra, later


def expert_pieces(packed):
    if lax.axis_size("dp") != 4:
        return (lax.all_gather(packed, "dp", axis=1, tiled=False),)
    return (
        packed,
        lax.ppermute(packed, "dp", xor_pairs(4, 1)),
        lax.ppermute(packed, "dp", xor_pairs(4, 2)),
    )


def expert_groups(experts):
    half = max(experts // 2, 1)
    bounds = sorted({0, min(1, half), half, experts})
    return [slice(first, last) for first, last in zip(bounds[:-1], bounds[1:])]


def expert_weights(pieces, up_rows):
    if len(pieces[0]) == 1:
        got = jnp.concatenate([piece[0] for piece in pieces], axis=0)
        experts, columns = got.shape[0], got.shape[3]
        ups = [got[e, :, :up_rows].reshape(-1, columns) for e in range(experts)]
        downs = [got[e, :, up_rows:].reshape(-1, columns) for e in range(experts)]
        return ups, downs
    passed = [lax.ppermute(piece[1], "dp", xor_pairs(4, 2)) for piece in pieces[:-1]]
    passed.append(lax.ppermute(pieces[-1][2], "dp", xor_pairs(4, 1)))
    where = lax.axis_index("dp").astype(jnp.int32).reshape(1)
    experts = sum(piece[0].shape[0] for piece in pieces)
    rows, columns = pieces[0][0].shape[1:]
    shapes = [(4, up_rows, columns)] * experts + [(4, rows - up_rows, columns)] * experts
    sources = [part for piece, last in zip(pieces, passed) for part in (*piece, last)]
    placed = place(place_experts_kernel, where, sources, 4 * experts, shapes)
    placed = [part.reshape(-1, columns) for part in placed]
    return placed[:experts], placed[experts:]


def by_distance(values):
    size = lax.axis_size("dp")
    if size != 4:
        return values
    width = values.shape[1] // size
    me = lax.axis_index("dp")
    parts = [
        lax.dynamic_slice_in_dim(values, (me ^ step) * width, width, 1) for step in range(size)
    ]
    return jnp.concatenate(parts, axis=1)


def expert_grad_kernel(
    where_ref, slot_ref, up_back_ref, act_ref, slot_grad_ref, *refs, order
):
    parts, (up_ref, down_ref) = refs[:4], refs[4:]
    step = pl.program_id(0)
    up = dot(slot_ref[...], up_back_ref[...], 0, 0)
    down = dot(act_ref[...], slot_grad_ref[...], 0, 0)

    @pl.when(step == 0)
    def _():
        up_ref[...] = up
        down_ref[...] = down

    @pl.when(step > 0)
    def _():
        up_ref[...] += up
        down_ref[...] += down

    @pl.when(step == pl.num_programs(0) - 1)
    def _():
        up_rows, down_rows = up_ref.shape[0] // 4, down_ref.shape[0] // 4
        for target, part in zip(parts, order):
            target[:up_rows] = up_ref[part * up_rows : (part + 1) * up_rows].astype(jnp.bfloat16)
            row = pl.multiple_of((where_ref[0] ^ part) * down_rows, down_rows)
            target[up_rows:] = down_ref[pl.ds(row, down_rows), :].astype(jnp.bfloat16)


def expert_grads(where, slot, up_back, act, slot_grad, order):
    rows, depth = slot.shape
    hidden, width = act.shape[1], slot_grad.shape[1]
    part_rows = (depth + hidden) // 4
    steps = 2
    blocks = [
        pl.BlockSpec((rows // steps, array.shape[1]), lambda i: (i, 0))
        for array in (slot, up_back, act, slot_grad)
    ]
    result = jax.ShapeDtypeStruct((part_rows, width), jnp.bfloat16)
    return pl.pallas_call(
        lambda *refs: expert_grad_kernel(*refs, order=order),
        grid=(steps,),
        in_specs=[pl.BlockSpec(memory_space=pltpu.SMEM)] + blocks,
        out_specs=[pl.BlockSpec((part_rows, width), lambda i: (0, 0))] * 4,
        out_shape=[result] * 4,
        scratch_shapes=[
            pltpu.VMEM((depth, up_back.shape[1]), jnp.float32),
            pltpu.VMEM((hidden, width), jnp.float32),
        ],
        compiler_params=pltpu.CompilerParams(vmem_limit_bytes=VMEM_BYTES),
    )(where, slot, up_back, act, slot_grad)


def by_core(values):
    width = values.shape[1] // 8
    me, core = lax.axis_index("dp"), lax.axis_index("expert") % 2
    parts = [
        lax.dynamic_slice_in_dim(values, (2 * (me ^ step) + side) * width, width, 1)
        for side in (core, 1 - core)
        for step in range(4)
    ]
    return jnp.concatenate(parts, axis=1)


def core_sums(grad):
    owners = lax.axis_size("expert")
    rows, columns = grad.shape
    grad = row_major(grad.astype(jnp.bfloat16)).reshape(2, 4, rows // 8, columns)
    return row_major(add_low(grad[0], lax.ppermute(grad[1], "expert", xor_pairs(owners, 1))))


def square_start(pair):
    half = pair.shape[2] // 2
    first, second = pair[:, :, :half], pair[:, :, half:]
    return (
        lax.ppermute(jnp.stack([first[1], first[3]]), "dp", xor_pairs(4, 1)),
        lax.ppermute(jnp.stack([second[2], second[3]]), "dp", xor_pairs(4, 2)),
    )


def square_finish(pair, gots):
    half = pair.shape[2] // 2
    first, second = pair[:, :, :half], pair[:, :, half:]
    first_last = lax.ppermute(add_low(first[2], gots[0][1]), "dp", xor_pairs(4, 2))
    second_last = lax.ppermute(add_low(second[1], gots[1][1]), "dp", xor_pairs(4, 1))

    def total(own, one, two):
        return own.astype(jnp.float32) + one.astype(jnp.float32) + two.astype(jnp.float32)

    parts = [total(first[0], gots[0][0], first_last), total(second[0], gots[1][0], second_last)]
    return row_major(jnp.concatenate(parts, axis=1).astype(jnp.bfloat16))


def line_reduce(total, step, most):
    owners = lax.axis_size("expert")
    place_index = lax.axis_index("expert")
    while step < most:
        side = (place_index // step) % 2
        half = total.shape[0] // 2
        mine = lax.dynamic_slice_in_dim(total, side * half, half, 0)
        other = lax.dynamic_slice_in_dim(total, (1 - side) * half, half, 0)
        total = row_major(add_low(mine, lax.ppermute(other, "expert", xor_pairs(owners, step))))
        step *= 2
    return total


def line_gather(total, step, least):
    place_index = lax.axis_index("expert")
    while step > least:
        step //= 2
        side = (place_index // step) % 2
        other = lax.ppermute(total, "expert", xor_pairs(lax.axis_size("expert"), step))
        total = jnp.where(
            side == 0,
            jnp.concatenate([total, other], axis=0),
            jnp.concatenate([other, total], axis=0),
        )
    return row_major(total)


def plain_sums(grad):
    part = lax.psum_scatter(grad.astype(jnp.bfloat16), "dp", scatter_dimension=0, tiled=True)
    return lax.psum(part.astype(jnp.float32), "expert")


def per_device(
    hidden_in,
    out_grad,
    expert_ids,
    route_gates,
    norm_gains,
    qkv_weight,
    out_weight,
    gate_up_weight,
    down_weight,
    gains_first,
    gains_second,
    qkv_first,
    qkv_second,
    out_first,
    out_second,
    gate_up_first,
    gate_up_second,
    down_first,
    down_second,
):
    sequences, span_len, model_width = hidden_in.shape
    owners = lax.axis_size("expert")
    dp_size = lax.axis_size("dp")
    position = lax.axis_index("expert")
    seq_len = span_len * owners
    group = HEADS // KV_HEADS
    kv_width = KV_HEADS * HEAD
    tok_rows = sequences * span_len
    local_experts = EXPERTS // owners
    blocks = owners * sequences
    low = jnp.bfloat16

    square = dp_size == 4 and owners % 2 == 0 and owners & (owners - 1) == 0
    shard_rows = qkv_weight.shape[0]
    half_rows = shard_rows // 2
    attention_low = jnp.concatenate([qkv_weight.astype(low), out_weight.astype(low)], axis=1)
    gain_rows = jnp.zeros((16, attention_low.shape[1]), low)
    gain_rows = gain_rows.at[:2, : norm_gains.shape[1]].set(norm_gains.astype(low))
    attention_pack = jnp.concatenate(
        [attention_low[:half_rows], gain_rows, attention_low[half_rows:], gain_rows], axis=0
    )
    query_pos = position * span_len + jnp.arange(span_len, dtype=jnp.int32)
    cosine, sine = rotation(query_pos.astype(jnp.float32))
    cosine = row_major(jnp.tile(cosine, (sequences, 4)))
    sine = row_major(jnp.tile(jnp.concatenate([-sine, sine], axis=1), (sequences, 2)))
    up_rows = gate_up_weight.shape[1]
    down_rows = down_weight.shape[1]
    packed = jnp.concatenate([gate_up_weight.astype(low), down_weight.astype(low)], axis=1)
    packed = [packed[span] for span in expert_groups(local_experts)]
    qkv_low, out_low, extra, (packed, cosine, sine) = gather_rows(
        attention_pack, half_rows, qkv_weight.shape[1], (packed, cosine, sine)
    )
    gains_used = (
        extra[:, 0, :2, : norm_gains.shape[1]]
        .transpose(1, 0, 2)
        .reshape(2, model_width)
        .astype(jnp.float32)
    )
    pieces = [expert_pieces(part) for part in packed]

    tokens = hidden_in.astype(jnp.float32).reshape(tok_rows, model_width)
    normed = rms_norm(tokens, gains_used[0]).astype(low)
    queries, kv_local = project(normed, qkv_low, cosine, sine)
    gates = route_gates.reshape(tok_rows, TOP)
    gates_high = gates.astype(low)
    gates_rest = (gates - gates_high.astype(jnp.float32)).astype(low)
    routes = jnp.concatenate([expert_ids.reshape(tok_rows, TOP).astype(low), gates_high, gates_rest], axis=1)
    route_rows = -(-tok_rows * 3 * TOP // model_width)
    pad_rows = -(-route_rows // 16) * 16
    routes = jnp.pad(routes.reshape(-1), (0, pad_rows * model_width - routes.size))
    upstream_low = out_grad.reshape(tok_rows, model_width)
    upstream_pack = jnp.concatenate([upstream_low, routes.reshape(pad_rows, model_width)], axis=0)
    upstream_got = lax.all_gather(upstream_pack, "expert", axis=0, tiled=False)
    kv_local, upstream_got, pieces[0] = lax.optimization_barrier((kv_local, upstream_got, pieces[0]))
    kv_all = lax.all_gather(kv_local, "expert", axis=0, tiled=False)
    place_index = position.astype(jnp.int32).reshape(1)

    upstream_all = upstream_got[:, :tok_rows].reshape(blocks, span_len, model_width)
    routes_all = (
        upstream_got[:, tok_rows:]
        .reshape(owners, -1)[:, : tok_rows * 3 * TOP]
        .reshape(blocks, span_len, 3, TOP)
        .astype(jnp.float32)
    )
    local_ids = position * local_experts + jnp.arange(local_experts, dtype=jnp.int32)
    named = (routes_all[:, :, 0, None, :] == local_ids.astype(jnp.float32)[None, None, :, None]).astype(
        jnp.float32
    )
    hits = jnp.sum(named, axis=3)
    hit_gates = jnp.sum(named * (routes_all[:, :, 1] + routes_all[:, :, 2])[:, :, None, :], axis=3)
    before = jnp.tril(jnp.ones((span_len, span_len), jnp.float32), -1).astype(low)
    ranks = jnp.einsum("tu,bul->blt", before, hits.astype(low), preferred_element_type=jnp.float32)
    hits = hits.transpose(0, 2, 1)
    hit_gates = hit_gates.transpose(0, 2, 1)
    place = jnp.where(hits > 0.5, ranks, -1.0)
    chosen = place[:, :, None, :] == jnp.arange(CAP, dtype=jnp.float32)[None, None, :, None]
    slot_gates = jnp.sum(jnp.where(chosen, hit_gates[:, :, None, :], 0.0), axis=3)
    chosen = chosen.astype(low)

    attn_mix, mix_wide, mix_stat = attend(place_index, queries, kv_all)
    residual = tokens + jnp.dot(attn_mix, out_low, preferred_element_type=jnp.float32)
    normed_two = rms_norm(residual, gains_used[1]).astype(low)
    normed_two, pieces, chosen, slot_gates = lax.optimization_barrier(
        (normed_two, pieces, chosen, slot_gates)
    )
    gate_up_low, down_low = expert_weights(pieces, up_rows)
    normed_two_all = lax.all_gather(by_distance(normed_two), "expert", axis=0, tiled=False).reshape(
        blocks, span_len, model_width
    )

    if square:
        normed_cut, mix_cut = by_core(normed), by_core(attn_mix)
        normed_two_all, normed_cut, mix_cut = lax.optimization_barrier(
            (normed_two_all, normed_cut, mix_cut)
        )

    def take(rows, which):
        return jnp.einsum("brt,btd->brd", chosen[:, which], rows, preferred_element_type=jnp.float32)

    slot_rows = blocks * CAP
    slot_grads, act_backs = [], []
    for which in range(local_experts):
        slot_grad = (
            (take(upstream_all, which) * slot_gates[:, which, :, None])
            .astype(low)
            .reshape(slot_rows, model_width)
        )
        slot_grads.append(slot_grad)
        act_backs.append(dot(slot_grad, down_low[which], 1, 1))
    slots, hidden_acts, gate_up_backs, slot_backs = [], [], [], []
    for which in range(local_experts):
        slot_in = take(normed_two_all, which).astype(low).reshape(slot_rows, model_width)
        gate_up = dot(slot_in, gate_up_low[which], 1, 0)
        gate_part = gate_up[:, :FF]
        up_part = gate_up[:, FF:]
        act_back = act_backs[which]
        sigmoid_g = jax.nn.sigmoid(gate_part)
        hidden_act = (gate_part * sigmoid_g * up_part).astype(low)
        gate_up_back = jnp.concatenate(
            [
                act_back * up_part * sigmoid_g * (1.0 + gate_part * (1.0 - sigmoid_g)),
                act_back * gate_part * sigmoid_g,
            ],
            axis=-1,
        ).astype(low)
        slot_back = dot(gate_up_back, gate_up_low[which], 1, 1).astype(low)
        slots.append(slot_in)
        hidden_acts.append(hidden_act)
        gate_up_backs.append(gate_up_back)
        slot_backs.append(slot_back.reshape(blocks, CAP, model_width))
    chosen_all = chosen.reshape(blocks, local_experts * CAP, span_len)

    def partial_sums(parts):
        joined = jnp.concatenate(parts, axis=1)
        partial = jnp.einsum("brt,brd->btd", chosen_all, joined, preferred_element_type=jnp.float32)
        return row_major(partial.astype(low).reshape(owners, tok_rows, model_width))

    def send_back(partial):
        return lax.psum_scatter(partial, "expert", scatter_dimension=0, tiled=False)

    back_part = partial_sums(slot_backs)
    back_part, hidden_acts = lax.optimization_barrier((back_part, hidden_acts))
    normed_two_back = send_back(back_part)
    outs = []
    for which in range(local_experts):
        result = dot(hidden_acts[which], down_low[which], 1, 0)
        outs.append(
            (result.reshape(blocks, CAP, model_width) * slot_gates[:, which, :, None]).astype(low)
        )
    out_part = partial_sums(outs)
    if square:
        where = lax.axis_index("dp").astype(jnp.int32).reshape(1)
        half = local_experts // 2
        near, far = xor_pairs(dp_size, 1), xor_pairs(dp_size, 2)
        keeps, gots, sent = [None] * local_experts, [None] * local_experts, [None] * local_experts
        for which in [e + side for e in range(half) for side in (0, half)]:
            first = which < half
            *sends, keep, keep_pass = expert_grads(
                where,
                slots[which],
                gate_up_backs[which],
                hidden_acts[which],
                slot_grads[which],
                (1, 3, 0, 2) if first else (2, 3, 0, 1),
            )
            keeps[which] = (keep, keep_pass)
            sent[which] = sends[0]
            gots[which] = [
                lax.ppermute(sends[0], "dp", near if first else far) if which % half == 0 else None,
                lax.ppermute(sends[1], "dp", near if first else far),
            ]
        normed_two_back, out_part, keeps = lax.optimization_barrier((normed_two_back, out_part, keeps))
    else:
        grads = [
            jnp.concatenate(
                [
                    dot(slots[which], gate_up_backs[which], 0, 0).reshape(dp_size, up_rows, -1),
                    dot(hidden_acts[which], slot_grads[which], 0, 0).reshape(dp_size, down_rows, -1),
                ],
                axis=1,
            )
            for which in range(local_experts)
        ]
        expert_sum = lax.psum_scatter(
            jnp.stack(grads).astype(low), "dp", scatter_dimension=1, tiled=False
        ).astype(jnp.float32)
    normed_two_back = by_distance(normed_two_back).astype(jnp.float32)
    upstream = upstream_low.astype(jnp.float32)

    residual_part, gain_two_grad = norm_backward(residual, gains_used[1], normed_two_back)
    residual_back = upstream + residual_part
    mix_back = residual_back.astype(low)
    attn_back = jnp.einsum(
        "re,de->rd", mix_back, out_low, preferred_element_type=jnp.float32
    ).astype(low)
    query_back, kv_term = attend_back(
        place_index, queries, attn_back, kv_all, mix_wide, mix_stat, cosine, sine
    )
    if square:
        early = [0, half]
        late = [which for which in range(local_experts) if which not in early]
        ready = [gots[which] for which in early], [gots[which][1] for which in late]
        kv_term, ready, sent = lax.optimization_barrier((kv_term, ready, [sent[which] for which in late]))
        for which, got in zip(early, ready[0]):
            gots[which] = got
        for which, got in zip(late, ready[1]):
            gots[which][1] = got
        for which, send in zip(late, sent):
            gots[which][0] = lax.ppermute(send, "dp", near if which < half else far)

        def pass_on(which, summed):
            return lax.ppermute(summed, "dp", far if which < half else near)

        lasts = {which: pass_on(which, add_low(keeps[which][1], gots[which][1])) for which in early}
    kv_back = lax.psum_scatter(kv_term, "expert", scatter_dimension=0, tiled=False)
    if square:
        early_pair = core_sums(
            jnp.concatenate(
                [dot(normed_cut, query_back, 0, 0).astype(low), dot(mix_cut, mix_back, 0, 0).astype(low)],
                axis=1,
            )
        )
        early_start = square_start(early_pair)
        kv_back, out_part, gots, lasts, early_pair, early_start = lax.optimization_barrier(
            (kv_back, out_part, gots, lasts, early_pair, early_start)
        )
        early_part = square_finish(early_pair, early_start)
    kv_low = turn_back(kv_back, cosine, sine)
    projected_back = jnp.concatenate([query_back, kv_low], axis=1)
    normed_back = jnp.einsum(
        "rf,df->rd", projected_back, qkv_low, preferred_element_type=jnp.float32
    )
    input_part, gain_one_grad = norm_backward(tokens, gains_used[0], normed_back)
    input_grad = (residual_back + input_part).reshape(sequences, span_len, model_width)
    gains_grad = jnp.stack([gain_one_grad, gain_two_grad])
    qkv_width = qkv_weight.shape[1]
    rates = learning_rates()

    def update_experts(grads):
        return (
            adamw(gate_up_weight, grads[:, :up_rows], gate_up_first, gate_up_second, rates[3], DECAY),
            adamw(down_weight, grads[:, up_rows:], down_first, down_second, rates[4], DECAY),
        )

    if square:
        late_pair = core_sums(dot(normed_cut, kv_low, 0, 0))
        gain_rows = by_distance(gains_grad).reshape(2, 4, -1).transpose(1, 0, 2)
        gain_rows = jnp.pad(gain_rows.reshape(4, half_rows, -1).astype(low), ((0, 0), (0, 0), (0, 256 - 4)))
        gain_rows = row_major(gain_rows)
        gain_pair = row_major(
            add_low(gain_rows, lax.ppermute(gain_rows, "expert", xor_pairs(owners, 1)))
        )
        late_pair = jnp.concatenate([late_pair, gain_pair], axis=2)
        late_pair, early_part = lax.optimization_barrier((late_pair, early_part))
        late_part = square_finish(late_pair, square_start(late_pair))
        part = row_major(jnp.concatenate([early_part, late_part], axis=1))
        summed = {which: add_low(keeps[which][1], gots[which][1]) for which in late}
        part, summed = lax.optimization_barrier((part, summed))
        lasts.update({which: pass_on(which, summed[which]) for which in late})
        out_sum_low = send_back(out_part)
        part, out_sum_low, lasts = lax.optimization_barrier(
            (line_reduce(part, 2, 4), out_sum_low, lasts)
        )
        part = line_reduce(part, 4, owners)
        expert_sum = jnp.stack(
            [
                keeps[e][0].astype(jnp.float32)
                + gots[e][0].astype(jnp.float32)
                + lasts[e].astype(jnp.float32)
                for e in range(local_experts)
            ]
        )
        part, expert_sum = lax.optimization_barrier((line_gather(part, owners, owners // 2), expert_sum))
        expert_up = update_experts(expert_sum)
        part, expert_up = lax.optimization_barrier((line_gather(part, owners // 2, 2), expert_up))
        attention_sum = line_gather(part, 2, 1).astype(jnp.float32)
    else:
        query_grad, kv_grad = dot(normed, query_back, 0, 0), dot(normed, kv_low, 0, 0)
        out_grad_sum = dot(attn_mix, mix_back, 0, 0)
        expert_up = update_experts(expert_sum)
        attention_sum = plain_sums(
            jnp.concatenate([query_grad, out_grad_sum, kv_grad, gains_grad.T], axis=1)
        )
        out_sum_low = send_back(out_part)
    hidden_out = (
        (residual + out_sum_low).astype(low).reshape(sequences, span_len, model_width)
    )
    kv_first = 2 * model_width
    qkv_sum = jnp.concatenate(
        [attention_sum[:, :D], attention_sum[:, kv_first : kv_first + qkv_width - D]], axis=1
    )
    out_sum = attention_sum[:, model_width:kv_first]
    gain_first = model_width + qkv_width
    if square:
        gains_sum = attention_sum[:half_rows, gain_first : gain_first + 4].reshape(2, -1)
    else:
        gains_sum = attention_sum[:, gain_first : gain_first + 2].T
    gains_sum = row_major(gains_sum)
    gains_up = adamw(norm_gains, gains_sum, gains_first, gains_second, rates[0], 0.0)
    qkv_up = adamw(qkv_weight, qkv_sum, qkv_first, qkv_second, rates[1], DECAY)
    out_up = adamw(out_weight, out_sum, out_first, out_second, rates[2], DECAY)
    gate_up_up, down_up = expert_up
    return (
        hidden_out,
        input_grad,
        *gains_up,
        *qkv_up,
        *out_up,
        *gate_up_up,
        *down_up,
    )


def solution(mesh):
    return jax.shard_map(
        per_device,
        mesh=mesh,
        in_specs=(
            P("dp", "expert", None),
            P("dp", "expert", None),
            P("dp", "expert", None),
            P("dp", "expert", None),
            P(None, "dp"),
            P("dp", None),
            P("dp", None),
            P("expert", "dp", None),
            P("expert", "dp", None),
            P(None, "dp"),
            P(None, "dp"),
            P("dp", None),
            P("dp", None),
            P("dp", None),
            P("dp", None),
            P("expert", "dp", None),
            P("expert", "dp", None),
            P("expert", "dp", None),
            P("expert", "dp", None),
        ),
        out_specs=(
            P("dp", "expert", None),
            P("dp", "expert", None),
            P(None, "dp"),
            P(None, "dp"),
            P(None, "dp"),
            P("dp", None),
            P("dp", None),
            P("dp", None),
            P("dp", None),
            P("dp", None),
            P("dp", None),
            P("expert", "dp", None),
            P("expert", "dp", None),
            P("expert", "dp", None),
            P("expert", "dp", None),
            P("expert", "dp", None),
            P("expert", "dp", None),
        ),
        check_vma=False,
    )
```

```python
import jax
import jax.numpy as jnp
from jax import lax
from jax.experimental import pallas as pl
from jax.experimental.layout import Layout, with_layout_constraint
from jax.experimental.pallas import tpu as pltpu
from jax.sharding import PartitionSpec as P

D = 1024
HEADS = 16
KV_HEADS = 8
HEAD = 64
EXPERTS = 32
FF = 512
TOP = 8
STEP = 10
CAP = 48


EPS_NORM = 1e-06
EPS_ADAM = 1e-08
BETA_ONE = 0.9
BETA_TWO = 0.95
DECAY = 0.1
THETA = 10000.0
NEG_FILL = -1e30


def rotation(positions):
    half_width = HEAD // 2
    frequency = jnp.power(THETA, -jnp.arange(half_width, dtype=jnp.float32) * (2.0 / HEAD))
    angles = positions[:, None] * frequency[None, :]
    return (jnp.cos(angles), jnp.sin(angles))


def rotate(values, cosine, sine):
    half_width = HEAD // 2
    first_half = values[..., :half_width]
    second_half = values[..., half_width:]
    cos_part = cosine[:, None, :]
    sin_part = sine[:, None, :]
    return jnp.concatenate(
        [
            first_half * cos_part - second_half * sin_part,
            second_half * cos_part + first_half * sin_part,
        ],
        axis=-1,
    )


def rms_norm(values, gain):
    return values * lax.rsqrt(jnp.mean(values * values, axis=-1, keepdims=True) + EPS_NORM) * gain


def norm_backward(values, gain, upstream_grad):
    result, pullback = jax.vjp(rms_norm, values, gain)
    return pullback(upstream_grad)


def adamw(weight, grad, first, second, rate, decay):
    first = BETA_ONE * first + (1.0 - BETA_ONE) * grad
    second = BETA_TWO * second + (1.0 - BETA_TWO) * grad * grad
    first_hat = first / (1.0 - BETA_ONE**STEP)
    second_hat = second / (1.0 - BETA_TWO**STEP)
    weight = weight - rate * (first_hat / (jnp.sqrt(second_hat) + EPS_ADAM) + decay * weight)
    return (first, second, weight)


def learning_rates():
    return (
        0.6,
        3.0 * (2.0 / D) ** 0.5,
        3.0 * (16.0 / D) ** 0.5,
        3.0 * D ** (-0.5),
        3.0 * (16.0 / FF) ** 0.5,
    )


def head_scores(query_head, key_head, causal):
    scores = jnp.einsum(
        "sgqd,std->sgqt", query_head, key_head, preferred_element_type=jnp.float32
    ) * HEAD ** (-0.5)
    return jnp.where(causal, scores, NEG_FILL)


VMEM_BYTES = 56 * 1024 * 1024
CHUNK = 4


def dot(left, right, left_dim, right_dim):
    return lax.dot_general(
        left, right, (((left_dim,), (right_dim,)), ((), ())), preferred_element_type=jnp.float32
    )


def turn(values, cosine, sine):
    lane = lax.broadcasted_iota(jnp.int32, values.shape, 1)
    half = HEAD // 2
    swapped = jnp.where(
        lane % HEAD < half, pltpu.roll(values, 2 * HEAD - half, 1), pltpu.roll(values, half, 1)
    )
    return values * cosine + swapped * sine


def project_kernel(normed_ref, weight_ref, cosine_ref, sine_ref, query_ref, kv_ref):
    step = pl.program_id(0)
    product = dot(normed_ref[...], weight_ref[...], 1, 0)
    def turned():
        parts = [product[:, first : first + 2 * HEAD] for first in range(0, product.shape[1], 2 * HEAD)]
        return jnp.concatenate([turn(part, cosine_ref[...], sine_ref[...]) for part in parts], axis=1)

    @pl.when(step < 2)
    def _():
        query_ref[...] = (turned() * HEAD ** (-0.5)).astype(jnp.bfloat16)

    @pl.when(step == 2)
    def _():
        kv_ref[...] = turned().astype(jnp.bfloat16)

    @pl.when(step == 3)
    def _():
        kv_ref[...] = product.astype(jnp.bfloat16)


def project(normed, weight, cosine, sine):
    rows, depth = normed.shape
    kv_width = KV_HEADS * HEAD
    return pl.pallas_call(
        project_kernel,
        grid=(4,),
        in_specs=[
            pl.BlockSpec((rows, depth), lambda i: (0, 0)),
            pl.BlockSpec((depth, 512), lambda i: (0, i)),
            pl.BlockSpec((rows, 2 * HEAD), lambda i: (0, 0)),
            pl.BlockSpec((rows, 2 * HEAD), lambda i: (0, 0)),
        ],
        out_specs=[
            pl.BlockSpec((rows, 512), lambda i: (0, jnp.minimum(i, 1))),
            pl.BlockSpec((rows, 512), lambda i: (0, jnp.maximum(i - 2, 0))),
        ],
        out_shape=[
            jax.ShapeDtypeStruct((rows, D), jnp.bfloat16),
            jax.ShapeDtypeStruct((rows, 2 * kv_width), jnp.bfloat16),
        ],
        compiler_params=pltpu.CompilerParams(vmem_limit_bytes=VMEM_BYTES),
    )(normed, weight, cosine, sine)


def spread_heads(tile):
    flipped = jnp.transpose(tile.astype(jnp.float32), (1, 0))
    blank = jnp.zeros((HEAD, flipped.shape[1]), jnp.float32)
    parts = [flipped[h * HEAD : (h + 1) * HEAD] for h in range(4)]
    return jnp.concatenate(
        [
            jnp.concatenate([parts[0], blank], axis=0),
            jnp.concatenate([parts[1], blank], axis=0),
            jnp.concatenate([blank, parts[2]], axis=0),
            jnp.concatenate([blank, parts[3]], axis=0),
        ],
        axis=1,
    )


def gather_heads(wide):
    span = wide.shape[1] // 4
    first = jnp.concatenate([wide[:HEAD, :span], wide[:HEAD, span : 2 * span]], axis=0)
    second = jnp.concatenate([wide[HEAD:, 2 * span : 3 * span], wide[HEAD:, 3 * span :]], axis=0)
    return jnp.transpose(first, (1, 0)), jnp.transpose(second, (1, 0))


def key_lead(rows, span):
    key_row = lax.broadcasted_iota(jnp.int32, (rows, 4 * span), 0)
    query_column = lax.broadcasted_iota(jnp.int32, (rows, 4 * span), 1) % span
    return key_row - query_column


def attend_kernel(place_ref, query_ref, key_ref, value_ref, mix_ref, wide_ref, stat_ref, score_ref):
    place = place_ref[0]
    owners, span, width = key_ref.shape
    query = spread_heads(query_ref[...]).astype(jnp.bfloat16)
    rows = CHUNK * span
    lead = key_lead(rows, span)
    top = jnp.full((1, 4 * span), NEG_FILL, jnp.float32)
    for chunk in range(owners // CHUNK):
        key = key_ref[chunk * CHUNK : (chunk + 1) * CHUNK].reshape(rows, width)
        scores = jnp.where(lead <= place * span - chunk * rows, dot(key, query, 1, 0), NEG_FILL)
        score_ref[chunk] = scores
        top = jnp.maximum(top, jnp.max(scores, axis=0, keepdims=True))
    total = jnp.zeros((1, 4 * span), jnp.float32)
    mixed = jnp.zeros((width, 4 * span), jnp.float32)
    for chunk in range(owners // CHUNK):
        value = value_ref[chunk * CHUNK : (chunk + 1) * CHUNK].reshape(rows, width)
        exponent = jnp.exp(score_ref[chunk] - top)
        total = total + jnp.sum(exponent, axis=0, keepdims=True)
        mixed = mixed + dot(value, exponent.astype(jnp.bfloat16), 0, 0)
    mixed = mixed / total
    wide_ref[0] = mixed
    stat_ref[0] = top + jnp.log(total)
    first, second = gather_heads(mixed)
    mix_ref[...] = jnp.concatenate([first, second], axis=1).astype(jnp.bfloat16)


def attend(place, queries, kv_all):
    owners, rows, kv_columns = kv_all.shape
    span = 128
    pairs = KV_HEADS // 2
    sequences = rows // span
    steps = sequences * pairs
    return pl.pallas_call(
        attend_kernel,
        grid=(sequences, pairs),
        in_specs=[
            pl.BlockSpec(memory_space=pltpu.SMEM),
            pl.BlockSpec((span, 4 * HEAD), lambda s, j: (s, j)),
            pl.BlockSpec((owners, span, 2 * HEAD), lambda s, j: (0, s, j)),
            pl.BlockSpec((owners, span, 2 * HEAD), lambda s, j: (0, s, j + pairs)),
        ],
        out_specs=[
            pl.BlockSpec((span, 4 * HEAD), lambda s, j: (s, j)),
            pl.BlockSpec((1, 2 * HEAD, 4 * span), lambda s, j: (s * pairs + j, 0, 0)),
            pl.BlockSpec((1, 1, 4 * span), lambda s, j: (s * pairs + j, 0, 0)),
        ],
        out_shape=[
            jax.ShapeDtypeStruct((rows, D), jnp.bfloat16),
            jax.ShapeDtypeStruct((steps, 2 * HEAD, 4 * span), jnp.float32),
            jax.ShapeDtypeStruct((steps, 1, 4 * span), jnp.float32),
        ],
        scratch_shapes=[pltpu.VMEM((owners // CHUNK, CHUNK * span, 4 * span), jnp.float32)],
        compiler_params=pltpu.CompilerParams(vmem_limit_bytes=VMEM_BYTES),
    )(place, queries, kv_all, kv_all)


def turn_back_kernel(values_ref, cosine_ref, sine_ref, turned_ref):
    width = 2 * HEAD
    for first in range(0, values_ref.shape[1], width):
        part = values_ref[:, first : first + width]
        if first < KV_HEADS * HEAD:
            part = turn(part.astype(jnp.float32), cosine_ref[...], -sine_ref[...]).astype(jnp.bfloat16)
        turned_ref[:, first : first + width] = part


def turn_back(values, cosine, sine):
    return pl.pallas_call(
        turn_back_kernel,
        out_shape=jax.ShapeDtypeStruct(values.shape, jnp.bfloat16),
        compiler_params=pltpu.CompilerParams(vmem_limit_bytes=VMEM_BYTES),
    )(values, cosine, sine)


def attend_back_kernel(
    place_ref, query_ref, back_ref, key_ref, value_ref, wide_ref, stat_ref, cosine_ref, sine_ref,
    query_back_ref, kv_back_ref,
):
    place = place_ref[0]
    span = query_ref.shape[0]
    owners = key_ref.shape[0]
    query = spread_heads(query_ref[...]).astype(jnp.bfloat16)
    back_wide = spread_heads(back_ref[...])
    back = back_wide.astype(jnp.bfloat16)
    stat = stat_ref[0]
    row_dot = jnp.sum(back_wide * wide_ref[0], axis=0, keepdims=True)

    width = key_ref.shape[2]
    rows = CHUNK * span
    lead = key_lead(rows, span)
    total = jnp.zeros((width, 4 * span), jnp.float32)
    for chunk in range(owners // CHUNK):
        part = slice(chunk * CHUNK, (chunk + 1) * CHUNK)
        key = key_ref[part].reshape(rows, width)
        value = value_ref[part].reshape(rows, width)
        probability = jnp.exp(dot(key, query, 1, 0) - stat)
        probability = jnp.where(lead <= place * span - chunk * rows, probability, 0.0)
        weight_back = dot(value, back, 1, 0)
        score_back = (probability * (weight_back - row_dot)).astype(jnp.bfloat16)
        key_back = dot(score_back, query, 1, 1)
        value_back = dot(probability.astype(jnp.bfloat16), back, 1, 1)
        for first, result in ((0, key_back), (KV_HEADS * HEAD, value_back)):
            column = pl.multiple_of(first + pl.program_id(1) * width, width)
            kv_back_ref[part, :, pl.ds(column, width)] = result.astype(jnp.bfloat16).reshape(
                CHUNK, span, width
            )
        total = total + dot(key, score_back, 0, 0)

    halves = gather_heads(total * HEAD ** (-0.5))
    query_back_ref[...] = jnp.concatenate(
        [turn(half, cosine_ref[...], -sine_ref[...]) for half in halves], axis=1
    ).astype(jnp.bfloat16)


def attend_back(place, queries, attn_back, kv_all, wide, stat, cosine, sine):
    owners, rows, kv_columns = kv_all.shape
    span = 128
    pairs = KV_HEADS // 2
    sequences = rows // span
    kv_width = KV_HEADS * HEAD
    flat = pl.BlockSpec((span, 4 * HEAD), lambda s, j: (s, j))
    kv_block = (owners, span, 2 * HEAD)
    table = pl.BlockSpec((span, 2 * HEAD), lambda s, j: (s, 0))
    return pl.pallas_call(
        attend_back_kernel,
        grid=(sequences, pairs),
        in_specs=[
            pl.BlockSpec(memory_space=pltpu.SMEM),
            flat,
            flat,
            pl.BlockSpec(kv_block, lambda s, j: (0, s, j)),
            pl.BlockSpec(kv_block, lambda s, j: (0, s, j + pairs)),
            pl.BlockSpec((1, 2 * HEAD, 4 * span), lambda s, j: (s * pairs + j, 0, 0)),
            pl.BlockSpec((1, 1, 4 * span), lambda s, j: (s * pairs + j, 0, 0)),
            table,
            table,
        ],
        out_specs=[
            flat,
            pl.BlockSpec((owners, span, 2 * kv_width), lambda s, j: (0, s, 0)),
        ],
        out_shape=[
            jax.ShapeDtypeStruct((rows, D), jnp.bfloat16),
            jax.ShapeDtypeStruct((owners, rows, 2 * kv_width), jnp.bfloat16),
        ],
        compiler_params=pltpu.CompilerParams(vmem_limit_bytes=VMEM_BYTES),
    )(place, queries, attn_back, kv_all, kv_all, wide, stat, cosine, sine)


def pass_through(pairs, hold_ref, in_sems, out_sems):
    reads = [
        pltpu.make_async_copy(source, hold_ref.at[slot], in_sems.at[slot])
        for slot, (source, targets) in enumerate(pairs)
    ]
    for read in reads:
        read.start()
    writes = []
    for slot, (source, targets) in enumerate(pairs):
        reads[slot].wait()
        for number, (row, rows, column, columns, target) in enumerate(targets):
            write = pltpu.make_async_copy(
                hold_ref.at[slot, pl.ds(row, rows), pl.ds(column, columns)],
                target,
                out_sems.at[slot, number],
            )
            write.start()
            writes.append(write)
    for write in writes:
        write.wait()


def place_rows_kernel(
    where_ref, mine_ref, other_ref, first_ref, second_ref, extra_ref, hold_ref, in_sems, out_sems
):
    me, core = where_ref[0], where_ref[1]
    half, rest = first_ref.shape[2], extra_ref.shape[2]
    columns = first_ref.shape[3]
    pairs = []
    for source, which in ((mine_ref, core), (other_ref, 1 - core)):
        for step in range(source.shape[0]):
            targets = (
                (0, half, 0, columns, first_ref.at[me ^ step, which]),
                (0, half, columns, second_ref.shape[3], second_ref.at[me ^ step, which]),
                (half, rest, 0, columns, extra_ref.at[me ^ step, which]),
            )
            pairs.append((source.at[step], targets))
    pass_through(pairs, hold_ref, in_sems, out_sems)


def place_experts_kernel(where_ref, *refs):
    hold_ref, in_sems, out_sems = refs[-3:]
    experts = hold_ref.shape[0] // 4
    sources = refs[: len(refs) - 3 - 2 * experts]
    ups, downs = refs[len(sources) : len(sources) + experts], refs[len(sources) + experts : -3]
    me = where_ref[0]
    up_rows, down_rows, columns = ups[0].shape[1], downs[0].shape[1], ups[0].shape[2]
    pairs = []
    target = 0
    for first in range(0, len(sources), 4):
        for index in range(sources[first].shape[0]):
            for step, source in enumerate(sources[first : first + 4]):
                targets = (
                    (0, up_rows, 0, columns, ups[target].at[step]),
                    (up_rows, down_rows, 0, columns, downs[target].at[me ^ step]),
                )
                pairs.append((source.at[index], targets))
            target += 1
    pass_through(pairs, hold_ref, in_sems, out_sems)


def place(kernel, where, pieces, slots, shapes):
    anywhere = pl.BlockSpec(memory_space=pl.ANY)
    rows, columns = pieces[0].shape[-2:]
    kind = pieces[0].dtype
    return pl.pallas_call(
        kernel,
        in_specs=[pl.BlockSpec(memory_space=pltpu.SMEM)] + [anywhere] * len(pieces),
        out_specs=[anywhere] * len(shapes),
        out_shape=[jax.ShapeDtypeStruct(shape, kind) for shape in shapes],
        scratch_shapes=[
            pltpu.VMEM((slots, rows, columns), kind),
            pltpu.SemaphoreType.DMA((slots,)),
            pltpu.SemaphoreType.DMA((slots, 3)),
        ],
        compiler_params=pltpu.CompilerParams(vmem_limit_bytes=VMEM_BYTES),
    )(where, *pieces)


def row_major(values):
    return with_layout_constraint(values, Layout(major_to_minor=tuple(range(values.ndim))))


def xor_pairs(size, step):
    return [(index, index ^ step) for index in range(size)]


def square_gather(first, second):
    size = lax.axis_size("dp")
    near, far = xor_pairs(size, 1), xor_pairs(size, 2)
    first_one = lax.ppermute(first, "dp", near)
    second_two = lax.ppermute(second, "dp", far)
    first_rest = lax.ppermute(jnp.stack([first, first_one]), "dp", far)
    second_rest = lax.ppermute(jnp.stack([second, second_two]), "dp", near)
    return (first, first_one, first_rest, second, second_two, second_rest)


def add_low(left, right):
    return (left.astype(jnp.float32) + right.astype(jnp.float32)).astype(jnp.bfloat16)


def gather_rows(shard, half, columns, later):
    size, cores = lax.axis_size("dp"), lax.axis_size("expert")
    rows, width = shard.shape
    if size != 4 or cores % 2:
        got = lax.all_gather(shard, "dp", axis=0, tiled=False).reshape(size, 2, rows // 2, width)
        first, second = got[:, :, :half, :columns], got[:, :, :half, columns:]
        extra = got[:, :, half:, :columns]
        return first.reshape(-1, columns), second.reshape(-1, width - columns), extra, later
    core = lax.axis_index("expert") % 2
    mine = lax.dynamic_slice_in_dim(shard, core * (rows // 2), rows // 2, 0)
    first, first_one, first_rest, second, second_two, second_rest = square_gather(
        mine[:, : width // 2], mine[:, width // 2 :]
    )
    stacked = jnp.concatenate(
        [
            jnp.stack([first, first_one, first_rest[0], first_rest[1]]),
            jnp.stack([second, second_rest[0], second_two, second_rest[1]]),
        ],
        axis=2,
    )
    stacked, later = lax.optimization_barrier((stacked, later))
    other = lax.ppermute(stacked, "expert", xor_pairs(cores, 1))
    where = jnp.stack([lax.axis_index("dp"), core]).astype(jnp.int32)
    shapes = [
        (size, 2, half, columns),
        (size, 2, half, width - columns),
        (size, 2, rows // 2 - half, columns),
    ]
    whole, second, extra = place(place_rows_kernel, where, (stacked, other), 2 * size, shapes)
    return whole.reshape(-1, columns), second.reshape(-1, width - columns), extra, later


def expert_pieces(packed):
    if lax.axis_size("dp") != 4:
        return (lax.all_gather(packed, "dp", axis=1, tiled=False),)
    return (
        packed,
        lax.ppermute(packed, "dp", xor_pairs(4, 1)),
        lax.ppermute(packed, "dp", xor_pairs(4, 2)),
    )


def expert_groups(experts):
    half = max(experts // 2, 1)
    bounds = sorted({0, min(1, half), half, experts})
    return [slice(first, last) for first, last in zip(bounds[:-1], bounds[1:])]


def expert_weights(pieces, up_rows):
    if len(pieces[0]) == 1:
        got = jnp.concatenate([piece[0] for piece in pieces], axis=0)
        experts, columns = got.shape[0], got.shape[3]
        ups = [got[e, :, :up_rows].reshape(-1, columns) for e in range(experts)]
        downs = [got[e, :, up_rows:].reshape(-1, columns) for e in range(experts)]
        return ups, downs
    passed = [lax.ppermute(piece[1], "dp", xor_pairs(4, 2)) for piece in pieces[:-1]]
    passed.append(lax.ppermute(pieces[-1][2], "dp", xor_pairs(4, 1)))
    where = lax.axis_index("dp").astype(jnp.int32).reshape(1)
    experts = sum(piece[0].shape[0] for piece in pieces)
    rows, columns = pieces[0][0].shape[1:]
    shapes = [(4, up_rows, columns)] * experts + [(4, rows - up_rows, columns)] * experts
    sources = [part for piece, last in zip(pieces, passed) for part in (*piece, last)]
    placed = place(place_experts_kernel, where, sources, 4 * experts, shapes)
    placed = [part.reshape(-1, columns) for part in placed]
    return placed[:experts], placed[experts:]


def by_distance(values):
    size = lax.axis_size("dp")
    if size != 4:
        return values
    width = values.shape[1] // size
    me = lax.axis_index("dp")
    parts = [
        lax.dynamic_slice_in_dim(values, (me ^ step) * width, width, 1) for step in range(size)
    ]
    return jnp.concatenate(parts, axis=1)


def expert_grad_kernel(
    where_ref, slot_ref, up_back_ref, act_ref, slot_grad_ref, *refs, order
):
    parts, (up_ref, down_ref) = refs[:4], refs[4:]
    step = pl.program_id(0)
    up = dot(slot_ref[...], up_back_ref[...], 0, 0)
    down = dot(act_ref[...], slot_grad_ref[...], 0, 0)

    @pl.when(step == 0)
    def _():
        up_ref[...] = up
        down_ref[...] = down

    @pl.when(step > 0)
    def _():
        up_ref[...] += up
        down_ref[...] += down

    @pl.when(step == pl.num_programs(0) - 1)
    def _():
        up_rows, down_rows = up_ref.shape[0] // 4, down_ref.shape[0] // 4
        for target, part in zip(parts, order):
            target[:up_rows] = up_ref[part * up_rows : (part + 1) * up_rows].astype(jnp.bfloat16)
            row = pl.multiple_of((where_ref[0] ^ part) * down_rows, down_rows)
            target[up_rows:] = down_ref[pl.ds(row, down_rows), :].astype(jnp.bfloat16)


def expert_grads(where, slot, up_back, act, slot_grad, order):
    rows, depth = slot.shape
    hidden, width = act.shape[1], slot_grad.shape[1]
    part_rows = (depth + hidden) // 4
    steps = 2
    blocks = [
        pl.BlockSpec((rows // steps, array.shape[1]), lambda i: (i, 0))
        for array in (slot, up_back, act, slot_grad)
    ]
    result = jax.ShapeDtypeStruct((part_rows, width), jnp.bfloat16)
    return pl.pallas_call(
        lambda *refs: expert_grad_kernel(*refs, order=order),
        grid=(steps,),
        in_specs=[pl.BlockSpec(memory_space=pltpu.SMEM)] + blocks,
        out_specs=[pl.BlockSpec((part_rows, width), lambda i: (0, 0))] * 4,
        out_shape=[result] * 4,
        scratch_shapes=[
            pltpu.VMEM((depth, up_back.shape[1]), jnp.float32),
            pltpu.VMEM((hidden, width), jnp.float32),
        ],
        compiler_params=pltpu.CompilerParams(vmem_limit_bytes=VMEM_BYTES),
    )(where, slot, up_back, act, slot_grad)


def by_core(values):
    width = values.shape[1] // 8
    me, core = lax.axis_index("dp"), lax.axis_index("expert") % 2
    parts = [
        lax.dynamic_slice_in_dim(values, (2 * (me ^ step) + side) * width, width, 1)
        for side in (core, 1 - core)
        for step in range(4)
    ]
    return jnp.concatenate(parts, axis=1)


def core_sums(grad):
    owners = lax.axis_size("expert")
    rows, columns = grad.shape
    grad = row_major(grad.astype(jnp.bfloat16)).reshape(2, 4, rows // 8, columns)
    return row_major(add_low(grad[0], lax.ppermute(grad[1], "expert", xor_pairs(owners, 1))))


def square_start(pair):
    half = pair.shape[2] // 2
    first, second = pair[:, :, :half], pair[:, :, half:]
    return (
        lax.ppermute(jnp.stack([first[1], first[3]]), "dp", xor_pairs(4, 1)),
        lax.ppermute(jnp.stack([second[2], second[3]]), "dp", xor_pairs(4, 2)),
    )


def square_finish(pair, gots):
    half = pair.shape[2] // 2
    first, second = pair[:, :, :half], pair[:, :, half:]
    first_last = lax.ppermute(add_low(first[2], gots[0][1]), "dp", xor_pairs(4, 2))
    second_last = lax.ppermute(add_low(second[1], gots[1][1]), "dp", xor_pairs(4, 1))

    def total(own, one, two):
        return own.astype(jnp.float32) + one.astype(jnp.float32) + two.astype(jnp.float32)

    parts = [total(first[0], gots[0][0], first_last), total(second[0], gots[1][0], second_last)]
    return row_major(jnp.concatenate(parts, axis=1).astype(jnp.bfloat16))


def line_reduce(total, step, most):
    owners = lax.axis_size("expert")
    place_index = lax.axis_index("expert")
    while step < most:
        side = (place_index // step) % 2
        half = total.shape[0] // 2
        mine = lax.dynamic_slice_in_dim(total, side * half, half, 0)
        other = lax.dynamic_slice_in_dim(total, (1 - side) * half, half, 0)
        total = row_major(add_low(mine, lax.ppermute(other, "expert", xor_pairs(owners, step))))
        step *= 2
    return total


def line_gather(total, step, least):
    place_index = lax.axis_index("expert")
    while step > least:
        step //= 2
        side = (place_index // step) % 2
        other = lax.ppermute(total, "expert", xor_pairs(lax.axis_size("expert"), step))
        total = jnp.where(
            side == 0,
            jnp.concatenate([total, other], axis=0),
            jnp.concatenate([other, total], axis=0),
        )
    return row_major(total)


def plain_sums(grad):
    part = lax.psum_scatter(grad.astype(jnp.bfloat16), "dp", scatter_dimension=0, tiled=True)
    return lax.psum(part.astype(jnp.float32), "expert")


def per_device(
    hidden_in,
    out_grad,
    expert_ids,
    route_gates,
    norm_gains,
    qkv_weight,
    out_weight,
    gate_up_weight,
    down_weight,
    gains_first,
    gains_second,
    qkv_first,
    qkv_second,
    out_first,
    out_second,
    gate_up_first,
    gate_up_second,
    down_first,
    down_second,
):
    sequences, span_len, model_width = hidden_in.shape
    owners = lax.axis_size("expert")
    dp_size = lax.axis_size("dp")
    position = lax.axis_index("expert")
    seq_len = span_len * owners
    group = HEADS // KV_HEADS
    kv_width = KV_HEADS * HEAD
    tok_rows = sequences * span_len
    local_experts = EXPERTS // owners
    blocks = owners * sequences
    low = jnp.bfloat16

    square = dp_size == 4 and owners % 2 == 0 and owners & (owners - 1) == 0
    shard_rows = qkv_weight.shape[0]
    half_rows = shard_rows // 2
    attention_low = jnp.concatenate([qkv_weight.astype(low), out_weight.astype(low)], axis=1)
    gain_rows = jnp.zeros((16, attention_low.shape[1]), low)
    gain_rows = gain_rows.at[:2, : norm_gains.shape[1]].set(norm_gains.astype(low))
    attention_pack = jnp.concatenate(
        [attention_low[:half_rows], gain_rows, attention_low[half_rows:], gain_rows], axis=0
    )
    query_pos = position * span_len + jnp.arange(span_len, dtype=jnp.int32)
    cosine, sine = rotation(query_pos.astype(jnp.float32))
    cosine = row_major(jnp.tile(cosine, (sequences, 4)))
    sine = row_major(jnp.tile(jnp.concatenate([-sine, sine], axis=1), (sequences, 2)))
    up_rows = gate_up_weight.shape[1]
    down_rows = down_weight.shape[1]
    packed = jnp.concatenate([gate_up_weight.astype(low), down_weight.astype(low)], axis=1)
    packed = [packed[span] for span in expert_groups(local_experts)]
    qkv_low, out_low, extra, (packed, cosine, sine) = gather_rows(
        attention_pack, half_rows, qkv_weight.shape[1], (packed, cosine, sine)
    )
    gains_used = (
        extra[:, 0, :2, : norm_gains.shape[1]]
        .transpose(1, 0, 2)
        .reshape(2, model_width)
        .astype(jnp.float32)
    )
    pieces = [expert_pieces(part) for part in packed]

    tokens = hidden_in.astype(jnp.float32).reshape(tok_rows, model_width)
    normed = rms_norm(tokens, gains_used[0]).astype(low)
    queries, kv_local = project(normed, qkv_low, cosine, sine)
    gates = route_gates.reshape(tok_rows, TOP)
    gates_high = gates.astype(low)
    gates_rest = (gates - gates_high.astype(jnp.float32)).astype(low)
    routes = jnp.concatenate([expert_ids.reshape(tok_rows, TOP).astype(low), gates_high, gates_rest], axis=1)
    route_rows = -(-tok_rows * 3 * TOP // model_width)
    pad_rows = -(-route_rows // 16) * 16
    routes = jnp.pad(routes.reshape(-1), (0, pad_rows * model_width - routes.size))
    upstream_low = out_grad.reshape(tok_rows, model_width)
    upstream_pack = jnp.concatenate([upstream_low, routes.reshape(pad_rows, model_width)], axis=0)
    upstream_got = lax.all_gather(upstream_pack, "expert", axis=0, tiled=False)
    kv_local, upstream_got, pieces[0] = lax.optimization_barrier((kv_local, upstream_got, pieces[0]))
    kv_all = lax.all_gather(kv_local, "expert", axis=0, tiled=False)
    place_index = position.astype(jnp.int32).reshape(1)

    upstream_all = upstream_got[:, :tok_rows].reshape(blocks, span_len, model_width)
    routes_all = (
        upstream_got[:, tok_rows:]
        .reshape(owners, -1)[:, : tok_rows * 3 * TOP]
        .reshape(blocks, span_len, 3, TOP)
        .astype(jnp.float32)
    )
    local_ids = position * local_experts + jnp.arange(local_experts, dtype=jnp.int32)
    named = (routes_all[:, :, 0, None, :] == local_ids.astype(jnp.float32)[None, None, :, None]).astype(
        jnp.float32
    )
    hits = jnp.sum(named, axis=3)
    hit_gates = jnp.sum(named * (routes_all[:, :, 1] + routes_all[:, :, 2])[:, :, None, :], axis=3)
    before = jnp.tril(jnp.ones((span_len, span_len), jnp.float32), -1).astype(low)
    ranks = jnp.einsum("tu,bul->blt", before, hits.astype(low), preferred_element_type=jnp.float32)
    hits = hits.transpose(0, 2, 1)
    hit_gates = hit_gates.transpose(0, 2, 1)
    place = jnp.where(hits > 0.5, ranks, -1.0)
    chosen = place[:, :, None, :] == jnp.arange(CAP, dtype=jnp.float32)[None, None, :, None]
    slot_gates = jnp.sum(jnp.where(chosen, hit_gates[:, :, None, :], 0.0), axis=3)
    chosen = chosen.astype(low)

    attn_mix, mix_wide, mix_stat = attend(place_index, queries, kv_all)
    residual = tokens + jnp.dot(attn_mix, out_low, preferred_element_type=jnp.float32)
    normed_two = rms_norm(residual, gains_used[1]).astype(low)
    normed_two, pieces, chosen, slot_gates = lax.optimization_barrier(
        (normed_two, pieces, chosen, slot_gates)
    )
    gate_up_low, down_low = expert_weights(pieces, up_rows)
    normed_two_all = lax.all_gather(by_distance(normed_two), "expert", axis=0, tiled=False).reshape(
        blocks, span_len, model_width
    )

    if square:
        normed_cut, mix_cut = by_core(normed), by_core(attn_mix)
        normed_two_all, normed_cut, mix_cut = lax.optimization_barrier(
            (normed_two_all, normed_cut, mix_cut)
        )

    def take(rows, which):
        return jnp.einsum("brt,btd->brd", chosen[:, which], rows, preferred_element_type=jnp.float32)

    slot_rows = blocks * CAP
    slot_grads, act_backs = [], []
    for which in range(local_experts):
        slot_grad = (
            (take(upstream_all, which) * slot_gates[:, which, :, None])
            .astype(low)
            .reshape(slot_rows, model_width)
        )
        slot_grads.append(slot_grad)
        act_backs.append(dot(slot_grad, down_low[which], 1, 1))
    slots, hidden_acts, gate_up_backs, slot_backs = [], [], [], []
    for which in range(local_experts):
        slot_in = take(normed_two_all, which).astype(low).reshape(slot_rows, model_width)
        gate_up = dot(slot_in, gate_up_low[which], 1, 0)
        gate_part = gate_up[:, :FF]
        up_part = gate_up[:, FF:]
        act_back = act_backs[which]
        sigmoid_g = jax.nn.sigmoid(gate_part)
        hidden_act = (gate_part * sigmoid_g * up_part).astype(low)
        gate_up_back = jnp.concatenate(
            [
                act_back * up_part * sigmoid_g * (1.0 + gate_part * (1.0 - sigmoid_g)),
                act_back * gate_part * sigmoid_g,
            ],
            axis=-1,
        ).astype(low)
        slot_back = dot(gate_up_back, gate_up_low[which], 1, 1).astype(low)
        slots.append(slot_in)
        hidden_acts.append(hidden_act)
        gate_up_backs.append(gate_up_back)
        slot_backs.append(slot_back.reshape(blocks, CAP, model_width))
    chosen_all = chosen.reshape(blocks, local_experts * CAP, span_len)

    def partial_sums(parts):
        joined = jnp.concatenate(parts, axis=1)
        partial = jnp.einsum("brt,brd->btd", chosen_all, joined, preferred_element_type=jnp.float32)
        return row_major(partial.astype(low).reshape(owners, tok_rows, model_width))

    def send_back(partial):
        return lax.psum_scatter(partial, "expert", scatter_dimension=0, tiled=False)

    back_part = partial_sums(slot_backs)
    back_part, hidden_acts = lax.optimization_barrier((back_part, hidden_acts))
    normed_two_back = send_back(back_part)
    outs = []
    for which in range(local_experts):
        result = dot(hidden_acts[which], down_low[which], 1, 0)
        outs.append(
            (result.reshape(blocks, CAP, model_width) * slot_gates[:, which, :, None]).astype(low)
        )
    out_part = partial_sums(outs)
    if square:
        where = lax.axis_index("dp").astype(jnp.int32).reshape(1)
        half = local_experts // 2
        near, far = xor_pairs(dp_size, 1), xor_pairs(dp_size, 2)
        keeps, gots, sent = [None] * local_experts, [None] * local_experts, [None] * local_experts
        for which in [e + side for e in range(half) for side in (0, half)]:
            first = which < half
            *sends, keep, keep_pass = expert_grads(
                where,
                slots[which],
                gate_up_backs[which],
                hidden_acts[which],
                slot_grads[which],
                (1, 3, 0, 2) if first else (2, 3, 0, 1),
            )
            keeps[which] = (keep, keep_pass)
            sent[which] = sends[0]
            gots[which] = [
                lax.ppermute(sends[0], "dp", near if first else far) if which % half == 0 else None,
                lax.ppermute(sends[1], "dp", near if first else far),
            ]
        normed_two_back, keeps = lax.optimization_barrier((normed_two_back, keeps))
    else:
        grads = [
            jnp.concatenate(
                [
                    dot(slots[which], gate_up_backs[which], 0, 0).reshape(dp_size, up_rows, -1),
                    dot(hidden_acts[which], slot_grads[which], 0, 0).reshape(dp_size, down_rows, -1),
                ],
                axis=1,
            )
            for which in range(local_experts)
        ]
        expert_sum = lax.psum_scatter(
            jnp.stack(grads).astype(low), "dp", scatter_dimension=1, tiled=False
        ).astype(jnp.float32)
    normed_two_back = by_distance(normed_two_back).astype(jnp.float32)
    upstream = upstream_low.astype(jnp.float32)

    residual_part, gain_two_grad = norm_backward(residual, gains_used[1], normed_two_back)
    residual_back = upstream + residual_part
    mix_back = residual_back.astype(low)
    attn_back = jnp.einsum(
        "re,de->rd", mix_back, out_low, preferred_element_type=jnp.float32
    ).astype(low)
    query_back, kv_term = attend_back(
        place_index, queries, attn_back, kv_all, mix_wide, mix_stat, cosine, sine
    )
    if square:
        early = [0, half]
        late = [which for which in range(local_experts) if which not in early]
        ready = [gots[which] for which in early], [gots[which][1] for which in late]
        kv_term, ready, sent = lax.optimization_barrier((kv_term, ready, [sent[which] for which in late]))
        for which, got in zip(early, ready[0]):
            gots[which] = got
        for which, got in zip(late, ready[1]):
            gots[which][1] = got
        for which, send in zip(late, sent):
            gots[which][0] = lax.ppermute(send, "dp", near if which < half else far)

        def pass_on(which, summed):
            return lax.ppermute(summed, "dp", far if which < half else near)

        lasts = {which: pass_on(which, add_low(keeps[which][1], gots[which][1])) for which in early}
    kv_back = lax.psum_scatter(kv_term, "expert", scatter_dimension=0, tiled=False)
    if square:
        early_pair = core_sums(
            jnp.concatenate(
                [dot(normed_cut, query_back, 0, 0).astype(low), dot(mix_cut, mix_back, 0, 0).astype(low)],
                axis=1,
            )
        )
        early_start = square_start(early_pair)
        kv_back, out_part, gots, lasts, early_pair, early_start = lax.optimization_barrier(
            (kv_back, out_part, gots, lasts, early_pair, early_start)
        )
        early_part = square_finish(early_pair, early_start)
    kv_low = turn_back(kv_back, cosine, sine)
    projected_back = jnp.concatenate([query_back, kv_low], axis=1)
    normed_back = jnp.einsum(
        "rf,df->rd", projected_back, qkv_low, preferred_element_type=jnp.float32
    )
    input_part, gain_one_grad = norm_backward(tokens, gains_used[0], normed_back)
    input_grad = (residual_back + input_part).reshape(sequences, span_len, model_width)
    gains_grad = jnp.stack([gain_one_grad, gain_two_grad])
    qkv_width = qkv_weight.shape[1]
    rates = learning_rates()

    def update_experts(grads):
        return (
            adamw(gate_up_weight, grads[:, :up_rows], gate_up_first, gate_up_second, rates[3], DECAY),
            adamw(down_weight, grads[:, up_rows:], down_first, down_second, rates[4], DECAY),
        )

    if square:
        late_pair = core_sums(dot(normed_cut, kv_low, 0, 0))
        gain_rows = by_distance(gains_grad).reshape(2, 4, -1).transpose(1, 0, 2)
        gain_rows = jnp.pad(gain_rows.reshape(4, half_rows, -1).astype(low), ((0, 0), (0, 0), (0, 256 - 4)))
        gain_rows = row_major(gain_rows)
        gain_pair = row_major(
            add_low(gain_rows, lax.ppermute(gain_rows, "expert", xor_pairs(owners, 1)))
        )
        late_pair = jnp.concatenate([late_pair, gain_pair], axis=2)
        late_pair, early_part = lax.optimization_barrier((late_pair, early_part))
        late_part = square_finish(late_pair, square_start(late_pair))
        part = row_major(jnp.concatenate([early_part, late_part], axis=1))
        summed = {which: add_low(keeps[which][1], gots[which][1]) for which in late}
        part, summed = lax.optimization_barrier((part, summed))
        lasts.update({which: pass_on(which, summed[which]) for which in late})
        out_sum_low = send_back(out_part)
        part, out_sum_low, lasts = lax.optimization_barrier(
            (line_reduce(part, 2, 4), out_sum_low, lasts)
        )
        part = line_reduce(part, 4, owners)
        expert_sum = jnp.stack(
            [
                keeps[e][0].astype(jnp.float32)
                + gots[e][0].astype(jnp.float32)
                + lasts[e].astype(jnp.float32)
                for e in range(local_experts)
            ]
        )
        part, expert_sum = lax.optimization_barrier((line_gather(part, owners, owners // 2), expert_sum))
        expert_up = update_experts(expert_sum)
        part, expert_up = lax.optimization_barrier((line_gather(part, owners // 2, 2), expert_up))
        attention_sum = line_gather(part, 2, 1).astype(jnp.float32)
    else:
        query_grad, kv_grad = dot(normed, query_back, 0, 0), dot(normed, kv_low, 0, 0)
        out_grad_sum = dot(attn_mix, mix_back, 0, 0)
        expert_up = update_experts(expert_sum)
        attention_sum = plain_sums(
            jnp.concatenate([query_grad, out_grad_sum, kv_grad, gains_grad.T], axis=1)
        )
        out_sum_low = send_back(out_part)
    hidden_out = (
        (residual + out_sum_low).astype(low).reshape(sequences, span_len, model_width)
    )
    kv_first = 2 * model_width
    qkv_sum = jnp.concatenate(
        [attention_sum[:, :D], attention_sum[:, kv_first : kv_first + qkv_width - D]], axis=1
    )
    out_sum = attention_sum[:, model_width:kv_first]
    gain_first = model_width + qkv_width
    if square:
        gains_sum = attention_sum[:half_rows, gain_first : gain_first + 4].reshape(2, -1)
    else:
        gains_sum = attention_sum[:, gain_first : gain_first + 2].T
    gains_sum = row_major(gains_sum)
    gains_up = adamw(norm_gains, gains_sum, gains_first, gains_second, rates[0], 0.0)
    qkv_up = adamw(qkv_weight, qkv_sum, qkv_first, qkv_second, rates[1], DECAY)
    out_up = adamw(out_weight, out_sum, out_first, out_second, rates[2], DECAY)
    gate_up_up, down_up = expert_up
    return (
        hidden_out,
        input_grad,
        *gains_up,
        *qkv_up,
        *out_up,
        *gate_up_up,
        *down_up,
    )


def solution(mesh):
    return jax.shard_map(
        per_device,
        mesh=mesh,
        in_specs=(
            P("dp", "expert", None),
            P("dp", "expert", None),
            P("dp", "expert", None),
            P("dp", "expert", None),
            P(None, "dp"),
            P("dp", None),
            P("dp", None),
            P("expert", "dp", None),
            P("expert", "dp", None),
            P(None, "dp"),
            P(None, "dp"),
            P("dp", None),
            P("dp", None),
            P("dp", None),
            P("dp", None),
            P("expert", "dp", None),
            P("expert", "dp", None),
            P("expert", "dp", None),
            P("expert", "dp", None),
        ),
        out_specs=(
            P("dp", "expert", None),
            P("dp", "expert", None),
            P(None, "dp"),
            P(None, "dp"),
            P(None, "dp"),
            P("dp", None),
            P("dp", None),
            P("dp", None),
            P("dp", None),
            P("dp", None),
            P("dp", None),
            P("expert", "dp", None),
            P("expert", "dp", None),
            P("expert", "dp", None),
            P("expert", "dp", None),
            P("expert", "dp", None),
            P("expert", "dp", None),
        ),
        check_vma=False,
    )
```
